512 devices in a mesh: ctx: 8 (over x, core), ep: 64 (over y, z).
Axes of the slice: x: 4, y: 4, z: 16, core: 2. Of those that a mesh axis runs over, the one named last changes fastest.
Arguments:
- queries: bfloat16 [256, 64, 576], P('ep'), may hold values from -32 to 32
- new_key: bfloat16 [256, 576], P('ep'), may hold values from -4 to 4
- latent_cache: bfloat16 [8, 1024, 64, 576], P('ctx', 'ep'), may hold values from -6 to 6
- page_table: int32 [256, 8, 4], P('ep', 'ctx'), may hold values from 0 to 15, as said below
- lengths: int32 [256], P('ep'), may hold values from 1 to 2048
- hidden_in: bfloat16 [256, 7168], P('ep', 'ctx'), may hold values from -6 to 6
- w_uv: bfloat16 [64, 512, 128], P('ep'), may hold values from -0.25 to 0.25
- w_out: bfloat16 [8192, 7168], P('ep', 'ctx'), may hold values from -0.0625 to 0.0625
- norm_gain: float32 [7168], P('ctx'), may hold values from 0.1 to 1.9
- routes: int32 [256, 8], P('ep'), may hold values from 0 to 15, as said below
- route_weight: float32 [256, 8], P('ep'), may hold values from 0.1 to 0.6
- w_gate: bfloat16 [7168, 32768], P('ctx', 'ep'), may hold values from -0.0625 to 0.0625
- w_up: bfloat16 [7168, 32768], P('ctx', 'ep'), may hold values from -0.0625 to 0.0625
- w_down: bfloat16 [32768, 7168], P('ep', 'ctx'), may hold values from -0.125 to 0.125
Outputs:
- attn_proj: bfloat16 [256, 7168], P('ep', 'ctx')
- layer_out: bfloat16 [256, 7168], P('ep', 'ctx')
The draws below stay inside these ranges and needn't reach their ends.
Inputs may be any that keep to these rules, and one draw needn't show every extreme that they name: The slots that page_table gives for the requests of one index of ep on one index of ctx are distinct. `routes`: each request names 8 different experts; among the 4 requests of one index of ep every expert is named by exactly 2 of them.
All inputs are finite; a program needn't handle non-finite values.
Results may differ from the reference program's by a relative error of at most 0.013.
Values may be sent and summed in bfloat16 or wider, within the bound.
A program may use at most 64 MiB of HBM per device.

```python
import math
import jax
import jax.numpy as jnp
from jax import lax

D = 7168
HEADS = 64
LAT = 512
VDIM = 128
FF = 2048
TOP = 8
EXPERTS = 16
PAGE = 64
R_DEV = 4
PAGES_RANK = 4
ROWS = 256
KDIM = 576
POOL = 16
SLOTS = 1024
CTXMAX = 2048
N_CTX = 8
N_EP = 64


def shared_vector(key):
    signs = jax.random.randint(jax.random.fold_in(key, 77), (ROWS, KDIM), 0, 2).astype(jnp.float32) * 2.0 - 1.0
    return 3.5 * signs


def page_slots(key):
    key_list = jax.random.split(jax.random.fold_in(key, 91), N_EP * N_CTX)
    orders = jax.vmap(lambda single: jax.random.permutation(single, POOL))(key_list)
    orders = orders.reshape(N_EP, N_CTX, R_DEV, PAGES_RANK).transpose(0, 2, 1, 3)
    return orders.reshape(ROWS, N_CTX, PAGES_RANK).astype(jnp.int32)


def background(key, shape):
    return jnp.clip(jax.random.normal(key, shape, jnp.float32), -4.0, 4.0)


def draw_queries(key, part):
    shared = shared_vector(key)
    key = jax.random.fold_in(key, 1)
    first_key, second_key, third_key = jax.random.split(key, 3)
    base_draw = background(first_key, (ROWS, HEADS, KDIM))
    aligned_mask = jax.random.randint(second_key, (ROWS, HEADS), 0, 16) == 0
    strength = jnp.array([4.0, 6.5, 9.0], jnp.float32)[jax.random.randint(third_key, (ROWS, HEADS), 0, 3)]
    aligned = strength[:, :, None] * shared[:, None, :]
    base_draw = jnp.where(aligned_mask[:, :, None], aligned, base_draw)
    return base_draw.astype(jnp.bfloat16)


def draw_new_key(key, part):
    shared = shared_vector(key)
    return shared.astype(jnp.bfloat16)


def draw_latent_cache(key, part):
    shared = shared_vector(key)
    page_list = page_slots(key)
    key = jax.random.fold_in(key, 3)
    first_key, second_key = jax.random.split(key)
    cache_draw = background(first_key, (N_CTX, SLOTS, PAGE, KDIM))
    noise_draw = jax.random.uniform(second_key, (ROWS, LAT), jnp.float32, -0.4, 0.4)
    copied = jnp.concatenate([shared[:, :LAT] + noise_draw, shared[:, LAT:]], axis=1)
    first_slot = page_list[:, 0, 0] + jnp.arange(ROWS, dtype=jnp.int32) // R_DEV * POOL
    cache_draw = cache_draw.at[0, first_slot, 0, :].set(copied)
    return cache_draw.astype(jnp.bfloat16)


def draw_page_table(key, part):
    page_list = page_slots(key)
    return page_list


def draw_lengths(key, part):
    key = jax.random.fold_in(key, 5)
    first_key, second_key = jax.random.split(key)
    sampled = jax.random.randint(first_key, (ROWS,), 1, CTXMAX + 1, dtype=jnp.int32)
    longest = jax.random.randint(second_key, (), 0, ROWS, dtype=jnp.int32)
    return sampled.at[longest].set(CTXMAX)


def draw_hidden_in(key, part):
    key = jax.random.fold_in(key, 6)
    column_ramp = jnp.arange(D, dtype=jnp.float32) / D
    sampled = jnp.clip(jax.random.normal(key, (ROWS, D), jnp.float32), -4.0, 4.0) * (0.5 + column_ramp)[None, :]
    return sampled.astype(jnp.bfloat16)


def draw_routes(key, part):
    key = jax.random.fold_in(key, 7)
    key_list = jax.random.split(key, N_EP)
    orders = jax.vmap(lambda single: jax.random.permutation(single, EXPERTS))(key_list)
    stride = EXPERTS // R_DEV
    spots = (jnp.arange(R_DEV, dtype=jnp.int32)[:, None] * stride + jnp.arange(TOP, dtype=jnp.int32)[None, :]) % EXPERTS
    chosen = orders[:, spots]
    return chosen.reshape(ROWS, TOP).astype(jnp.int32)


def levels(own_key, shape, cuts, low, top_value):
    loudness = 1.0
    for position, shards_of in cuts:
        heights = jax.random.uniform(jax.random.fold_in(jax.random.fold_in(own_key, 6), position), (shards_of,), jnp.float32, low / len(cuts), top_value / len(cuts))
        loudness = loudness * jnp.repeat(jnp.exp(heights), shape[position] // shards_of).reshape((-1,) + (1,) * (len(shape) - 1 - position))
    return loudness


def gaussian(rng, extent, deviation, reach, shards=(), held_as=jnp.bfloat16):
    values = jax.random.normal(rng, extent, jnp.float32) * deviation
    if len(shards) > 0:
        values = levels(rng, extent, shards, -0.22, 0.18) * values
    return jnp.clip(values, min=-reach, max=reach).astype(held_as)


def setup_inputs(seed: int = 0) -> dict:
    key_of = jax.random.split(jax.random.key(seed), 15)
    return {
        "queries": draw_queries(jax.random.fold_in(key_of[14], 71), 0),
        "new_key": draw_new_key(jax.random.fold_in(key_of[14], 71), 0),
        "latent_cache": draw_latent_cache(jax.random.fold_in(key_of[14], 71), 0),
        "page_table": draw_page_table(jax.random.fold_in(key_of[14], 71), 0),
        "lengths": draw_lengths(jax.random.fold_in(key_of[14], 71), 0),
        "hidden_in": draw_hidden_in(jax.random.fold_in(key_of[14], 71), 0),
        "w_uv": gaussian(key_of[6], (HEADS, LAT, VDIM), LAT ** -0.5, 0.25, ((0, 64),)),
        "w_out": gaussian(key_of[7], (HEADS * VDIM, D), (HEADS * VDIM) ** -0.5, 0.0625, ((0, 64), (1, 8))),
        "norm_gain": jnp.clip(1.0 + 0.18 * jax.random.normal(key_of[8], (D,), jnp.float32), 0.1, 1.9),
        "routes": draw_routes(jax.random.fold_in(key_of[14], 71), 0),
        "route_weight": jnp.clip(jnp.exp(math.log(0.6) - 1.7917595 * jax.random.uniform(key_of[10], (ROWS, TOP), jnp.float32) ** levels(key_of[10], (ROWS, TOP), ((0, 64),), -0.2, 0.2)), 0.1, 0.6),
        "w_gate": gaussian(key_of[11], (D, EXPERTS * FF), D ** -0.5, 0.0625, ((0, 8), (1, 64))),
        "w_up": gaussian(key_of[12], (D, EXPERTS * FF), D ** -0.5, 0.0625, ((0, 8), (1, 64))),
        "w_down": gaussian(key_of[13], (EXPERTS * FF, D), FF ** -0.5, 0.125, ((0, 64), (1, 8))),
    }


score_scale = 192.0 ** (-0.5)
epsilon = 1e-06

def reference(queries, new_key, latent_cache, page_table, lengths, hidden_in, w_uv, w_out, norm_gain, routes, route_weight, w_gate, w_up, w_down):
    positions = jnp.arange(CTXMAX, dtype=jnp.int32)
    page_number = positions // PAGE
    rank_of = page_number % N_CTX
    local_page = page_number // N_CTX
    offsets = positions % PAGE

    def attend_row(packed):
        row_query, row_new, row_pages, row_length, group_index = packed
        slot_ids = (row_pages[rank_of, local_page] + group_index * POOL).astype(jnp.int32)
        key_rows = latent_cache[rank_of, slot_ids, offsets].astype(jnp.float32)
        query32 = row_query.astype(jnp.float32)
        new32 = row_new.astype(jnp.float32)
        scores = jnp.einsum('hk,tk->ht', query32, key_rows, precision=lax.Precision.HIGHEST) * score_scale
        scores = jnp.where(positions[None, :] < row_length, scores, -jnp.inf)
        own_score = jnp.einsum('hk,k->h', query32, new32, precision=lax.Precision.HIGHEST) * score_scale
        peak_score = jnp.maximum(lax.optimization_barrier(jnp.max(scores, axis=1)), own_score)
        weights = jnp.exp(scores - peak_score[:, None])
        own_weight = jnp.exp(own_score - peak_score)
        totals = lax.optimization_barrier(jnp.sum(weights, axis=1)) + own_weight
        mixture = jnp.einsum('ht,tl->hl', weights, key_rows[:, :LAT], precision=lax.Precision.HIGHEST)
        mixture = mixture + own_weight[:, None] * new32[None, :LAT]
        return (mixture / totals[:, None]).astype(jnp.bfloat16)
    groups = jnp.arange(ROWS, dtype=jnp.int32) // R_DEV
    attended = lax.map(attend_row, (queries, new_key, page_table, lengths, groups))
    values = jnp.einsum('rhl,hlv->rhv', attended.astype(jnp.float32), w_uv.astype(jnp.float32)).astype(jnp.bfloat16)
    attention = jnp.dot(values.reshape(ROWS, HEADS * VDIM), w_out, preferred_element_type=jnp.float32)
    residual = hidden_in.astype(jnp.float32) + attention
    mean_sq = lax.optimization_barrier(jnp.mean(residual * residual, axis=1, keepdims=True))
    normed = (residual * lax.rsqrt(mean_sq + epsilon) * norm_gain.astype(jnp.float32)[None, :]).astype(jnp.bfloat16)
    per_expert = ROWS * TOP // EXPERTS

    def add_expert(expert, running):
        hit_mask = routes == expert
        chosen = jnp.any(hit_mask, axis=1)
        picked = jnp.nonzero(chosen, size=per_expert)[0].astype(jnp.int32)
        row_scale = lax.optimization_barrier(jnp.sum(jnp.where(hit_mask, route_weight, 0.0), axis=1))[picked]
        inputs = normed[picked]
        gate_val = jnp.dot(inputs, lax.dynamic_slice_in_dim(w_gate, expert * FF, FF, 1), preferred_element_type=jnp.float32)
        up_val = jnp.dot(inputs, lax.dynamic_slice_in_dim(w_up, expert * FF, FF, 1), preferred_element_type=jnp.float32)
        middle = (jax.nn.silu(gate_val) * up_val).astype(jnp.bfloat16)
        result = jnp.dot(middle, lax.dynamic_slice_in_dim(w_down, expert * FF, FF, 0), preferred_element_type=jnp.float32)
        return running.at[picked].add(row_scale[:, None] * result)
    routed = lax.fori_loop(jnp.int32(0), jnp.int32(EXPERTS), add_expert, jnp.zeros((ROWS, D), jnp.float32))
    return (attention.astype(jnp.bfloat16), (residual + routed).astype(jnp.bfloat16))
```

```python
import jax
import jax.numpy as jnp
from jax import lax
from jax.experimental import pallas as pl
from jax.experimental.pallas import tpu as pltpu
from jax.sharding import PartitionSpec as P

D = 7168
LAT = 512
KDIM = 576
TOP = 8
N_CTX = 8
N_Y = 4
N_Z = 16
COLS = 896
NJ = 7
HALF = 512

score_scale = 192.0 ** (-0.5)
epsilon = 1e-06
very_low = -1e30

MESH = pl.DeviceIdType.MESH
F32 = jnp.float32
BF16 = jnp.bfloat16


def dot(a, b):
    return jnp.dot(a, b, preferred_element_type=F32)


def dot_nt(a, b):
    return lax.dot_general(a, b, (((1,), (1,)), ((), ())), preferred_element_type=F32)


def iota(shape, dim):
    return lax.broadcasted_iota(jnp.int32, shape, dim)


def three_parts(x, shape):
    hi = x.astype(BF16).astype(F32)
    mid = (x - hi).astype(BF16).astype(F32)
    low = x - hi - mid
    lane = iota(shape, 1)
    zero = jnp.zeros(shape, F32)
    return jnp.where(lane == 0, hi, jnp.where(lane == 1, mid, jnp.where(lane == 2, low, zero)))


def kernel(
    page_table,
    lengths,
    routes,
    route_weight,
    new_key,
    hidden,
    gain,
    queries,
    cache,
    w_uv,
    w_out,
    w_gate,
    w_up,
    w_down,
    attn_out,
    layer_out,
    q_vm,
    cache_vm,
    wuv_vm,
    wout_vm,
    gate_vm,
    up_vm,
    down_vm,
    nk_scr,
    att_scr,
    tile_scr,
    lhs_scr,
    wide_scr,
    z_scr,
    small_scr,
    hid_scr,
    gain_scr,
    res_scr,
    col_scr,
    sel_scr,
    comb_scr,
    info_send,
    info_recv,
    p2_send,
    p2_recv,
    p3_send,
    p3_recv,
    p4_send,
    p4_recv,
    p5_send,
    p5_recv,
    p6_send,
    p6_recv,
    p6b_send,
    xe,
    p7_send,
    p7_recv,
    p8_send,
    mid_all,
    p9_send,
    p9_recv,
    p10_send,
    p10_recv,
    lsem,
    wo_s,
    wo_r,
    info_s,
    info_r,
    p2_s,
    p2_r,
    p3_s,
    p3_r,
    p4_s,
    p4_r,
    p5_s,
    p5_r,
    p6_s,
    p6_r,
    p6b_s,
    p6b_r,
    p7_s,
    p7_r,
    p8_s,
    p8_r,
    p9_s,
    p9_r,
    p10_s,
    p10_r,
):
    c = lax.axis_index("ctx")
    ep = lax.axis_index("ep")
    y = ep // N_Z
    z = ep % N_Z
    g = ep // 8
    s8 = ep % 8

    def remote(src, dst, ssem, rsem, to_ctx, to_ep):
        return pltpu.make_async_remote_copy(
            src_ref=src,
            dst_ref=dst,
            send_sem=ssem,
            recv_sem=rsem,
            device_id={"ctx": to_ctx, "ep": to_ep},
            device_id_type=MESH,
        )

    def each(count, step):
        def body(i, carry):
            step(i)
            return carry

        lax.fori_loop(0, count, body, 0)

    loads = [
        pltpu.make_async_copy(src, dst, lsem.at[i])
        for i, (src, dst) in enumerate(
            [
                (queries, q_vm),
                (cache, cache_vm),
                (w_uv, wuv_vm),
                (w_out, wout_vm.at[y]),
                (w_gate, gate_vm),
                (w_up, up_vm),
                (w_down, down_vm),
            ]
        )
    ]
    for load in loads:
        load.start()

    barrier = pltpu.get_barrier_semaphore()

    def greet(to_ctx, to_ep):
        pl.semaphore_signal(
            barrier, inc=1, device_id={"ctx": to_ctx, "ep": to_ep}, device_id_type=MESH
        )

    def greet_plane(i):
        k = i + 1
        greet((c + k % N_CTX) % N_CTX, (y + k // N_CTX) % N_Y * N_Z + z)

    each(N_CTX * N_Y - 1, greet_plane)
    each(N_Z - 1, lambda i: greet(c, y * N_Z + (z + i + 1) % N_Z))

    def greet_swap(i):
        @pl.when(jnp.logical_not((c == g) & (i == s8)))
        def _():
            greet(g, c * 8 + i)

    each(8, greet_swap)

    row = iota((32, 128), 0)
    expert = (row // 2) % 4 * 4 + row // 8
    place = row % 2
    before = jnp.zeros((32, 128), jnp.int32)
    pick = jnp.zeros((32, 128), F32)
    weight = jnp.zeros((32, 128), F32)
    for r in range(4):
        named = jnp.zeros((32, 128), jnp.int32)
        w_r = jnp.zeros((32, 128), F32)
        for k in range(TOP):
            hit = expert == routes[r, k]
            named = jnp.where(hit, 1, named)
            w_r = jnp.where(hit, route_weight[r, k], w_r)
        taken = (named == 1) & (before == place)
        pick = jnp.where(taken, float(r), pick)
        weight = jnp.where(taken, w_r, weight)
        before = before + named
    info = jnp.where(iota((32, 128), 1) < 64, pick, weight)
    info_send[...] = info.reshape(4, 8, 128)
    info_recv[z] = info_send[z // 4]

    small_scr[0:4, :] = jnp.zeros((4, 128), F32)
    hid_scr[28:32, :] = jnp.zeros((4, 128), F32)
    gain_scr[28:32, :] = jnp.zeros((4, 128), F32)
    hid32 = hidden[...].astype(F32)
    for j in range(NJ):
        hid_scr[4 * j : 4 * j + 4, :] = hid32[:, 128 * j : 128 * j + 128]
        gain_scr[4 * j : 4 * j + 4, :] = jnp.broadcast_to(
            gain[:, 128 * j : 128 * j + 128], (4, 128)
        )
    nk_scr[...] = jnp.zeros((128, KDIM), BF16)
    nk_scr[0:4, :] = new_key[...]
    for zz in range(N_Z):
        z_scr[32 * zz + 28 : 32 * zz + 32, :] = jnp.zeros((4, 128), F32)

    col = iota((1, 1024), 1)
    slot = col // 64
    owner = jnp.full((1, 1024), -1, jnp.int32)
    for r in range(4):
        for p in range(4):
            position = (p * N_CTX + c) * 64 + col % 64
            good = (slot == page_table[r, 0, p]) & (position < lengths[r])
            owner = jnp.where(good, r, owner)
    i0 = iota((256, 256), 0)
    shuffle = jnp.where((i0 % 4) * 64 + i0 // 4 == iota((256, 256), 1), 1.0, 0.0).astype(BF16)
    loads[0].wait()
    q = dot(shuffle, q_vm[...].reshape(256, KDIM)).astype(BF16)
    loads[1].wait()
    keys = cache_vm[...].reshape(1024, KDIM)
    scores = dot_nt(q, keys) * score_scale
    fresh = dot_nt(q, nk_scr[...]) * score_scale
    mask = owner == iota((256, 1024), 0) % 4
    mask_new = iota((256, 128), 1) + 1024 * c == iota((256, 128), 0) % 4
    peak = jnp.maximum(
        jnp.max(jnp.where(mask, scores, very_low), axis=1, keepdims=True),
        jnp.max(jnp.where(mask_new, fresh, very_low), axis=1, keepdims=True),
    )
    weights = jnp.where(mask, jnp.exp(scores - peak), 0.0).astype(BF16)
    weights_new = jnp.where(mask_new, jnp.exp(fresh - peak), 0.0).astype(BF16)
    total = jnp.sum(weights.astype(F32), axis=1, keepdims=True) + jnp.sum(
        weights_new.astype(F32), axis=1, keepdims=True
    )
    mixture = dot(weights, keys[:, :LAT]) + dot(weights_new, nk_scr[:, :LAT])
    some = total > 0.0
    total = jnp.where(some, total, 1.0)
    logsum = jnp.where(some, peak + jnp.log(total), very_low)
    p2_send[:, :, :LAT] = (mixture / total).astype(BF16).reshape(N_CTX, 32, LAT)
    p2_send[:, :, LAT:] = three_parts(logsum, (256, 128)).astype(BF16).reshape(N_CTX, 32, 128)

    pl.semaphore_wait(
        barrier, N_CTX * N_Y - 1 + N_Z - 1 + 8 - jnp.where(c == g, 1, 0).astype(jnp.int32)
    )

    def p2_copy(i):
        to = (c + i + 1) % N_CTX
        return remote(p2_send.at[to], p2_recv.at[i], p2_s.at[i], p2_r.at[i], to, ep)

    each(N_CTX - 1, lambda i: p2_copy(i).start())

    def info_copy(i):
        to = (z + i + 1) % N_Z
        return remote(
            info_send.at[to // 4], info_recv.at[z], info_s.at[i], info_r.at[i], c, y * N_Z + to
        )

    def info_arrival(i):
        frm = (z + N_Z - i - 1) % N_Z
        return remote(info_send.at[0], info_recv.at[frm], info_s.at[i], info_r.at[i], c, y * N_Z + frm)

    each(N_Z - 1, lambda i: info_copy(i).start())

    def wo_copy(i):
        to = (y + i + 1) % N_Y
        return remote(w_out, wout_vm.at[y], wo_s.at[i], wo_r.at[i], c, to * N_Z + z)

    def wo_arrival(i):
        frm = (y + N_Y - i - 1) % N_Y
        return remote(w_out, wout_vm.at[frm], wo_s.at[i], wo_r.at[i], c, frm * N_Z + z)

    each(N_Y - 1, lambda i: wo_copy(i).start())

    each(N_CTX - 1, lambda i: p2_copy(i).wait_recv())
    parts = [p2_send[c]] + [p2_recv[i] for i in range(N_CTX - 1)]
    logs = [jnp.sum(p[:, LAT:].astype(F32), axis=1, keepdims=True) for p in parts]
    top = logs[0]
    for l in logs[1:]:
        top = jnp.maximum(top, l)
    above = jnp.zeros((32, LAT), F32)
    below = jnp.zeros((32, 1), F32)
    for p, l in zip(parts, logs):
        f = jnp.exp(l - top)
        above = above + f * p[:, :LAT].astype(F32)
        below = below + f
    att_scr[...] = above / below
    for i in range(8):
        for j in range(4):
            tile_scr[16 * i + 4 * j : 16 * i + 4 * j + 4, :] = att_scr[
                4 * i : 4 * i + 4, 128 * j : 128 * j + 128
            ]
    p3_send[...] = tile_scr[...].astype(BF16).reshape(8, 16, 128)

    def p3_copy(i):
        return remote(
            p3_send.at[i], p3_recv.at[s8], p3_s.at[i], p3_r.at[s8], g, c * 8 + i
        )

    def p3_arrival(i):
        return remote(p3_send.at[i], p3_recv.at[i], p3_s.at[i], p3_r.at[i], g, c * 8 + i)

    def p3_each(step):
        def one(i):
            @pl.when(jnp.logical_not((c == g) & (i == s8)))
            def _():
                step(i)

        each(8, one)

    p3_each(lambda i: p3_copy(i).start())

    @pl.when(c == g)
    def _():
        p3_recv[s8] = p3_send[s8]

    loads[2].wait()
    p3_each(lambda i: p3_arrival(i).wait_recv())
    tile_scr[...] = p3_recv[...].astype(F32).reshape(128, 128)
    for i in range(8):
        for j in range(4):
            lhs_scr[4 * i : 4 * i + 4, 128 * j : 128 * j + 128] = tile_scr[
                16 * i + 4 * j : 16 * i + 4 * j + 4, :
            ]
    values = dot(lhs_scr[...].astype(BF16), wuv_vm[0]).astype(BF16)
    p4_send[...] = values

    home = c // 2
    mine = home == y
    slot4 = y * 2 + c % 2

    def p4_copy(i):
        return remote(p4_send, p4_recv.at[slot4], p4_s.at[i], p4_r.at[slot4], i, home * N_Z + z)

    def p4_arrival(i):
        return remote(
            p4_send, p4_recv.at[i], p4_s.at[i], p4_r.at[i], y * 2 + i % 2, i // 2 * N_Z + z
        )

    def p4_sends(step):
        def one(i):
            @pl.when(jnp.logical_not(mine & (i == c)))
            def _():
                step(i)

        each(8, one)

    def p4_arrives(step):
        def one(i):
            @pl.when(jnp.logical_not(mine & (i == slot4)))
            def _():
                step(i)

        each(8, one)

    p4_sends(lambda i: p4_copy(i).start())

    @pl.when(mine)
    def _():
        p4_recv[slot4] = p4_send[...]

    each(N_Z - 1, lambda i: info_arrival(i).wait_recv())
    for k in range(8):
        col_scr[16 * k : 16 * k + 16, :] = info_recv[:, k, :]
    pick_col = col_scr[:, 0:1].astype(jnp.int32)
    weight_col = col_scr[:, 64:65]
    source = iota((128, 1), 0) % 16
    target = source * 32 + pick_col
    lane = iota((128, 512), 1)
    for j in range(8):
        sel_scr[128 * j : 128 * j + 128, :] = jnp.where(lane == target + 4 * j, 1.0, 0.0).astype(BF16)
    spread = jnp.where(iota((128, 128), 1) == source * 4 + pick_col, weight_col, 0.0)
    comb = jnp.transpose(spread)[0:64, :]
    comb_hi = comb.astype(BF16)
    comb_scr[0] = comb_hi
    comb_scr[1] = (comb - comb_hi.astype(F32)).astype(BF16)

    loads[3].wait()
    each(N_Y - 1, lambda i: wo_arrival(i).wait_recv())
    p4_arrives(lambda i: p4_arrival(i).wait_recv())
    lhs = jnp.concatenate(
        [p4_recv[2 * k : 2 * k + 2].reshape(64, 128) for k in range(N_Y)], axis=1
    )

    def to_tiles(values32, send):
        wide_scr[...] = values32
        for zz in range(N_Z):
            for j in range(NJ):
                z_scr[32 * zz + 4 * j : 32 * zz + 4 * j + 4, :] = wide_scr[
                    4 * zz : 4 * zz + 4, 128 * j : 128 * j + 128
                ]
        send[...] = z_scr[...].astype(BF16).reshape(N_Z, 32, 128)

    def z_scatter(send, recv, ssem, rsem):
        def copy(i):
            to = (z + i + 1) % N_Z
            return remote(send.at[to], recv.at[i], ssem.at[i], rsem.at[i], c, y * N_Z + to)

        each(N_Z - 1, lambda i: copy(i).start())
        each(N_Z - 1, lambda i: copy(i).wait_recv())
        total = z_scr[pl.ds(pl.multiple_of(z * 32, 32), 32), :]
        for i in range(N_Z - 1):
            total = total + recv[i].astype(F32)
        return total, copy

    to_tiles(dot(lhs, wout_vm[...].reshape(512, COLS)), p5_send)
    attention, p5_copy = z_scatter(p5_send, p5_recv, p5_s, p5_r)
    residual = hid_scr[...] + attention
    res_scr[...] = residual
    small_scr[...] = residual * residual
    squares = small_scr[0:4, :]
    for j in range(1, NJ):
        squares = squares + small_scr[4 * j : 4 * j + 4, :]
    squares = jnp.sum(squares, axis=1, keepdims=True)
    small_scr[...] = residual * gain_scr[...]
    small_scr[28:32, :] = three_parts(squares, (4, 128))
    scaled = small_scr[...].astype(BF16)
    p6_send[...] = scaled
    p6_recv[z] = scaled

    def p6_copy(i):
        to = (z + i + 1) % N_Z
        return remote(p6_send, p6_recv.at[z], p6_s.at[i], p6_r.at[i], c, y * N_Z + to)

    def p6_arrival(i):
        frm = (z + N_Z - i - 1) % N_Z
        return remote(p6_send, p6_recv.at[frm], p6_s.at[i], p6_r.at[i], c, y * N_Z + frm)

    each(N_Z - 1, lambda i: p6_copy(i).start())
    small_scr[...] = attention
    for j in range(NJ):
        attn_out[:, 128 * j : 128 * j + 128] = small_scr[4 * j : 4 * j + 4, :].astype(BF16)
    each(N_Z - 1, lambda i: p6_arrival(i).wait_recv())

    picked = dot(sel_scr[...], p6_recv[...].reshape(512, 128)).astype(BF16)
    for j in range(8):
        p6b_send[:, :, 128 * j : 128 * j + 128] = picked[128 * j : 128 * j + 128, :].reshape(
            N_Y, 32, 128
        )

    def y_copy(send, recv, ssem, rsem):
        def copy(i):
            to = (y + i + 1) % N_Y
            return remote(send.at[to], recv.at[y], ssem.at[i], rsem.at[i], c, to * N_Z + z)

        def arrival(i):
            frm = (y + N_Y - i - 1) % N_Y
            return remote(send.at[y], recv.at[frm], ssem.at[i], rsem.at[i], c, frm * N_Z + z)

        each(N_Y - 1, lambda i: copy(i).start())
        recv[y] = send[y]
        each(N_Y - 1, lambda i: arrival(i).wait_recv())
        return copy

    p6b_copy = y_copy(p6b_send, xe, p6b_s, p6b_r)

    rows = xe[...].reshape(128, 1024)
    loads[4].wait()
    loads[5].wait()
    p7_send[:, :, :HALF] = dot(rows[:, :COLS], gate_vm[...]).astype(BF16).reshape(N_CTX, 16, HALF)
    p7_send[:, :, HALF : 2 * HALF] = (
        dot(rows[:, :COLS], up_vm[...]).astype(BF16).reshape(N_CTX, 16, HALF)
    )
    p7_send[:, :, 2 * HALF :] = rows[:, COLS:].reshape(N_CTX, 16, 128)

    def p7_copy(i):
        to = (c + i + 1) % N_CTX
        return remote(p7_send.at[to], p7_recv.at[i], p7_s.at[i], p7_r.at[i], to, ep)

    each(N_CTX - 1, lambda i: p7_copy(i).start())
    each(N_CTX - 1, lambda i: p7_copy(i).wait_recv())
    sums = p7_send[c].astype(F32)
    for i in range(N_CTX - 1):
        sums = sums + p7_recv[i].astype(F32)
    mean = jnp.sum(sums[:, 2 * HALF :], axis=1, keepdims=True) / D
    scale = lax.rsqrt(mean + epsilon)
    gate = sums[:, :HALF] * scale
    up = sums[:, HALF : 2 * HALF] * scale
    middle = (gate / (1.0 + jnp.exp(-gate)) * up).astype(BF16)
    p8_send[...] = middle
    mid_all[c] = middle

    def p8_copy(i):
        to = (c + i + 1) % N_CTX
        return remote(p8_send, mid_all.at[c], p8_s.at[i], p8_r.at[i], to, ep)

    def p8_arrival(i):
        frm = (c + N_CTX - i - 1) % N_CTX
        return remote(p8_send, mid_all.at[frm], p8_s.at[i], p8_r.at[i], frm, ep)

    each(N_CTX - 1, lambda i: p8_copy(i).start())
    loads[6].wait()
    each(N_CTX - 1, lambda i: p8_arrival(i).wait_recv())

    produced = dot(mid_all[...].reshape(128, HALF), down_vm[...])
    p9_send[...] = produced.astype(BF16).reshape(N_Y, 32, COLS)
    p9_copy = y_copy(p9_send, p9_recv, p9_s, p9_r)
    back = p9_recv[...].reshape(128, COLS)
    to_tiles(dot(comb_scr[0], back) + dot(comb_scr[1], back), p10_send)
    routed, p10_copy = z_scatter(p10_send, p10_recv, p10_s, p10_r)
    small_scr[...] = res_scr[...] + routed
    for j in range(NJ):
        layer_out[:, 128 * j : 128 * j + 128] = small_scr[4 * j : 4 * j + 4, :].astype(BF16)

    each(N_CTX - 1, lambda i: p2_copy(i).wait_send())
    each(N_Z - 1, lambda i: info_copy(i).wait_send())
    each(N_Y - 1, lambda i: wo_copy(i).wait_send())
    p3_each(lambda i: p3_copy(i).wait_send())
    p4_sends(lambda i: p4_copy(i).wait_send())
    each(N_Z - 1, lambda i: p5_copy(i).wait_send())
    each(N_Z - 1, lambda i: p6_copy(i).wait_send())
    each(N_Y - 1, lambda i: p6b_copy(i).wait_send())
    each(N_CTX - 1, lambda i: p7_copy(i).wait_send())
    each(N_CTX - 1, lambda i: p8_copy(i).wait_send())
    each(N_Y - 1, lambda i: p9_copy(i).wait_send())
    each(N_Z - 1, lambda i: p10_copy(i).wait_send())


def per_device(
    queries,
    new_key,
    latent_cache,
    page_table,
    lengths,
    hidden_in,
    w_uv,
    w_out,
    norm_gain,
    routes,
    route_weight,
    w_gate,
    w_up,
    w_down,
):
    smem = pl.BlockSpec(memory_space=pltpu.SMEM)
    vmem = pl.BlockSpec(memory_space=pltpu.VMEM)
    anywhere = pl.BlockSpec(memory_space=pl.ANY)
    dma = pltpu.SemaphoreType.DMA
    scratch = [
        pltpu.VMEM((4, 64, KDIM), BF16),
        pltpu.VMEM((1, 16, 64, KDIM), BF16),
        pltpu.VMEM((1, LAT, 128), BF16),
        pltpu.VMEM((N_Y, 128, COLS), BF16),
        pltpu.VMEM((COLS, HALF), BF16),
        pltpu.VMEM((COLS, HALF), BF16),
        pltpu.VMEM((HALF, COLS), BF16),
        pltpu.VMEM((128, KDIM), BF16),
        pltpu.VMEM((32, LAT), F32),
        pltpu.VMEM((128, 128), F32),
        pltpu.VMEM((32, LAT), F32),
        pltpu.VMEM((64, COLS), F32),
        pltpu.VMEM((512, 128), F32),
        pltpu.VMEM((32, 128), F32),
        pltpu.VMEM((32, 128), F32),
        pltpu.VMEM((32, 128), F32),
        pltpu.VMEM((32, 128), F32),
        pltpu.VMEM((128, 128), F32),
        pltpu.VMEM((1024, 512), BF16),
        pltpu.VMEM((2, 64, 128), BF16),
        pltpu.VMEM((4, 8, 128), F32),
        pltpu.VMEM((N_Z, 8, 128), F32),
        pltpu.VMEM((N_CTX, 32, 640), BF16),
        pltpu.VMEM((N_CTX - 1, 32, 640), BF16),
        pltpu.VMEM((8, 16, 128), BF16),
        pltpu.VMEM((8, 16, 128), BF16),
        pltpu.VMEM((32, 128), BF16),
        pltpu.VMEM((8, 32, 128), BF16),
        pltpu.VMEM((N_Z, 32, 128), BF16),
        pltpu.VMEM((N_Z - 1, 32, 128), BF16),
        pltpu.VMEM((32, 128), BF16),
        pltpu.VMEM((N_Z, 32, 128), BF16),
        pltpu.VMEM((N_Y, 32, 1024), BF16),
        pltpu.VMEM((N_Y, 32, 1024), BF16),
        pltpu.VMEM((N_CTX, 16, 1152), BF16),
        pltpu.VMEM((N_CTX - 1, 16, 1152), BF16),
        pltpu.VMEM((16, HALF), BF16),
        pltpu.VMEM((N_CTX, 16, HALF), BF16),
        pltpu.VMEM((N_Y, 32, COLS), BF16),
        pltpu.VMEM((N_Y, 32, COLS), BF16),
        pltpu.VMEM((N_Z, 32, 128), BF16),
        pltpu.VMEM((N_Z - 1, 32, 128), BF16),
        dma((7,)),
    ]
    for count in (3, 15, 7, 8, 8, 15, 15, 3, 7, 7, 3, 15):
        scratch += [dma((count,)), dma((count,))]
    out = jax.ShapeDtypeStruct((4, COLS), BF16)
    return pl.pallas_call(
        kernel,
        out_shape=(out, out),
        in_specs=[smem] * 4 + [vmem] * 3 + [anywhere] * 7,
        out_specs=(vmem, vmem),
        scratch_shapes=scratch,
        compiler_params=pltpu.CompilerParams(
            collective_id=0, has_side_effects=True, vmem_limit_bytes=40 * 1024 * 1024
        ),
    )(
        page_table,
        lengths,
        routes,
        route_weight,
        new_key,
        hidden_in,
        norm_gain.reshape(1, COLS),
        queries,
        latent_cache,
        w_uv,
        w_out,
        w_gate,
        w_up,
        w_down,
    )


def solution(mesh):
    placed = (
        P("ep", None, None),
        P("ep", None),
        P("ctx", "ep", None, None),
        P("ep", "ctx", None),
        P("ep"),
        P("ep", "ctx"),
        P("ep", None, None),
        P("ep", "ctx"),
        P("ctx"),
        P("ep", None),
        P("ep", None),
        P("ctx", "ep"),
        P("ctx", "ep"),
        P("ep", "ctx"),
    )
    return jax.shard_map(
        per_device,
        mesh=mesh,
        in_specs=placed,
        out_specs=(P("ep", "ctx"), P("ep", "ctx")),
        check_vma=False,
    )
```

```python
import jax
import jax.numpy as jnp
from jax import lax
from jax.experimental import pallas as pl
from jax.experimental.pallas import tpu as pltpu
from jax.sharding import PartitionSpec as P

D = 7168
LAT = 512
KDIM = 576
TOP = 8
N_CTX = 8
N_Y = 4
N_Z = 16
COLS = 896
NJ = 7
HALF = 512

score_scale = 192.0 ** (-0.5)
epsilon = 1e-06
very_low = -1e30

MESH = pl.DeviceIdType.MESH
F32 = jnp.float32
BF16 = jnp.bfloat16


def dot(a, b):
    return jnp.dot(a, b, preferred_element_type=F32)


def dot_nt(a, b):
    return lax.dot_general(a, b, (((1,), (1,)), ((), ())), preferred_element_type=F32)


def iota(shape, dim):
    return lax.broadcasted_iota(jnp.int32, shape, dim)


def three_parts(x, shape):
    hi = x.astype(BF16).astype(F32)
    mid = (x - hi).astype(BF16).astype(F32)
    low = x - hi - mid
    lane = iota(shape, 1)
    zero = jnp.zeros(shape, F32)
    return jnp.where(lane == 0, hi, jnp.where(lane == 1, mid, jnp.where(lane == 2, low, zero)))


def kernel(
    page_table_in,
    lengths_in,
    routes_in,
    route_weight_in,
    new_key_in,
    hidden_in,
    gain_in,
    queries,
    cache,
    w_uv,
    w_out,
    w_gate,
    w_up,
    w_down,
    attn_out,
    layer_out,
    page_table,
    lengths,
    routes,
    route_weight,
    new_key,
    hidden,
    gain,
    q_vm,
    cache_vm,
    wuv_vm,
    wout_vm,
    gate_vm,
    up_vm,
    down_vm,
    nk_scr,
    att_scr,
    tile_scr,
    lhs_scr,
    wide_scr,
    z_scr,
    small_scr,
    hid_scr,
    gain_scr,
    res_scr,
    col_scr,
    sel_scr,
    comb_scr,
    info_send,
    info_recv,
    p2_send,
    p2_recv,
    p3_send,
    p3_recv,
    p4_send,
    p4_recv,
    p5_send,
    p5_recv,
    p6_send,
    p6_recv,
    p6b_send,
    xe,
    p7_send,
    p7_recv,
    p8_send,
    mid_all,
    p9_send,
    p9_recv,
    p10_send,
    p10_recv,
    lsem,
    wo_s,
    wo_r,
    info_s,
    info_r,
    p2_s,
    p2_r,
    p3_s,
    p3_r,
    p4_s,
    p4_r,
    p5_s,
    p5_r,
    p6_s,
    p6_r,
    p6b_s,
    p6b_r,
    p7_s,
    p7_r,
    p8_s,
    p8_r,
    p9_s,
    p9_r,
    p10_s,
    p10_r,
):
    c = lax.axis_index("ctx")
    ep = lax.axis_index("ep")
    y = ep // N_Z
    z = ep % N_Z
    g = ep // 8
    s8 = ep % 8

    def remote(src, dst, ssem, rsem, to_ctx, to_ep):
        return pltpu.make_async_remote_copy(
            src_ref=src,
            dst_ref=dst,
            send_sem=ssem,
            recv_sem=rsem,
            device_id={"ctx": to_ctx, "ep": to_ep},
            device_id_type=MESH,
        )

    def each(count, step):
        def body(i, carry):
            step(i)
            return carry

        lax.fori_loop(0, count, body, 0)

    loads = [
        pltpu.make_async_copy(src, dst, lsem.at[i])
        for i, (src, dst) in enumerate(
            [
                (queries, q_vm),
                (cache, cache_vm),
                (w_uv, wuv_vm),
                (w_out, wout_vm.at[y]),
                (w_gate, gate_vm),
                (w_up, up_vm),
                (w_down, down_vm),
                (page_table_in, page_table),
                (lengths_in, lengths),
                (routes_in, routes),
                (route_weight_in, route_weight),
                (new_key_in, new_key),
                (hidden_in, hidden),
                (gain_in, gain),
            ]
        )
    ]
    for load in loads[:2] + loads[7:] + loads[2:7]:
        load.start()
    pending = []

    def finish():
        for wait in pending:
            wait()

    def landed(buffer, sem):
        pltpu.make_async_copy(buffer, buffer, sem).wait()

    def z_step(i):
        return 8 + (i + 1) // 2 * (1 - 2 * (i % 2))

    barrier = pltpu.get_barrier_semaphore()

    def greet(to_ctx, to_ep):
        pl.semaphore_signal(
            barrier, inc=1, device_id={"ctx": to_ctx, "ep": to_ep}, device_id_type=MESH
        )

    def greet_plane(i):
        k = i + 1
        greet((c + k % N_CTX) % N_CTX, (y + k // N_CTX) % N_Y * N_Z + z)

    g_to = (g + 4) % 8
    c_from = (c + 4) % 8
    each(N_Z - 1, lambda i: greet(c, y * N_Z + (z + z_step(i)) % N_Z))
    each(8, lambda i: greet(g_to, c * 8 + i))
    each(8, lambda i: greet(g, c_from * 8 + i))
    each(N_CTX * N_Y - 1, greet_plane)

    for load in loads[7:]:
        load.wait()

    row = iota((32, 128), 0)
    expert = ((row // 2) % 4 + y) % 4 * 4 + row // 8
    place = row % 2
    before = jnp.zeros((32, 128), jnp.int32)
    pick = jnp.zeros((32, 128), F32)
    weight = jnp.zeros((32, 128), F32)
    for r in range(4):
        named = jnp.zeros((32, 128), jnp.int32)
        w_r = jnp.zeros((32, 128), F32)
        for k in range(TOP):
            hit = expert == routes[r, k]
            named = jnp.where(hit, 1, named)
            w_r = jnp.where(hit, route_weight[r, k], w_r)
        taken = (named == 1) & (before == place)
        pick = jnp.where(taken, float(r), pick)
        weight = jnp.where(taken, w_r, weight)
        before = before + named
    info = jnp.where(iota((32, 128), 1) < 64, pick, weight)
    info_send[...] = info.reshape(4, 8, 128)
    info_recv[0] = info_send[z // 4]

    small_scr[0:4, :] = jnp.zeros((4, 128), F32)
    hid_scr[28:32, :] = jnp.zeros((4, 128), F32)
    gain_scr[28:32, :] = jnp.zeros((4, 128), F32)
    hid32 = hidden[...].astype(F32)
    for j in range(NJ):
        hid_scr[4 * j : 4 * j + 4, :] = hid32[:, 128 * j : 128 * j + 128]
        gain_scr[4 * j : 4 * j + 4, :] = jnp.broadcast_to(
            gain[128 * j : 128 * j + 128].reshape(1, 128), (4, 128)
        )
    nk_scr[...] = jnp.zeros((128, KDIM), BF16)
    nk_scr[0:4, :] = new_key[...]
    for zz in range(N_Z):
        z_scr[32 * zz + 28 : 32 * zz + 32, :] = jnp.zeros((4, 128), F32)

    col = iota((1, 1024), 1)
    slot = col // 64
    owner = jnp.full((1, 1024), -1, jnp.int32)
    for r in range(4):
        for p in range(4):
            position = (p * N_CTX + c) * 64 + col % 64
            good = (slot == page_table[r, 0, p]) & (position < lengths[r])
            owner = jnp.where(good, r, owner)
    i0 = iota((256, 256), 0)
    shuffle = jnp.where((i0 % 4) * 64 + i0 // 4 == iota((256, 256), 1), 1.0, 0.0).astype(BF16)
    loads[0].wait()
    q = dot(shuffle, q_vm[...].reshape(256, KDIM)).astype(BF16)
    loads[1].wait()
    keys = cache_vm[...].reshape(1024, KDIM)
    scores = dot_nt(q, keys) * score_scale
    fresh = dot_nt(q, nk_scr[...]) * score_scale
    mask = owner == iota((256, 1024), 0) % 4
    mask_new = iota((256, 128), 1) + 1024 * c == iota((256, 128), 0) % 4
    peak = jnp.maximum(
        jnp.max(jnp.where(mask, scores, very_low), axis=1, keepdims=True),
        jnp.max(jnp.where(mask_new, fresh, very_low), axis=1, keepdims=True),
    )
    weights = jnp.where(mask, jnp.exp(scores - peak), 0.0).astype(BF16)
    weights_new = jnp.where(mask_new, jnp.exp(fresh - peak), 0.0).astype(BF16)
    total = jnp.sum(weights.astype(F32), axis=1, keepdims=True) + jnp.sum(
        weights_new.astype(F32), axis=1, keepdims=True
    )
    mixture = dot(weights, keys[:, :LAT]) + dot(weights_new, nk_scr[:, :LAT])
    some = total > 0.0
    total = jnp.where(some, total, 1.0)
    logsum = jnp.where(some, peak + jnp.log(total), very_low)
    p2_send[:, :, :LAT] = (mixture / total).astype(BF16).reshape(N_CTX, 32, LAT)
    p2_send[:, :, LAT:] = three_parts(logsum, (256, 128)).astype(BF16).reshape(N_CTX, 32, 128)

    pl.semaphore_wait(barrier, N_CTX * N_Y - 1 + N_Z - 1 + 16)

    def ctx_step(k):
        return (c // 2 + k // 2) % 4 * 2 + (c + k) % 2

    def ctx_back(k):
        return (c // 2 + 4 - k // 2) % 4 * 2 + (c + k) % 2

    ctx_order = (4, 5, 2, 3, 6, 7, 1)
    y_order = (2, 1, 3)

    def ctx_scatter(send, recv, ssem, rsem):
        for k in ctx_order:
            to = ctx_step(k)
            remote(send.at[to], recv.at[k - 1], ssem, rsem, to, ep).start()
        pending.append(lambda: landed(recv, ssem))

    ctx_scatter(p2_send, p2_recv, p2_s, p2_r)

    def info_copy(i):
        step = z_step(i)
        to = (z + step) % N_Z
        remote(
            info_send.at[to // 4], info_recv.at[step], info_s, info_r, c, y * N_Z + to
        ).start()

    each(N_Z - 1, info_copy)
    pending.append(lambda: landed(info_recv.at[1:N_Z], info_s))

    for k in y_order:
        remote(
            w_out, wout_vm.at[y], wo_s.at[k - 1], wo_r.at[k - 1], c, (y + k) % N_Y * N_Z + z
        ).start()
    for k in y_order:
        pending.append(
            remote(
                w_out, wout_vm.at[y], wo_s.at[k - 1], wo_r.at[k - 1], c, (y + k) % N_Y * N_Z + z
            ).wait_send
        )

    def wo_arrival(k):
        frm = (y + N_Y - k) % N_Y
        return remote(w_out, wout_vm.at[frm], wo_s.at[k - 1], wo_r.at[k - 1], c, frm * N_Z + z)

    landed(p2_recv, p2_r)
    parts = [p2_send[c]] + [p2_recv[i] for i in range(N_CTX - 1)]
    logs = [jnp.sum(p[:, LAT:].astype(F32), axis=1, keepdims=True) for p in parts]
    top = logs[0]
    for l in logs[1:]:
        top = jnp.maximum(top, l)
    above = jnp.zeros((32, LAT), F32)
    below = jnp.zeros((32, 1), F32)
    for p, l in zip(parts, logs):
        f = jnp.exp(l - top)
        above = above + f * p[:, :LAT].astype(F32)
        below = below + f
    att_scr[...] = above / below
    for i in range(8):
        for j in range(4):
            tile_scr[16 * i + 4 * j : 16 * i + 4 * j + 4, :] = att_scr[
                4 * i : 4 * i + 4, 128 * j : 128 * j + 128
            ]
    p3_send[...] = tile_scr[...].astype(BF16).reshape(8, 16, 128)

    each(
        8, lambda i: remote(p3_send.at[i], p3_recv.at[s8], p3_s, p3_r, g_to, c * 8 + i).start()
    )
    pending.append(lambda: landed(p3_recv, p3_s))
    loads[2].wait()
    landed(p3_recv, p3_r)
    tile_scr[...] = p3_recv[...].astype(F32).reshape(128, 128)
    for i in range(8):
        for j in range(4):
            lhs_scr[4 * i : 4 * i + 4, 128 * j : 128 * j + 128] = tile_scr[
                16 * i + 4 * j : 16 * i + 4 * j + 4, :
            ]
    values = dot(lhs_scr[...].astype(BF16), wuv_vm[0]).astype(BF16)
    p4_send[...] = values

    home = (c // 2 + 2) % N_Y
    mine = home == y
    slot4 = y * 2 + c % 2

    def p4_copy(i):
        return remote(p4_send, p4_recv.at[slot4], p4_s.at[i], p4_r.at[slot4], i, home * N_Z + z)

    def p4_arrival(i):
        return remote(
            p4_send,
            p4_recv.at[i],
            p4_s.at[i],
            p4_r.at[i],
            (y + 2) % N_Y * 2 + i % 2,
            i // 2 * N_Z + z,
        )

    def p4_sends(step):
        def one(i):
            @pl.when(jnp.logical_not(mine & (i == c)))
            def _():
                step(i)

        each(8, one)

    def p4_arrives(step):
        def one(i):
            @pl.when(jnp.logical_not(mine & (i == slot4)))
            def _():
                step(i)

        each(8, one)

    p4_sends(lambda i: p4_copy(i).start())
    pending.append(lambda: p4_sends(lambda i: p4_copy(i).wait_send()))

    @pl.when(mine)
    def _():
        p4_recv[slot4] = p4_send[...]

    landed(info_recv.at[1:N_Z], info_r)
    for k in range(8):
        col_scr[16 * k : 16 * k + 16, :] = info_recv[:, k, :]
    pick_col = col_scr[:, 0:1].astype(jnp.int32)
    weight_col = col_scr[:, 64:65]
    source = iota((128, 1), 0) % 16
    target = source * 32 + pick_col
    lane = iota((128, 512), 1)
    for j in range(8):
        sel_scr[128 * j : 128 * j + 128, :] = jnp.where(lane == target + 4 * j, 1.0, 0.0).astype(BF16)
    spread = jnp.where(iota((128, 128), 1) == source * 4 + pick_col, weight_col, 0.0)
    comb = jnp.transpose(spread)[0:64, :]
    comb_hi = comb.astype(BF16)
    comb_scr[0] = comb_hi
    comb_scr[1] = (comb - comb_hi.astype(F32)).astype(BF16)

    loads[3].wait()
    for k in y_order:
        wo_arrival(k).wait_recv()
    p4_arrives(lambda i: p4_arrival(i).wait_recv())
    lhs = jnp.concatenate(
        [p4_recv[2 * k : 2 * k + 2].reshape(64, 128) for k in range(N_Y)], axis=1
    )

    def to_tiles(values32, send):
        wide_scr[...] = values32
        for zz in range(N_Z):
            for j in range(NJ):
                z_scr[32 * zz + 4 * j : 32 * zz + 4 * j + 4, :] = wide_scr[
                    4 * zz : 4 * zz + 4, 128 * j : 128 * j + 128
                ]
        send[...] = z_scr[...].astype(BF16).reshape(N_Z, 32, 128)

    def z_scatter(send, own, index, recv, ssem, rsem):
        def copy(i):
            step = z_step(i)
            remote(
                send.at[index(step)],
                recv.at[step - 1],
                ssem,
                rsem,
                c,
                y * N_Z + (z + step) % N_Z,
            ).start()

        each(N_Z - 1, copy)
        pending.append(lambda: landed(recv, ssem))
        total = z_scr[pl.ds(pl.multiple_of(own * 32, 32), 32), :]
        landed(recv, rsem)
        for i in range(N_Z - 1):
            total = total + recv[i].astype(F32)
        return total

    to_tiles(dot(lhs, wout_vm[...].reshape(512, COLS)), p5_send)
    attention = z_scatter(p5_send, z, lambda step: (z + step) % N_Z, p5_recv, p5_s, p5_r)
    residual = hid_scr[...] + attention
    res_scr[...] = residual
    small_scr[...] = residual * residual
    squares = small_scr[0:4, :]
    for j in range(1, NJ):
        squares = squares + small_scr[4 * j : 4 * j + 4, :]
    squares = jnp.sum(squares, axis=1, keepdims=True)
    small_scr[...] = residual * gain_scr[...]
    small_scr[28:32, :] = three_parts(squares, (4, 128))
    scaled = small_scr[...].astype(BF16)
    p6_send[...] = scaled
    p6_recv[0] = scaled

    def p6_copy(i):
        step = z_step(i)
        remote(
            p6_send, p6_recv.at[step], p6_s, p6_r, c, y * N_Z + (z + step) % N_Z
        ).start()

    each(N_Z - 1, p6_copy)
    pending.append(lambda: landed(p6_recv.at[1:N_Z], p6_s))
    small_scr[...] = attention
    for j in range(NJ):
        attn_out[:, 128 * j : 128 * j + 128] = small_scr[4 * j : 4 * j + 4, :].astype(BF16)
    landed(p6_recv.at[1:N_Z], p6_r)

    picked = dot(sel_scr[...], p6_recv[...].reshape(512, 128)).astype(BF16)
    for j in range(8):
        p6b_send[:, :, 128 * j : 128 * j + 128] = picked[128 * j : 128 * j + 128, :].reshape(
            N_Y, 32, 128
        )

    def y_copy(send, recv, ssem, rsem, sign):
        for k in y_order:
            remote(
                send.at[k], recv.at[k], ssem, rsem, c, (y + N_Y + sign * k) % N_Y * N_Z + z
            ).start()
        pending.append(lambda: landed(recv.at[1:N_Y], ssem))
        recv[0] = send[0]
        landed(recv.at[1:N_Y], rsem)

    y_copy(p6b_send, xe, p6b_s, p6b_r, 1)

    rows = xe[...].reshape(128, 1024)
    loads[4].wait()
    loads[5].wait()
    p7_send[:, :, :HALF] = dot(rows[:, :COLS], gate_vm[...]).astype(BF16).reshape(N_CTX, 16, HALF)
    p7_send[:, :, HALF : 2 * HALF] = (
        dot(rows[:, :COLS], up_vm[...]).astype(BF16).reshape(N_CTX, 16, HALF)
    )
    p7_send[:, :, 2 * HALF :] = rows[:, COLS:].reshape(N_CTX, 16, 128)

    ctx_scatter(p7_send, p7_recv, p7_s, p7_r)
    landed(p7_recv, p7_r)
    sums = p7_send[c].astype(F32)
    for i in range(N_CTX - 1):
        sums = sums + p7_recv[i].astype(F32)
    mean = jnp.sum(sums[:, 2 * HALF :], axis=1, keepdims=True) / D
    scale = lax.rsqrt(mean + epsilon)
    gate = sums[:, :HALF] * scale
    up = sums[:, HALF : 2 * HALF] * scale
    middle = (gate / (1.0 + jnp.exp(-gate)) * up).astype(BF16)
    p8_send[...] = middle
    mid_all[c] = middle

    for k in ctx_order:
        remote(
            p8_send, mid_all.at[c], p8_s.at[k - 1], p8_r.at[k - 1], ctx_step(k), ep
        ).start()
    for k in ctx_order:
        pending.append(
            remote(
                p8_send, mid_all.at[c], p8_s.at[k - 1], p8_r.at[k - 1], ctx_step(k), ep
            ).wait_send
        )
    loads[6].wait()
    for k in ctx_order:
        frm = ctx_back(k)
        remote(p8_send, mid_all.at[frm], p8_s.at[k - 1], p8_r.at[k - 1], frm, ep).wait_recv()

    produced = dot(mid_all[...].reshape(128, HALF), down_vm[...])
    p9_send[...] = produced.astype(BF16).reshape(N_Y, 32, COLS)
    y_copy(p9_send, p9_recv, p9_s, p9_r, -1)
    back = p9_recv[...].reshape(128, COLS)
    to_tiles(dot(comb_scr[0], back) + dot(comb_scr[1], back), p10_send)
    routed = z_scatter(p10_send, 0, lambda step: N_Z - step, p10_recv, p10_s, p10_r)
    small_scr[...] = res_scr[...] + routed
    for j in range(NJ):
        layer_out[:, 128 * j : 128 * j + 128] = small_scr[4 * j : 4 * j + 4, :].astype(BF16)

    finish()


def per_device(
    queries,
    new_key,
    latent_cache,
    page_table,
    lengths,
    hidden_in,
    w_uv,
    w_out,
    norm_gain,
    routes,
    route_weight,
    w_gate,
    w_up,
    w_down,
):
    vmem = pl.BlockSpec(memory_space=pltpu.VMEM)
    in_hbm = pl.BlockSpec(memory_space=pltpu.HBM)
    dma = pltpu.SemaphoreType.DMA
    scratch = [
        pltpu.SMEM((4, 1, 4), jnp.int32),
        pltpu.SMEM((4,), jnp.int32),
        pltpu.SMEM((4, TOP), jnp.int32),
        pltpu.SMEM((4, TOP), F32),
        pltpu.VMEM((4, KDIM), BF16),
        pltpu.VMEM((4, COLS), BF16),
        pltpu.VMEM((COLS,), F32),
        pltpu.VMEM((4, 64, KDIM), BF16),
        pltpu.VMEM((1, 16, 64, KDIM), BF16),
        pltpu.VMEM((1, LAT, 128), BF16),
        pltpu.VMEM((N_Y, 128, COLS), BF16),
        pltpu.VMEM((COLS, HALF), BF16),
        pltpu.VMEM((COLS, HALF), BF16),
        pltpu.VMEM((HALF, COLS), BF16),
        pltpu.VMEM((128, KDIM), BF16),
        pltpu.VMEM((32, LAT), F32),
        pltpu.VMEM((128, 128), F32),
        pltpu.VMEM((32, LAT), F32),
        pltpu.VMEM((64, COLS), F32),
        pltpu.VMEM((512, 128), F32),
        pltpu.VMEM((32, 128), F32),
        pltpu.VMEM((32, 128), F32),
        pltpu.VMEM((32, 128), F32),
        pltpu.VMEM((32, 128), F32),
        pltpu.VMEM((128, 128), F32),
        pltpu.VMEM((1024, 512), BF16),
        pltpu.VMEM((2, 64, 128), BF16),
        pltpu.VMEM((4, 8, 128), F32),
        pltpu.VMEM((N_Z, 8, 128), F32),
        pltpu.VMEM((N_CTX, 32, 640), BF16),
        pltpu.VMEM((N_CTX - 1, 32, 640), BF16),
        pltpu.VMEM((8, 16, 128), BF16),
        pltpu.VMEM((8, 16, 128), BF16),
        pltpu.VMEM((32, 128), BF16),
        pltpu.VMEM((8, 32, 128), BF16),
        pltpu.VMEM((N_Z, 32, 128), BF16),
        pltpu.VMEM((N_Z - 1, 32, 128), BF16),
        pltpu.VMEM((32, 128), BF16),
        pltpu.VMEM((N_Z, 32, 128), BF16),
        pltpu.VMEM((N_Y, 32, 1024), BF16),
        pltpu.VMEM((N_Y, 32, 1024), BF16),
        pltpu.VMEM((N_CTX, 16, 1152), BF16),
        pltpu.VMEM((N_CTX - 1, 16, 1152), BF16),
        pltpu.VMEM((16, HALF), BF16),
        pltpu.VMEM((N_CTX, 16, HALF), BF16),
        pltpu.VMEM((N_Y, 32, COLS), BF16),
        pltpu.VMEM((N_Y, 32, COLS), BF16),
        pltpu.VMEM((N_Z, 32, 128), BF16),
        pltpu.VMEM((N_Z - 1, 32, 128), BF16),
        dma((14,)),
    ]
    for count in (3, 0, 0, 0, 8, 0, 0, 0, 0, 7, 0, 0):
        scratch += [dma((count,)), dma((count,))] if count else [dma, dma]
    out = jax.ShapeDtypeStruct((4, COLS), BF16)
    return pl.pallas_call(
        kernel,
        out_shape=(out, out),
        in_specs=[in_hbm] * 14,
        out_specs=(vmem, vmem),
        scratch_shapes=scratch,
        compiler_params=pltpu.CompilerParams(
            collective_id=0, has_side_effects=True, vmem_limit_bytes=60 * 1024 * 1024
        ),
    )(
        page_table,
        lengths,
        routes,
        route_weight,
        new_key,
        hidden_in,
        norm_gain,
        queries,
        latent_cache,
        w_uv,
        w_out,
        w_gate,
        w_up,
        w_down,
    )


def solution(mesh):
    placed = (
        P("ep", None, None),
        P("ep", None),
        P("ctx", "ep", None, None),
        P("ep", "ctx", None),
        P("ep"),
        P("ep", "ctx"),
        P("ep", None, None),
        P("ep", "ctx"),
        P("ctx"),
        P("ep", None),
        P("ep", None),
        P("ctx", "ep"),
        P("ctx", "ep"),
        P("ep", "ctx"),
    )
    return jax.shard_map(
        per_device,
        mesh=mesh,
        in_specs=placed,
        out_specs=(P("ep", "ctx"), P("ep", "ctx")),
        check_vma=False,
    )
```

```python
import jax
import jax.numpy as jnp
from jax import lax
from jax.experimental import pallas as pl
from jax.experimental.pallas import tpu as pltpu
from jax.sharding import PartitionSpec as P

D = 7168
LAT = 512
KDIM = 576
TOP = 8
N_CTX = 8
N_Y = 4
N_Z = 16
COLS = 896
NJ = 7
HALF = 512

score_scale = 192.0 ** (-0.5)
epsilon = 1e-06
very_low = -1e30

MESH = pl.DeviceIdType.MESH
F32 = jnp.float32
BF16 = jnp.bfloat16


def dot(a, b):
    return jnp.dot(a, b, preferred_element_type=F32)


def dot_nt(a, b):
    return lax.dot_general(a, b, (((1,), (1,)), ((), ())), preferred_element_type=F32)


def iota(shape, dim):
    return lax.broadcasted_iota(jnp.int32, shape, dim)


def three_parts(x, shape):
    hi = x.astype(BF16).astype(F32)
    mid = (x - hi).astype(BF16).astype(F32)
    low = x - hi - mid
    lane = iota(shape, 1)
    zero = jnp.zeros(shape, F32)
    return jnp.where(lane == 0, hi, jnp.where(lane == 1, mid, jnp.where(lane == 2, low, zero)))


def kernel(
    page_table_in,
    lengths_in,
    routes_in,
    route_weight_in,
    new_key_in,
    hidden_in,
    gain_in,
    queries,
    cache,
    w_uv,
    w_out,
    w_gate,
    w_up,
    w_down,
    out,
    page_table,
    lengths,
    routes,
    route_weight,
    new_key,
    hidden,
    gain,
    q_vm,
    cache_vm,
    wuv_vm,
    wout_vm,
    gate_vm,
    up_vm,
    down_vm,
    nk_scr,
    att_scr,
    tile_scr,
    lhs_scr,
    wide_scr,
    z_scr,
    small_scr,
    hid_scr,
    gain_scr,
    res_scr,
    col_scr,
    sel_scr,
    comb_scr,
    info_send,
    info_recv,
    p2_send,
    p2_recv,
    p3_send,
    p3_recv,
    p4_send,
    p4_recv,
    p5_send,
    p5_recv,
    p6_send,
    p6_recv,
    p6b_send,
    xe,
    p7_send,
    p7_recv,
    p8_send,
    mid_all,
    p9_send,
    p9_recv,
    p10_send,
    p10_recv,
    lsem,
    wo_s,
    wo_r,
    info_s,
    info_r,
    p2_s,
    p2_r,
    p3_s,
    p3_r,
    p4_s,
    p4_r,
    p5_s,
    p5_r,
    p6_s,
    p6_r,
    p6f_s,
    p6f_r,
    p6b_s,
    p6b_r,
    p7_s,
    p7_r,
    p8_s,
    p8_r,
    p9_s,
    p9_r,
    p10_s,
    p10_r,
):
    c = lax.axis_index("ctx")
    ep = lax.axis_index("ep")
    y = ep // N_Z
    z = ep % N_Z
    g = ep // 8
    s8 = ep % 8
    x = c // 2
    core = c % 2

    def remote(src, dst, ssem, rsem, to_ctx, to_ep):
        return pltpu.make_async_remote_copy(
            src_ref=src,
            dst_ref=dst,
            send_sem=ssem,
            recv_sem=rsem,
            device_id={"ctx": to_ctx, "ep": to_ep},
            device_id_type=MESH,
        )

    def each(count, step):
        def body(i, carry):
            step(i)
            return carry

        lax.fori_loop(0, count, body, 0)

    loads = [
        pltpu.make_async_copy(src, dst, lsem.at[i])
        for i, (src, dst) in enumerate(
            [
                (queries, q_vm),
                (cache, cache_vm),
                (w_uv, wuv_vm),
                (w_out, wout_vm.at[y]),
                (w_gate, gate_vm),
                (w_up, up_vm),
                (w_down, down_vm),
                (page_table_in, page_table),
                (lengths_in, lengths),
                (routes_in, routes),
                (route_weight_in, route_weight),
                (new_key_in, new_key),
                (hidden_in, hidden),
                (gain_in, gain),
            ]
        )
    ]
    for load in loads[:2] + loads[7:] + loads[2:7]:
        load.start()
    pending = []

    def finish():
        for wait in pending:
            wait()

    def landed(buffer, sem):
        pltpu.make_async_copy(buffer, buffer, sem).wait()

    def z_step(i):
        return 8 + (i + 1) // 2 * (1 - 2 * (i % 2))

    def near(i):
        step = z_step(8 + i)
        return step, (step + 3 + step // 8) % N_Z

    def far(i):
        step = z_step(i)
        return step, step + 4

    barrier = pltpu.get_barrier_semaphore()

    def greet(to_ctx, to_ep):
        pl.semaphore_signal(
            barrier, inc=1, device_id={"ctx": to_ctx, "ep": to_ep}, device_id_type=MESH
        )

    def greet_plane(i):
        k = i + 1
        greet((c + k % N_CTX) % N_CTX, (y + k // N_CTX) % N_Y * N_Z + z)

    g_to = (g + 4) % 8
    c_from = (c + 4) % 8
    each(N_Z - 1, lambda i: greet(c, y * N_Z + (z + z_step(i)) % N_Z))
    each(8, lambda i: greet(g_to, c * 8 + i))
    each(8, lambda i: greet(g, c_from * 8 + i))
    each(N_CTX * N_Y - 1, greet_plane)

    for load in loads[7:]:
        load.wait()

    row = iota((32, 128), 0)
    expert = ((row // 2) % 4 + y) % 4 * 4 + row // 8
    place = row % 2
    before = jnp.zeros((32, 128), jnp.int32)
    pick = jnp.zeros((32, 128), F32)
    weight = jnp.zeros((32, 128), F32)
    for r in range(4):
        named = jnp.zeros((32, 128), jnp.int32)
        w_r = jnp.zeros((32, 128), F32)
        for k in range(TOP):
            hit = expert == routes[r, k]
            named = jnp.where(hit, 1, named)
            w_r = jnp.where(hit, route_weight[r, k], w_r)
        taken = (named == 1) & (before == place)
        pick = jnp.where(taken, float(r), pick)
        weight = jnp.where(taken, w_r, weight)
        before = before + named
    info = jnp.where(iota((32, 128), 1) < 64, pick, weight)
    info_send[...] = info.reshape(4, 8, 128)
    info_recv[7] = info_send[z // 4]

    hid_scr[28:32, :] = jnp.zeros((4, 128), F32)
    gain_scr[...] = jnp.zeros((128, 128), F32)
    hid32 = hidden[...].astype(F32)
    for j in range(NJ):
        hid_scr[4 * j : 4 * j + 4, :] = hid32[:, 128 * j : 128 * j + 128]
        gain_scr[j : j + 1, :] = gain[128 * j : 128 * j + 128].reshape(1, 128)
    gain_scr[...] = jnp.transpose(gain_scr[...])
    nk_scr[...] = jnp.zeros((128, KDIM), BF16)
    nk_scr[0:4, :] = new_key[...]
    for zz in range(N_Z):
        z_scr[32 * zz + 28 : 32 * zz + 32, :] = jnp.zeros((4, 128), F32)

    col = iota((1, 1024), 1)
    slot = col // 64
    owner = jnp.full((1, 1024), -1, jnp.int32)
    for r in range(4):
        for p in range(4):
            position = (p * N_CTX + c) * 64 + col % 64
            good = (slot == page_table[r, 0, p]) & (position < lengths[r])
            owner = jnp.where(good, r, owner)
    i0 = iota((256, 256), 0)
    shuffle = jnp.where((i0 % 4) * 64 + i0 // 4 == iota((256, 256), 1), 1.0, 0.0).astype(BF16)
    loads[0].wait()
    q = dot(shuffle, q_vm[...].reshape(256, KDIM)).astype(BF16)
    loads[1].wait()
    keys = cache_vm[...].reshape(1024, KDIM)
    scores = dot_nt(q, keys) * score_scale
    fresh = dot_nt(q, nk_scr[...]) * score_scale
    mask = owner == iota((256, 1024), 0) % 4
    mask_new = iota((256, 128), 1) + 1024 * c == iota((256, 128), 0) % 4
    peak = jnp.maximum(
        jnp.max(jnp.where(mask, scores, very_low), axis=1, keepdims=True),
        jnp.max(jnp.where(mask_new, fresh, very_low), axis=1, keepdims=True),
    )
    weights = jnp.where(mask, jnp.exp(scores - peak), 0.0).astype(BF16)
    weights_new = jnp.where(mask_new, jnp.exp(fresh - peak), 0.0).astype(BF16)
    total = jnp.sum(weights.astype(F32), axis=1, keepdims=True) + jnp.sum(
        weights_new.astype(F32), axis=1, keepdims=True
    )
    mixture = dot(weights, keys[:, :LAT]) + dot(weights_new, nk_scr[:, :LAT])
    some = total > 0.0
    total = jnp.where(some, total, 1.0)
    logsum = jnp.where(some, peak + jnp.log(total), very_low)
    p2_send[:, :, :LAT] = (mixture / total).astype(BF16).reshape(N_CTX, 32, LAT)
    p2_send[:, :, LAT:] = three_parts(logsum, (256, 128)).astype(BF16).reshape(N_CTX, 32, 128)

    pl.semaphore_wait(barrier, N_CTX * N_Y - 1 + N_Z - 1 + 16)

    def ctx_step(k):
        return (c // 2 + k // 2) % 4 * 2 + (c + k) % 2

    def ctx_back(k):
        return (c // 2 + 4 - k // 2) % 4 * 2 + (c + k) % 2

    ctx_order = (4, 5, 2, 3, 6, 7, 1)
    y_order = (2, 1, 3)

    def ctx_scatter(send, recv, ssem, rsem):
        for k in ctx_order:
            to = ctx_step(k)
            remote(send.at[to], recv.at[k - 1], ssem, rsem, to, ep).start()
        pending.append(lambda: landed(recv, ssem))

    ctx_scatter(p2_send, p2_recv, p2_s, p2_r)

    def info_copy(i, place):
        step, position = place(i)
        to = (z + step) % N_Z
        remote(
            info_send.at[to // 4], info_recv.at[position], info_s, info_r, c, y * N_Z + to
        ).start()

    each(8, lambda i: info_copy(i, far))
    each(7, lambda i: info_copy(i, near))
    pending.append(lambda: landed(info_recv.at[1:N_Z], info_s))

    for k in y_order:
        remote(
            w_out, wout_vm.at[y], wo_s.at[k - 1], wo_r.at[k - 1], c, (y + k) % N_Y * N_Z + z
        ).start()
    for k in y_order:
        pending.append(
            remote(
                w_out, wout_vm.at[y], wo_s.at[k - 1], wo_r.at[k - 1], c, (y + k) % N_Y * N_Z + z
            ).wait_send
        )

    def wo_arrival(k):
        frm = (y + N_Y - k) % N_Y
        return remote(w_out, wout_vm.at[frm], wo_s.at[k - 1], wo_r.at[k - 1], c, frm * N_Z + z)

    landed(p2_recv, p2_r)
    parts = [p2_send[c]] + [p2_recv[i] for i in range(N_CTX - 1)]
    logs = [jnp.sum(p[:, LAT:].astype(F32), axis=1, keepdims=True) for p in parts]
    top = logs[0]
    for l in logs[1:]:
        top = jnp.maximum(top, l)
    above = jnp.zeros((32, LAT), F32)
    below = jnp.zeros((32, 1), F32)
    for p, l in zip(parts, logs):
        f = jnp.exp(l - top)
        above = above + f * p[:, :LAT].astype(F32)
        below = below + f
    att_scr[...] = above / below
    for i in range(8):
        for j in range(4):
            tile_scr[16 * i + 4 * j : 16 * i + 4 * j + 4, :] = att_scr[
                4 * i : 4 * i + 4, 128 * j : 128 * j + 128
            ]
    p3_send[...] = tile_scr[...].astype(BF16).reshape(8, 16, 128)

    each(
        8, lambda i: remote(p3_send.at[i], p3_recv.at[s8], p3_s, p3_r, g_to, c * 8 + i).start()
    )
    pending.append(lambda: landed(p3_recv, p3_s))
    loads[4].wait()
    loads[5].wait()
    for j in range(NJ):
        factor = gain_scr[:, j : j + 1]
        for w in (gate_vm, up_vm):
            block = w[128 * j : 128 * j + 128, :].astype(F32)
            w[128 * j : 128 * j + 128, :] = (block * factor).astype(BF16)
    loads[2].wait()
    landed(p3_recv, p3_r)
    tile_scr[...] = p3_recv[...].astype(F32).reshape(128, 128)
    for i in range(8):
        for j in range(4):
            lhs_scr[4 * i : 4 * i + 4, 128 * j : 128 * j + 128] = tile_scr[
                16 * i + 4 * j : 16 * i + 4 * j + 4, :
            ]
    values = dot(lhs_scr[...].astype(BF16), wuv_vm[0]).astype(BF16)
    p4_send[...] = values

    home = (c // 2 + 2) % N_Y
    mine = home == y
    slot4 = y * 2 + c % 2

    def p4_copy(i):
        return remote(p4_send, p4_recv.at[slot4], p4_s.at[i], p4_r.at[slot4], i, home * N_Z + z)

    def p4_arrival(i):
        return remote(
            p4_send,
            p4_recv.at[i],
            p4_s.at[i],
            p4_r.at[i],
            (y + 2) % N_Y * 2 + i % 2,
            i // 2 * N_Z + z,
        )

    def p4_sends(step):
        def one(i):
            @pl.when(jnp.logical_not(mine & (i == c)))
            def _():
                step(i)

        each(8, one)

    def p4_arrives(step):
        def one(i):
            @pl.when(jnp.logical_not(mine & (i == slot4)))
            def _():
                step(i)

        each(8, one)

    p4_sends(lambda i: p4_copy(i).start())
    pending.append(lambda: p4_sends(lambda i: p4_copy(i).wait_send()))

    @pl.when(mine)
    def _():
        p4_recv[slot4] = p4_send[...]

    landed(info_recv.at[1:N_Z], info_r)
    for part in range(2):
        for k in range(8):
            row0 = 64 * part + 8 * k
            col_scr[row0 : row0 + 8, :] = info_recv[8 * part : 8 * part + 8, k, :]
    pick_col = col_scr[:, 0:1].astype(jnp.int32)
    weight_col = col_scr[:, 64:65]
    source = iota((128, 1), 0) % 8
    target = source * 32 + pick_col
    lane = iota((64, 256), 1)
    spread = jnp.where(iota((128, 128), 1) == source * 4 + pick_col, weight_col, 0.0)
    for part in range(2):
        for j in range(NJ):
            sel_scr[part, 64 * j : 64 * j + 64, :] = jnp.where(
                lane == target[64 * part : 64 * part + 64] + 4 * j, 1.0, 0.0
            ).astype(BF16)
        block = jnp.concatenate(
            [spread[64 * part : 64 * part + 64], jnp.zeros((64, 128), F32)], axis=0
        )
        comb = jnp.transpose(block)[0:32, :]
        comb_hi = comb.astype(BF16)
        comb_scr[part, 0] = comb_hi
        comb_scr[part, 1] = (comb - comb_hi.astype(F32)).astype(BF16)

    loads[3].wait()
    for k in y_order:
        wo_arrival(k).wait_recv()
    p4_arrives(lambda i: p4_arrival(i).wait_recv())
    lhs = jnp.concatenate(
        [p4_recv[2 * k : 2 * k + 2].reshape(64, 128) for k in range(N_Y)], axis=1
    )

    def to_tiles(values32, first, count):
        wide_scr[0 : 4 * count, :] = values32
        for zz in range(count):
            for j in range(NJ):
                row0 = 32 * (first + zz) + 4 * j
                z_scr[row0 : row0 + 4, :] = wide_scr[
                    4 * zz : 4 * zz + 4, 128 * j : 128 * j + 128
                ]
        tiles = z_scr[32 * first : 32 * (first + count), :]
        return tiles.astype(BF16).reshape(count, 32, 128)

    def z_total(own, recv, rsem):
        total = z_scr[pl.ds(pl.multiple_of(own * 32, 32), 32), :]
        landed(recv, rsem)
        for i in range(N_Z - 1):
            total = total + recv[i].astype(F32)
        return total

    p5_send[...] = to_tiles(dot(lhs, wout_vm[...].reshape(512, COLS)), 0, N_Z)

    def p5_copy(i):
        step = z_step(i)
        to = (z + step) % N_Z
        remote(p5_send.at[to], p5_recv.at[step - 1], p5_s, p5_r, c, y * N_Z + to).start()

    each(N_Z - 1, p5_copy)
    pending.append(lambda: landed(p5_recv, p5_s))
    attention = z_total(z, p5_recv, p5_r)
    residual = hid_scr[...] + attention
    rounded = residual.astype(BF16)
    p6_send[...] = rounded
    p6_recv[7] = rounded

    def p6_copy(i, place, ssem, rsem):
        step, position = place(i)
        remote(
            p6_send, p6_recv.at[position], ssem, rsem, c, y * N_Z + (z + step) % N_Z
        ).start()

    each(8, lambda i: p6_copy(i, far, p6f_s, p6f_r))
    each(7, lambda i: p6_copy(i, near, p6_s, p6_r))
    pending.append(lambda: landed(p6_recv.at[0:7], p6_s))
    pending.append(lambda: landed(p6_recv.at[8:16], p6f_s))
    res_scr[...] = residual
    small_scr[...] = attention
    for j in range(NJ):
        out[0:4, 128 * j : 128 * j + 128] = small_scr[4 * j : 4 * j + 4, :].astype(BF16)

    def y_send(send, recv, ssem, rsem, sign):
        for k in y_order:
            remote(
                send.at[k], recv.at[k], ssem, rsem, c, (y + N_Y + sign * k) % N_Y * N_Z + z
            ).start()
        pending.append(lambda: landed(recv.at[1:N_Y], ssem))
        recv[0] = send[0]

    def pick_rows(part):
        arrived = p6_recv[8 * part : 8 * part + 8].reshape(256, 128)
        picked = dot(sel_scr[part], arrived).astype(BF16)
        for j in range(NJ):
            p6b_send[part, :, :, 128 * j : 128 * j + 128] = picked[
                64 * j : 64 * j + 64, :
            ].reshape(N_Y, 16, 128)
        y_send(p6b_send.at[part], xe.at[part], p6b_s.at[part], p6b_r.at[part], 1)

    def gate_up(part):
        landed(xe.at[part].at[1:N_Y], p6b_r.at[part])
        rows = xe[part].reshape(64, COLS)
        rows32 = rows.astype(F32)
        squares = jnp.sum(rows32 * rows32, axis=1, keepdims=True)
        p7_send[part, :, :, 2 * HALF :] = (
            three_parts(squares, (64, 128)).astype(BF16).reshape(N_Y, 16, 128)
        )
        p7_send[part, :, :, :HALF] = dot(rows, gate_vm[...]).astype(BF16).reshape(N_Y, 16, HALF)
        p7_send[part, :, :, HALF : 2 * HALF] = (
            dot(rows, up_vm[...]).astype(BF16).reshape(N_Y, 16, HALF)
        )
        side = (core + part) % 2
        for dx in (2, 1, 3):
            there = (x + dx) % 4
            remote(
                p7_send.at[part, there],
                p7_recv.at[2 * dx + side - 1],
                p7_s.at[part],
                p7_r,
                there * 2 + part,
                ep,
            ).start()

        @pl.when(core != part)
        def _():
            remote(
                p7_send.at[part, x], p7_recv.at[0], p7_s.at[part], p7_r, x * 2 + part, ep
            ).start()

    def gate_up_sent(part):
        landed(p7_recv.at[0:3], p7_s.at[part])

        @pl.when(core != part)
        def _():
            landed(p7_recv.at[0], p7_s.at[part])

    landed(p6_recv.at[0:7], p6_r)
    pick_rows(0)
    landed(p6_recv.at[8:16], p6f_r)
    pick_rows(1)
    gate_up(0)
    gate_up(1)
    pending.append(lambda: gate_up_sent(0))
    pending.append(lambda: gate_up_sent(1))

    landed(p7_recv, p7_r)
    sums = p7_send[core, x].astype(F32)
    for i in range(N_CTX - 1):
        sums = sums + p7_recv[i].astype(F32)
    mean = jnp.sum(sums[:, 2 * HALF :], axis=1, keepdims=True) / D
    scale = lax.rsqrt(mean + epsilon)
    gate = sums[:, :HALF] * scale
    up = sums[:, HALF : 2 * HALF] * scale
    middle = (gate / (1.0 + jnp.exp(-gate)) * up).astype(BF16)
    p8_send[...] = middle
    mid_all[core, x] = middle
    for k in ctx_order:
        remote(
            p8_send, mid_all.at[core, x], p8_s.at[k - 1], p8_r.at[k - 1], ctx_step(k), ep
        ).start()
    for k in ctx_order:
        pending.append(
            remote(
                p8_send, mid_all.at[core, x], p8_s.at[k - 1], p8_r.at[k - 1], ctx_step(k), ep
            ).wait_send
        )
    loads[6].wait()

    def project(part):
        side = (core + part) % 2
        for dx in (1, 3, 2):
            frm = (x + 4 - dx) % 4
            sem = 2 * dx + side - 1
            remote(
                p8_send, mid_all.at[part, frm], p8_s.at[sem], p8_r.at[sem], frm * 2 + part, ep
            ).wait_recv()

        @pl.when(core != part)
        def _():
            remote(
                p8_send, mid_all.at[part, x], p8_s.at[0], p8_r.at[0], x * 2 + part, ep
            ).wait_recv()

        produced = dot(mid_all[part].reshape(64, HALF), down_vm[...])
        p9_send[part] = produced.astype(BF16).reshape(N_Y, 16, COLS)
        y_send(p9_send.at[part], p9_recv.at[part], p9_s.at[part], p9_r.at[part], -1)

    project(0)
    project(1)

    def combine(part, count, place):
        landed(p9_recv.at[part].at[1:N_Y], p9_r.at[part])
        back = p9_recv[part].reshape(64, COLS)
        mixed = dot(comb_scr[part, 0][:, :64], back) + dot(comb_scr[part, 1][:, :64], back)
        p10_send[8 * part : 8 * part + 8] = to_tiles(mixed, 8 * part, 8)

        def copy(i):
            step, position = place(i)
            remote(
                p10_send.at[position],
                p10_recv.at[step - 1],
                p10_s,
                p10_r,
                c,
                y * N_Z + (z + N_Z - step) % N_Z,
            ).start()

        each(count, copy)

    combine(0, 7, near)
    combine(1, 8, far)
    pending.append(lambda: landed(p10_recv, p10_s))
    routed = z_total(7, p10_recv, p10_r)
    small_scr[...] = res_scr[...] + routed
    for j in range(NJ):
        out[4:8, 128 * j : 128 * j + 128] = small_scr[4 * j : 4 * j + 4, :].astype(BF16)

    finish()


def per_device(
    queries,
    new_key,
    latent_cache,
    page_table,
    lengths,
    hidden_in,
    w_uv,
    w_out,
    norm_gain,
    routes,
    route_weight,
    w_gate,
    w_up,
    w_down,
):
    vmem = pl.BlockSpec(memory_space=pltpu.VMEM)
    in_hbm = pl.BlockSpec(memory_space=pltpu.HBM)
    dma = pltpu.SemaphoreType.DMA
    scratch = [
        pltpu.SMEM((4, 1, 4), jnp.int32),
        pltpu.SMEM((4,), jnp.int32),
        pltpu.SMEM((4, TOP), jnp.int32),
        pltpu.SMEM((4, TOP), F32),
        pltpu.VMEM((4, KDIM), BF16),
        pltpu.VMEM((4, COLS), BF16),
        pltpu.VMEM((COLS,), F32),
        pltpu.VMEM((4, 64, KDIM), BF16),
        pltpu.VMEM((1, 16, 64, KDIM), BF16),
        pltpu.VMEM((1, LAT, 128), BF16),
        pltpu.VMEM((N_Y, 128, COLS), BF16),
        pltpu.VMEM((COLS, HALF), BF16),
        pltpu.VMEM((COLS, HALF), BF16),
        pltpu.VMEM((HALF, COLS), BF16),
        pltpu.VMEM((128, KDIM), BF16),
        pltpu.VMEM((32, LAT), F32),
        pltpu.VMEM((128, 128), F32),
        pltpu.VMEM((32, LAT), F32),
        pltpu.VMEM((64, COLS), F32),
        pltpu.VMEM((512, 128), F32),
        pltpu.VMEM((32, 128), F32),
        pltpu.VMEM((32, 128), F32),
        pltpu.VMEM((128, 128), F32),
        pltpu.VMEM((32, 128), F32),
        pltpu.VMEM((128, 128), F32),
        pltpu.VMEM((2, 64 * NJ, 256), BF16),
        pltpu.VMEM((2, 2, 32, 128), BF16),
        pltpu.VMEM((4, 8, 128), F32),
        pltpu.VMEM((N_Z, 8, 128), F32),
        pltpu.VMEM((N_CTX, 32, 640), BF16),
        pltpu.VMEM((N_CTX - 1, 32, 640), BF16),
        pltpu.VMEM((8, 16, 128), BF16),
        pltpu.VMEM((8, 16, 128), BF16),
        pltpu.VMEM((32, 128), BF16),
        pltpu.VMEM((8, 32, 128), BF16),
        pltpu.VMEM((N_Z, 32, 128), BF16),
        pltpu.VMEM((N_Z - 1, 32, 128), BF16),
        pltpu.VMEM((32, 128), BF16),
        pltpu.VMEM((N_Z, 32, 128), BF16),
        pltpu.VMEM((2, N_Y, 16, COLS), BF16),
        pltpu.VMEM((2, N_Y, 16, COLS), BF16),
        pltpu.VMEM((2, 4, 16, 1152), BF16),
        pltpu.VMEM((N_CTX - 1, 16, 1152), BF16),
        pltpu.VMEM((16, HALF), BF16),
        pltpu.VMEM((2, 4, 16, HALF), BF16),
        pltpu.VMEM((2, N_Y, 16, COLS), BF16),
        pltpu.VMEM((2, N_Y, 16, COLS), BF16),
        pltpu.VMEM((N_Z, 32, 128), BF16),
        pltpu.VMEM((N_Z - 1, 32, 128), BF16),
        dma((14,)),
    ]
    for count in (3, 0, 0, 0, 8, 0, 0, 0, 2):
        scratch += [dma((count,)), dma((count,))] if count else [dma, dma]
    scratch += [dma((2,)), dma]
    for count in (7, 2, 0):
        scratch += [dma((count,)), dma((count,))] if count else [dma, dma]
    both = pl.pallas_call(
        kernel,
        out_shape=jax.ShapeDtypeStruct((8, COLS), BF16),
        in_specs=[in_hbm] * 14,
        out_specs=vmem,
        scratch_shapes=scratch,
        compiler_params=pltpu.CompilerParams(
            collective_id=0, has_side_effects=True, vmem_limit_bytes=60 * 1024 * 1024
        ),
    )(
        page_table,
        lengths,
        routes,
        route_weight,
        new_key,
        hidden_in,
        norm_gain,
        queries,
        latent_cache,
        w_uv,
        w_out,
        w_gate,
        w_up,
        w_down,
    )
    return both[:4], both[4:]


def solution(mesh):
    placed = (
        P("ep", None, None),
        P("ep", None),
        P("ctx", "ep", None, None),
        P("ep", "ctx", None),
        P("ep"),
        P("ep", "ctx"),
        P("ep", None, None),
        P("ep", "ctx"),
        P("ctx"),
        P("ep", None),
        P("ep", None),
        P("ctx", "ep"),
        P("ctx", "ep"),
        P("ep", "ctx"),
    )
    return jax.shard_map(
        per_device,
        mesh=mesh,
        in_specs=placed,
        out_specs=(P("ep", "ctx"), P("ep", "ctx")),
        check_vma=False,
    )
```

```python
import jax
import jax.numpy as jnp
from jax import lax
from jax.experimental import pallas as pl
from jax.experimental.pallas import tpu as pltpu
from jax.sharding import PartitionSpec as P

D = 7168
LAT = 512
KDIM = 576
TOP = 8
N_CTX = 8
N_Y = 4
N_Z = 16
COLS = 896
NJ = 7
HALF = 512

score_scale = 192.0 ** (-0.5)
epsilon = 1e-06
very_low = -1e30

MESH = pl.DeviceIdType.MESH
F32 = jnp.float32
BF16 = jnp.bfloat16


def dot(a, b):
    return jnp.dot(a, b, preferred_element_type=F32)


def dot_nt(a, b):
    return lax.dot_general(a, b, (((1,), (1,)), ((), ())), preferred_element_type=F32)


def iota(shape, dim):
    return lax.broadcasted_iota(jnp.int32, shape, dim)


def three_parts(x, shape):
    hi = x.astype(BF16).astype(F32)
    mid = (x - hi).astype(BF16).astype(F32)
    low = x - hi - mid
    lane = iota(shape, 1)
    zero = jnp.zeros(shape, F32)
    return jnp.where(lane == 0, hi, jnp.where(lane == 1, mid, jnp.where(lane == 2, low, zero)))


def kernel(
    page_table_in,
    lengths_in,
    routes_in,
    route_weight_in,
    new_key_in,
    hidden_in,
    gain_in,
    queries,
    cache,
    w_uv,
    w_out,
    w_gate,
    w_up,
    w_down,
    out,
    page_table,
    lengths,
    routes,
    route_weight,
    new_key,
    hidden,
    gain,
    q_vm,
    cache_vm,
    wuv_vm,
    wout_vm,
    gate_vm,
    up_vm,
    down_vm,
    nk_scr,
    att_scr,
    tile_scr,
    lhs_scr,
    wide_scr,
    z_scr,
    small_scr,
    hid_scr,
    gain_scr,
    res_scr,
    col_scr,
    sel_scr,
    comb_scr,
    info_send,
    info_recv,
    p2_send,
    p2_recv,
    p3_send,
    p3_recv,
    p4_send,
    p4_recv,
    p5_send,
    p5_recv,
    p6_send,
    p6_recv,
    p6b_send,
    xe,
    p7_send,
    p7_recv,
    p8_send,
    mid_all,
    p9_send,
    p9_recv,
    p10_send,
    p10_recv,
    lsem,
    uv_s,
    uv_r,
    wo_s,
    wo_r,
    info_s,
    info_r,
    p2_s,
    p2_r,
    p3_s,
    p3_r,
    p4_s,
    p4_r,
    p5_s,
    p5_r,
    p6_s,
    p6_r,
    p6f_s,
    p6f_r,
    p6b_s,
    p6b_r,
    p7_s,
    p7_r,
    p8_s,
    p8_r,
    p9_s,
    p9_r,
    p10_s,
    p10_r,
):
    c = lax.axis_index("ctx")
    ep = lax.axis_index("ep")
    y = ep // N_Z
    z = ep % N_Z
    x = c // 2
    core = c % 2
    has_head = z // 8 == core

    def remote(src, dst, ssem, rsem, to_ctx, to_ep):
        return pltpu.make_async_remote_copy(
            src_ref=src,
            dst_ref=dst,
            send_sem=ssem,
            recv_sem=rsem,
            device_id={"ctx": to_ctx, "ep": to_ep},
            device_id_type=MESH,
        )

    def each(count, step):
        def body(i, carry):
            step(i)
            return carry

        lax.fori_loop(0, count, body, 0)

    loads = [
        pltpu.make_async_copy(src, dst, lsem.at[i])
        for i, (src, dst) in enumerate(
            [
                (queries, q_vm),
                (cache, cache_vm),
                (w_uv, wuv_vm.at[0:1]),
                (w_out, wout_vm.at[y]),
                (w_gate, gate_vm),
                (w_up, up_vm),
                (w_down, down_vm),
                (page_table_in, page_table),
                (lengths_in, lengths),
                (routes_in, routes),
                (route_weight_in, route_weight),
                (new_key_in, new_key),
                (hidden_in, hidden),
                (gain_in, gain),
            ]
        )
    ]
    for load in loads[:2] + loads[7:] + loads[2:7]:
        load.start()
    pending = []

    def finish():
        for wait in pending:
            wait()

    def landed(buffer, sem):
        pltpu.make_async_copy(buffer, buffer, sem).wait()

    def z_step(i):
        return 8 + (i + 1) // 2 * (1 - 2 * (i % 2))

    def near(i):
        step = z_step(8 + i)
        return step, (step + 3 + step // 8) % N_Z

    def far(i):
        step = z_step(i)
        return step, step + 4

    barrier = pltpu.get_barrier_semaphore()

    def greet(to_ctx, to_ep):
        pl.semaphore_signal(
            barrier, inc=1, device_id={"ctx": to_ctx, "ep": to_ep}, device_id_type=MESH
        )

    each(N_Z - 1, lambda i: greet(c, y * N_Z + (z + z_step(i)) % N_Z))
    each(N_Y - 1, lambda i: greet(c, (y + i + 1) % N_Y * N_Z + z))
    each(N_CTX - 1, lambda i: greet((c + i + 1) % N_CTX, ep))

    for load in loads[7:]:
        load.wait()

    row = iota((32, 128), 0)
    expert = ((row // 2) % 4 + y) % 4 * 4 + row // 8
    place = row % 2
    before = jnp.zeros((32, 128), jnp.int32)
    pick = jnp.zeros((32, 128), F32)
    weight = jnp.zeros((32, 128), F32)
    for r in range(4):
        named = jnp.zeros((32, 128), jnp.int32)
        w_r = jnp.zeros((32, 128), F32)
        for k in range(TOP):
            hit = expert == routes[r, k]
            named = jnp.where(hit, 1, named)
            w_r = jnp.where(hit, route_weight[r, k], w_r)
        taken = (named == 1) & (before == place)
        pick = jnp.where(taken, float(r), pick)
        weight = jnp.where(taken, w_r, weight)
        before = before + named
    info = jnp.where(iota((32, 128), 1) < 64, pick, weight)
    info_send[...] = info.reshape(4, 8, 128)
    info_recv[7] = info_send[z // 4]

    hid_scr[28:32, :] = jnp.zeros((4, 128), F32)
    gain_scr[...] = jnp.zeros((128, 128), F32)
    hid32 = hidden[...].astype(F32)
    for j in range(NJ):
        hid_scr[4 * j : 4 * j + 4, :] = hid32[:, 128 * j : 128 * j + 128]
        gain_scr[j : j + 1, :] = gain[128 * j : 128 * j + 128].reshape(1, 128)
    gain_scr[...] = jnp.transpose(gain_scr[...])
    nk_scr[...] = jnp.zeros((128, KDIM), BF16)
    nk_scr[0:4, :] = new_key[...]
    for zz in range(N_Z):
        z_scr[32 * zz + 28 : 32 * zz + 32, :] = jnp.zeros((4, 128), F32)

    col = iota((1, 1024), 1)
    slot = col // 64
    owner = jnp.full((1, 1024), -1, jnp.int32)
    for r in range(4):
        for p in range(4):
            position = (p * N_CTX + c) * 64 + col % 64
            good = (slot == page_table[r, 0, p]) & (position < lengths[r])
            owner = jnp.where(good, r, owner)
    i0 = iota((256, 256), 0)
    shuffle = jnp.where((i0 % 4) * 64 + i0 // 4 == iota((256, 256), 1), 1.0, 0.0).astype(BF16)
    loads[0].wait()
    q = dot(shuffle, q_vm[...].reshape(256, KDIM)).astype(BF16)
    loads[1].wait()
    keys = cache_vm[...].reshape(1024, KDIM)
    scores = dot_nt(q, keys) * score_scale
    fresh = dot_nt(q, nk_scr[...]) * score_scale
    mask = owner == iota((256, 1024), 0) % 4
    mask_new = iota((256, 128), 1) + 1024 * c == iota((256, 128), 0) % 4
    peak = jnp.maximum(
        jnp.max(jnp.where(mask, scores, very_low), axis=1, keepdims=True),
        jnp.max(jnp.where(mask_new, fresh, very_low), axis=1, keepdims=True),
    )
    weights = jnp.where(mask, jnp.exp(scores - peak), 0.0).astype(BF16)
    weights_new = jnp.where(mask_new, jnp.exp(fresh - peak), 0.0).astype(BF16)
    total = jnp.sum(weights.astype(F32), axis=1, keepdims=True) + jnp.sum(
        weights_new.astype(F32), axis=1, keepdims=True
    )
    mixture = dot(weights, keys[:, :LAT]) + dot(weights_new, nk_scr[:, :LAT])
    some = total > 0.0
    total = jnp.where(some, total, 1.0)
    logsum = jnp.where(some, peak + jnp.log(total), very_low)
    p2_send[:, :, :LAT] = (mixture / total).astype(BF16).reshape(N_CTX, 32, LAT)
    p2_send[:, :, LAT:] = three_parts(logsum, (256, 128)).astype(BF16).reshape(N_CTX, 32, 128)

    pl.semaphore_wait(barrier, N_Z - 1 + N_Y - 1 + N_CTX - 1)

    def ctx_step(k):
        return (c // 2 + k // 2) % 4 * 2 + (c + k) % 2

    def ctx_back(k):
        return (c // 2 + 4 - k // 2) % 4 * 2 + (c + k) % 2

    ctx_order = (4, 5, 2, 3, 6, 7, 1)
    y_order = (2, 1, 3)

    def ctx_scatter(send, recv, ssem, rsem):
        for k in ctx_order:
            to = ctx_step(k)
            remote(send.at[to], recv.at[k - 1], ssem, rsem, to, ep).start()
        pending.append(lambda: landed(recv, ssem))

    ctx_scatter(p2_send, p2_recv, p2_s, p2_r)

    def info_copy(i, place):
        step, position = place(i)
        to = (z + step) % N_Z
        remote(
            info_send.at[to // 4], info_recv.at[position], info_s, info_r, c, y * N_Z + to
        ).start()

    each(8, lambda i: info_copy(i, far))
    each(7, lambda i: info_copy(i, near))
    pending.append(lambda: landed(info_recv.at[1:N_Z], info_s))

    def uv_copy(k):
        return remote(
            w_uv,
            wuv_vm.at[1:2],
            uv_s.at[k - 1],
            uv_r,
            c,
            (y + k) % N_Y * N_Z + z,
        )

    @pl.when(has_head & (y == x))
    def _():
        for k in y_order:
            uv_copy(k).start()

    def uv_sent():
        @pl.when(has_head & (y == x))
        def _():
            for k in y_order:
                uv_copy(k).wait_send()

    pending.append(uv_sent)

    for k in y_order:
        remote(
            w_out, wout_vm.at[y], wo_s.at[k - 1], wo_r.at[k - 1], c, (y + k) % N_Y * N_Z + z
        ).start()
    for k in y_order:
        pending.append(
            remote(
                w_out, wout_vm.at[y], wo_s.at[k - 1], wo_r.at[k - 1], c, (y + k) % N_Y * N_Z + z
            ).wait_send
        )

    def wo_arrival(k):
        frm = (y + N_Y - k) % N_Y
        return remote(w_out, wout_vm.at[frm], wo_s.at[k - 1], wo_r.at[k - 1], c, frm * N_Z + z)

    landed(p2_recv, p2_r)
    parts = [p2_send[c]] + [p2_recv[i] for i in range(N_CTX - 1)]
    logs = [jnp.sum(p[:, LAT:].astype(F32), axis=1, keepdims=True) for p in parts]
    top = logs[0]
    for l in logs[1:]:
        top = jnp.maximum(top, l)
    above = jnp.zeros((32, LAT), F32)
    below = jnp.zeros((32, 1), F32)
    for p, l in zip(parts, logs):
        f = jnp.exp(l - top)
        above = above + f * p[:, :LAT].astype(F32)
        below = below + f
    att_scr[...] = above / below
    for i in range(8):
        for j in range(4):
            tile_scr[16 * i + 4 * j : 16 * i + 4 * j + 4, :] = att_scr[
                4 * i : 4 * i + 4, 128 * j : 128 * j + 128
            ]
    p3_send[...] = tile_scr[0:128, :].astype(BF16).reshape(8, 16, 128)

    def p3_each(step):
        def one(i):
            @pl.when(z != 8 * core + i)
            def _():
                step(i)

        each(8, one)

    p3_each(
        lambda i: remote(
            p3_send.at[i], p3_recv.at[z], p3_s, p3_r, c, y * N_Z + 8 * core + i
        ).start()
    )

    def p3_sent():
        @pl.when(has_head)
        def _():
            landed(p3_send.at[0:7], p3_s)

        @pl.when(jnp.logical_not(has_head))
        def _():
            landed(p3_send, p3_s)

    pending.append(p3_sent)
    loads[4].wait()
    loads[5].wait()
    for j in range(NJ):
        factor = gain_scr[:, j : j + 1]
        for w in (gate_vm, up_vm):
            block = w[128 * j : 128 * j + 128, :].astype(F32)
            w[128 * j : 128 * j + 128, :] = (block * factor).astype(BF16)
    loads[2].wait()

    def p4_copy(k):
        return remote(p4_send, p4_recv.at[x], p4_s.at[k - 1], p4_r, ctx_step(k), ep)

    @pl.when(has_head)
    def _():
        p3_recv[z] = p3_send[z % 8]
        landed(p3_recv.at[1:N_Z], p3_r)

        @pl.when(y != x)
        def _():
            remote(w_uv, wuv_vm.at[1:2], uv_s.at[0], uv_r, c, x * N_Z + z).wait_recv()

        tile_scr[...] = p3_recv[...].astype(F32).reshape(256, 128)
        for i in range(N_Z):
            for j in range(4):
                lhs_scr[4 * i : 4 * i + 4, 128 * j : 128 * j + 128] = tile_scr[
                    16 * i + 4 * j : 16 * i + 4 * j + 4, :
                ]
        which = jnp.where(y == x, 0, 1).astype(jnp.int32)
        values = dot(lhs_scr[...].astype(BF16), wuv_vm[which]).astype(BF16)
        p4_send[...] = values
        p4_recv[x] = values

        for k in ctx_order:
            p4_copy(k).start()

    def p4_sent():
        @pl.when(has_head)
        def _():
            for k in ctx_order:
                p4_copy(k).wait_send()

    pending.append(p4_sent)

    landed(info_recv.at[1:N_Z], info_r)
    for part in range(2):
        for k in range(8):
            row0 = 64 * part + 8 * k
            col_scr[row0 : row0 + 8, :] = info_recv[8 * part : 8 * part + 8, k, :]
    pick_col = col_scr[:, 0:1].astype(jnp.int32)
    weight_col = col_scr[:, 64:65]
    source = iota((128, 1), 0) % 8
    target = source * 32 + pick_col
    lane = iota((64, 256), 1)
    spread = jnp.where(iota((128, 128), 1) == source * 4 + pick_col, weight_col, 0.0)
    for part in range(2):
        for j in range(NJ):
            sel_scr[part, 64 * j : 64 * j + 64, :] = jnp.where(
                lane == target[64 * part : 64 * part + 64] + 4 * j, 1.0, 0.0
            ).astype(BF16)
        block = jnp.concatenate(
            [spread[64 * part : 64 * part + 64], jnp.zeros((64, 128), F32)], axis=0
        )
        comb = jnp.transpose(block)[0:32, :]
        comb_hi = comb.astype(BF16)
        comb_scr[part, 0] = comb_hi
        comb_scr[part, 1] = (comb - comb_hi.astype(F32)).astype(BF16)

    loads[3].wait()
    for k in y_order:
        wo_arrival(k).wait_recv()
    @pl.when(has_head)
    def _():
        landed(p4_recv.at[0:3], p4_r)

    @pl.when(jnp.logical_not(has_head))
    def _():
        landed(p4_recv, p4_r)

    lhs = jnp.concatenate([p4_recv[k] for k in range(N_Y)], axis=1)

    def to_tiles(values32, first, count):
        wide_scr[0 : 4 * count, :] = values32
        for zz in range(count):
            for j in range(NJ):
                row0 = 32 * (first + zz) + 4 * j
                z_scr[row0 : row0 + 4, :] = wide_scr[
                    4 * zz : 4 * zz + 4, 128 * j : 128 * j + 128
                ]
        tiles = z_scr[32 * first : 32 * (first + count), :]
        return tiles.astype(BF16).reshape(count, 32, 128)

    def z_total(own, recv, rsem):
        total = z_scr[pl.ds(pl.multiple_of(own * 32, 32), 32), :]
        landed(recv, rsem)
        for i in range(N_Z - 1):
            total = total + recv[i].astype(F32)
        return total

    p5_send[...] = to_tiles(dot(lhs, wout_vm[...].reshape(512, COLS)), 0, N_Z)

    def p5_copy(i):
        step = z_step(i)
        to = (z + step) % N_Z
        remote(p5_send.at[to], p5_recv.at[step - 1], p5_s, p5_r, c, y * N_Z + to).start()

    each(N_Z - 1, p5_copy)
    pending.append(lambda: landed(p5_recv, p5_s))
    attention = z_total(z, p5_recv, p5_r)
    residual = hid_scr[...] + attention
    rounded = residual.astype(BF16)
    p6_send[...] = rounded
    p6_recv[7] = rounded

    def p6_copy(i, place, ssem, rsem):
        step, position = place(i)
        remote(
            p6_send, p6_recv.at[position], ssem, rsem, c, y * N_Z + (z + step) % N_Z
        ).start()

    each(7, lambda i: p6_copy(i, near, p6_s, p6_r))
    each(8, lambda i: p6_copy(i, far, p6f_s, p6f_r))
    pending.append(lambda: landed(p6_recv.at[0:7], p6_s))
    pending.append(lambda: landed(p6_recv.at[8:16], p6f_s))
    res_scr[...] = residual
    small_scr[...] = attention
    for j in range(NJ):
        out[0:4, 128 * j : 128 * j + 128] = small_scr[4 * j : 4 * j + 4, :].astype(BF16)

    def y_send(send, recv, ssem, rsem, sign):
        for k in y_order:
            remote(
                send.at[k], recv.at[k], ssem, rsem, c, (y + N_Y + sign * k) % N_Y * N_Z + z
            ).start()
        pending.append(lambda: landed(recv.at[1:N_Y], ssem))
        recv[0] = send[0]

    def pick_rows(part):
        arrived = p6_recv[8 * part : 8 * part + 8].reshape(256, 128)
        picked = dot(sel_scr[part], arrived).astype(BF16)
        for j in range(NJ):
            p6b_send[part, :, :, 128 * j : 128 * j + 128] = picked[
                64 * j : 64 * j + 64, :
            ].reshape(N_Y, 16, 128)
        y_send(p6b_send.at[part], xe.at[part], p6b_s.at[part], p6b_r.at[part], 1)

    def gate_up(part):
        landed(xe.at[part].at[1:N_Y], p6b_r.at[part])
        rows = xe[part].reshape(64, COLS)
        rows32 = rows.astype(F32)
        squares = jnp.sum(rows32 * rows32, axis=1, keepdims=True)
        p7_send[part, :, :, 2 * HALF :] = (
            three_parts(squares, (64, 128)).astype(BF16).reshape(N_Y, 16, 128)
        )
        p7_send[part, :, :, :HALF] = dot(rows, gate_vm[...]).astype(BF16).reshape(N_Y, 16, HALF)
        p7_send[part, :, :, HALF : 2 * HALF] = (
            dot(rows, up_vm[...]).astype(BF16).reshape(N_Y, 16, HALF)
        )
        side = (core + part) % 2
        for dx in (2, 1, 3):
            there = (x + dx) % 4
            remote(
                p7_send.at[part, there],
                p7_recv.at[2 * dx + side - 1],
                p7_s.at[part],
                p7_r,
                there * 2 + part,
                ep,
            ).start()

        @pl.when(core != part)
        def _():
            remote(
                p7_send.at[part, x], p7_recv.at[0], p7_s.at[part], p7_r, x * 2 + part, ep
            ).start()

    def gate_up_sent(part):
        landed(p7_recv.at[0:3], p7_s.at[part])

        @pl.when(core != part)
        def _():
            landed(p7_recv.at[0], p7_s.at[part])

    landed(p6_recv.at[0:7], p6_r)
    pick_rows(0)
    landed(p6_recv.at[8:16], p6f_r)
    pick_rows(1)
    gate_up(0)
    gate_up(1)
    pending.append(lambda: gate_up_sent(0))
    pending.append(lambda: gate_up_sent(1))

    landed(p7_recv, p7_r)
    sums = p7_send[core, x].astype(F32)
    for i in range(N_CTX - 1):
        sums = sums + p7_recv[i].astype(F32)
    mean = jnp.sum(sums[:, 2 * HALF :], axis=1, keepdims=True) / D
    scale = lax.rsqrt(mean + epsilon)
    gate = sums[:, :HALF] * scale
    up = sums[:, HALF : 2 * HALF] * scale
    middle = (gate / (1.0 + jnp.exp(-gate)) * up).astype(BF16)
    p8_send[...] = middle
    mid_all[core, x] = middle
    for k in ctx_order:
        remote(
            p8_send, mid_all.at[core, x], p8_s.at[k - 1], p8_r.at[k - 1], ctx_step(k), ep
        ).start()
    for k in ctx_order:
        pending.append(
            remote(
                p8_send, mid_all.at[core, x], p8_s.at[k - 1], p8_r.at[k - 1], ctx_step(k), ep
            ).wait_send
        )
    loads[6].wait()

    def project(part):
        side = (core + part) % 2
        for dx in (1, 3, 2):
            frm = (x + 4 - dx) % 4
            sem = 2 * dx + side - 1
            remote(
                p8_send, mid_all.at[part, frm], p8_s.at[sem], p8_r.at[sem], frm * 2 + part, ep
            ).wait_recv()

        @pl.when(core != part)
        def _():
            remote(
                p8_send, mid_all.at[part, x], p8_s.at[0], p8_r.at[0], x * 2 + part, ep
            ).wait_recv()

        produced = dot(mid_all[part].reshape(64, HALF), down_vm[...])
        p9_send[part] = produced.astype(BF16).reshape(N_Y, 16, COLS)
        y_send(p9_send.at[part], p9_recv.at[part], p9_s.at[part], p9_r.at[part], -1)

    project(1)
    project(0)

    def combine(part, count, place):
        landed(p9_recv.at[part].at[1:N_Y], p9_r.at[part])
        back = p9_recv[part].reshape(64, COLS)
        mixed = dot(comb_scr[part, 0][:, :64], back) + dot(comb_scr[part, 1][:, :64], back)
        p10_send[8 * part : 8 * part + 8] = to_tiles(mixed, 8 * part, 8)

        def copy(i):
            step, position = place(i)
            remote(
                p10_send.at[position],
                p10_recv.at[step - 1],
                p10_s,
                p10_r,
                c,
                y * N_Z + (z + N_Z - step) % N_Z,
            ).start()

        each(count, copy)

    combine(1, 8, far)
    combine(0, 7, near)
    pending.append(lambda: landed(p10_recv, p10_s))
    routed = z_total(7, p10_recv, p10_r)
    small_scr[...] = res_scr[...] + routed
    for j in range(NJ):
        out[4:8, 128 * j : 128 * j + 128] = small_scr[4 * j : 4 * j + 4, :].astype(BF16)

    finish()


def per_device(
    queries,
    new_key,
    latent_cache,
    page_table,
    lengths,
    hidden_in,
    w_uv,
    w_out,
    norm_gain,
    routes,
    route_weight,
    w_gate,
    w_up,
    w_down,
):
    vmem = pl.BlockSpec(memory_space=pltpu.VMEM)
    in_hbm = pl.BlockSpec(memory_space=pltpu.HBM)
    dma = pltpu.SemaphoreType.DMA
    scratch = [
        pltpu.SMEM((4, 1, 4), jnp.int32),
        pltpu.SMEM((4,), jnp.int32),
        pltpu.SMEM((4, TOP), jnp.int32),
        pltpu.SMEM((4, TOP), F32),
        pltpu.VMEM((4, KDIM), BF16),
        pltpu.VMEM((4, COLS), BF16),
        pltpu.VMEM((COLS,), F32),
        pltpu.VMEM((4, 64, KDIM), BF16),
        pltpu.VMEM((1, 16, 64, KDIM), BF16),
        pltpu.VMEM((2, LAT, 128), BF16),
        pltpu.VMEM((N_Y, 128, COLS), BF16),
        pltpu.VMEM((COLS, HALF), BF16),
        pltpu.VMEM((COLS, HALF), BF16),
        pltpu.VMEM((HALF, COLS), BF16),
        pltpu.VMEM((128, KDIM), BF16),
        pltpu.VMEM((32, LAT), F32),
        pltpu.VMEM((256, 128), F32),
        pltpu.VMEM((64, LAT), F32),
        pltpu.VMEM((64, COLS), F32),
        pltpu.VMEM((512, 128), F32),
        pltpu.VMEM((32, 128), F32),
        pltpu.VMEM((32, 128), F32),
        pltpu.VMEM((128, 128), F32),
        pltpu.VMEM((32, 128), F32),
        pltpu.VMEM((128, 128), F32),
        pltpu.VMEM((2, 64 * NJ, 256), BF16),
        pltpu.VMEM((2, 2, 32, 128), BF16),
        pltpu.VMEM((4, 8, 128), F32),
        pltpu.VMEM((N_Z, 8, 128), F32),
        pltpu.VMEM((N_CTX, 32, 640), BF16),
        pltpu.VMEM((N_CTX - 1, 32, 640), BF16),
        pltpu.VMEM((8, 16, 128), BF16),
        pltpu.VMEM((N_Z, 16, 128), BF16),
        pltpu.VMEM((64, 128), BF16),
        pltpu.VMEM((N_Y, 64, 128), BF16),
        pltpu.VMEM((N_Z, 32, 128), BF16),
        pltpu.VMEM((N_Z - 1, 32, 128), BF16),
        pltpu.VMEM((32, 128), BF16),
        pltpu.VMEM((N_Z, 32, 128), BF16),
        pltpu.VMEM((2, N_Y, 16, COLS), BF16),
        pltpu.VMEM((2, N_Y, 16, COLS), BF16),
        pltpu.VMEM((2, 4, 16, 1152), BF16),
        pltpu.VMEM((N_CTX - 1, 16, 1152), BF16),
        pltpu.VMEM((16, HALF), BF16),
        pltpu.VMEM((2, 4, 16, HALF), BF16),
        pltpu.VMEM((2, N_Y, 16, COLS), BF16),
        pltpu.VMEM((2, N_Y, 16, COLS), BF16),
        pltpu.VMEM((N_Z, 32, 128), BF16),
        pltpu.VMEM((N_Z - 1, 32, 128), BF16),
        dma((14,)),
    ]
    scratch += [dma((3,)), dma]
    scratch += [dma((3,)), dma((3,))] + [dma] * 6 + [dma((7,)), dma] + [dma] * 6
    scratch += [dma((2,)), dma((2,))]
    scratch += [dma((2,)), dma]
    for count in (7, 2, 0):
        scratch += [dma((count,)), dma((count,))] if count else [dma, dma]
    both = pl.pallas_call(
        kernel,
        out_shape=jax.ShapeDtypeStruct((8, COLS), BF16),
        in_specs=[in_hbm] * 14,
        out_specs=vmem,
        scratch_shapes=scratch,
        compiler_params=pltpu.CompilerParams(
            collective_id=0, has_side_effects=True, vmem_limit_bytes=60 * 1024 * 1024
        ),
    )(
        page_table,
        lengths,
        routes,
        route_weight,
        new_key,
        hidden_in,
        norm_gain,
        queries,
        latent_cache,
        w_uv,
        w_out,
        w_gate,
        w_up,
        w_down,
    )
    return both[:4], both[4:]


def solution(mesh):
    placed = (
        P("ep", None, None),
        P("ep", None),
        P("ctx", "ep", None, None),
        P("ep", "ctx", None),
        P("ep"),
        P("ep", "ctx"),
        P("ep", None, None),
        P("ep", "ctx"),
        P("ctx"),
        P("ep", None),
        P("ep", None),
        P("ctx", "ep"),
        P("ctx", "ep"),
        P("ep", "ctx"),
    )
    return jax.shard_map(
        per_device,
        mesh=mesh,
        in_specs=placed,
        out_specs=(P("ep", "ctx"), P("ep", "ctx")),
        check_vma=False,
    )
```

```python
import jax
import jax.numpy as jnp
from jax import lax
from jax.experimental import pallas as pl
from jax.experimental.pallas import tpu as pltpu
from jax.sharding import PartitionSpec as P

D = 7168
LAT = 512
KDIM = 576
TOP = 8
N_CTX = 8
N_Y = 4
N_Z = 16
COLS = 896
NJ = 7
HALF = 512

score_scale = 192.0 ** (-0.5)
epsilon = 1e-06
very_low = -1e30

MESH = pl.DeviceIdType.MESH
F32 = jnp.float32
BF16 = jnp.bfloat16


def dot(a, b):
    return jnp.dot(a, b, preferred_element_type=F32)


def dot_nt(a, b):
    return lax.dot_general(a, b, (((1,), (1,)), ((), ())), preferred_element_type=F32)


def iota(shape, dim):
    return lax.broadcasted_iota(jnp.int32, shape, dim)


def three_parts(x, shape):
    hi = x.astype(BF16).astype(F32)
    mid = (x - hi).astype(BF16).astype(F32)
    low = x - hi - mid
    lane = iota(shape, 1)
    zero = jnp.zeros(shape, F32)
    return jnp.where(lane == 0, hi, jnp.where(lane == 1, mid, jnp.where(lane == 2, low, zero)))


def kernel(
    page_table_in,
    lengths_in,
    routes_in,
    route_weight_in,
    new_key_in,
    hidden_in,
    gain_in,
    queries,
    cache,
    w_uv,
    w_out,
    w_gate,
    w_up,
    w_down,
    out,
    page_table,
    lengths,
    routes,
    route_weight,
    new_key,
    hidden,
    gain,
    q_vm,
    cache_vm,
    wuv_vm,
    wout_vm,
    gate_vm,
    up_vm,
    down_vm,
    nk_scr,
    att_scr,
    tile_scr,
    lhs_scr,
    wide_scr,
    z_scr,
    small_scr,
    hid_scr,
    gain_scr,
    res_scr,
    col_scr,
    sel_scr,
    comb_scr,
    info_send,
    info_recv,
    p2_send,
    p2_recv,
    p3_send,
    p3_recv,
    p4_send,
    p4_recv,
    p5_send,
    p5_recv,
    p6_send,
    p6_recv,
    p6b_send,
    xe,
    p7_send,
    p7_recv,
    p8_send,
    mid_all,
    p9_send,
    p9_recv,
    p10_send,
    p10_recv,
    lsem,
    uv_s,
    uv_r,
    wo_s,
    wo_r,
    info_s,
    info_r,
    p2_s,
    p2_r,
    p3_s,
    p3_r,
    p4_s,
    p4_r,
    p5_s,
    p5_r,
    p6_s,
    p6_r,
    p6f_s,
    p6f_r,
    p6b_s,
    p6b_r,
    p7_s,
    p7_r,
    p8_s,
    p8_r,
    p9_s,
    p9_r,
    p10_s,
    p10_r,
):
    c = lax.axis_index("ctx")
    ep = lax.axis_index("ep")
    y = ep // N_Z
    z = ep % N_Z
    x = c // 2
    core = c % 2
    has_head = z // 8 == core

    def remote(src, dst, ssem, rsem, to_ctx, to_ep):
        return pltpu.make_async_remote_copy(
            src_ref=src,
            dst_ref=dst,
            send_sem=ssem,
            recv_sem=rsem,
            device_id={"ctx": to_ctx, "ep": to_ep},
            device_id_type=MESH,
        )

    def each(count, step):
        def body(i, carry):
            step(i)
            return carry

        lax.fori_loop(0, count, body, 0)

    loads = [
        pltpu.make_async_copy(src, dst, lsem.at[i])
        for i, (src, dst) in enumerate(
            [
                (queries, q_vm),
                (cache, cache_vm),
                (w_uv, wuv_vm.at[0:1]),
                (w_out, wout_vm.at[y]),
                (w_gate, gate_vm),
                (w_up, up_vm),
                (w_down, down_vm),
                (page_table_in, page_table),
                (lengths_in, lengths),
                (routes_in, routes),
                (route_weight_in, route_weight),
                (new_key_in, new_key),
                (hidden_in, hidden),
                (gain_in, gain),
            ]
        )
    ]
    for load in loads[:2] + loads[7:] + loads[2:7]:
        load.start()
    pending = []

    def finish():
        for wait in pending:
            wait()

    def landed(buffer, sem):
        pltpu.make_async_copy(buffer, buffer, sem).wait()

    def z_step(i):
        return 8 + (i + 1) // 2 * (1 - 2 * (i % 2))

    def near(i):
        step = z_step(8 + i)
        return step, step % 8

    def far(i):
        step = z_step(i)
        return step, step + 4

    barrier = pltpu.get_barrier_semaphore()

    def greet(to_ctx, to_ep):
        pl.semaphore_signal(
            barrier, inc=1, device_id={"ctx": to_ctx, "ep": to_ep}, device_id_type=MESH
        )

    each(N_Z - 1, lambda i: greet(c, y * N_Z + (z + z_step(i)) % N_Z))
    each(N_Y - 1, lambda i: greet(c, (y + i + 1) % N_Y * N_Z + z))
    each(N_CTX - 1, lambda i: greet((c + i + 1) % N_CTX, ep))

    for load in loads[7:]:
        load.wait()

    row = iota((32, 128), 0)
    expert = ((row // 2) % 4 + y) % 4 * 4 + row // 8
    place = row % 2
    before = jnp.zeros((32, 128), jnp.int32)
    pick = jnp.zeros((32, 128), F32)
    weight = jnp.zeros((32, 128), F32)
    for r in range(4):
        named = jnp.zeros((32, 128), jnp.int32)
        w_r = jnp.zeros((32, 128), F32)
        for k in range(TOP):
            hit = expert == routes[r, k]
            named = jnp.where(hit, 1, named)
            w_r = jnp.where(hit, route_weight[r, k], w_r)
        taken = (named == 1) & (before == place)
        pick = jnp.where(taken, float(r), pick)
        weight = jnp.where(taken, w_r, weight)
        before = before + named
    info = jnp.where(iota((32, 128), 1) < 64, pick, weight)
    info_send[...] = info.reshape(4, 8, 128)
    info_recv[0] = info_send[z // 4]

    hid_scr[28:32, :] = jnp.zeros((4, 128), F32)
    gain_scr[...] = jnp.zeros((128, 128), F32)
    hid32 = hidden[...].astype(F32)
    for j in range(NJ):
        hid_scr[4 * j : 4 * j + 4, :] = hid32[:, 128 * j : 128 * j + 128]
        gain_scr[j : j + 1, :] = gain[128 * j : 128 * j + 128].reshape(1, 128)
    gain_scr[...] = jnp.transpose(gain_scr[...])
    nk_scr[...] = jnp.zeros((128, KDIM), BF16)
    nk_scr[0:4, :] = new_key[...]
    for zz in range(N_Z):
        z_scr[32 * zz + 28 : 32 * zz + 32, :] = jnp.zeros((4, 128), F32)

    col = iota((1, 1024), 1)
    slot = col // 64
    owner = jnp.full((1, 1024), -1, jnp.int32)
    for r in range(4):
        for p in range(4):
            position = (p * N_CTX + c) * 64 + col % 64
            good = (slot == page_table[r, 0, p]) & (position < lengths[r])
            owner = jnp.where(good, r, owner)
    i0 = iota((256, 256), 0)
    shuffle = jnp.where((i0 % 4) * 64 + i0 // 4 == iota((256, 256), 1), 1.0, 0.0).astype(BF16)
    loads[0].wait()
    q = dot(shuffle, q_vm[...].reshape(256, KDIM)).astype(BF16)
    loads[1].wait()
    keys = cache_vm[...].reshape(1024, KDIM)
    scores = dot_nt(q, keys) * score_scale
    fresh = dot_nt(q, nk_scr[...]) * score_scale
    mask = owner == iota((256, 1024), 0) % 4
    mask_new = iota((256, 128), 1) + 1024 * c == iota((256, 128), 0) % 4
    peak = jnp.maximum(
        jnp.max(jnp.where(mask, scores, very_low), axis=1, keepdims=True),
        jnp.max(jnp.where(mask_new, fresh, very_low), axis=1, keepdims=True),
    )
    weights = jnp.where(mask, jnp.exp(scores - peak), 0.0).astype(BF16)
    weights_new = jnp.where(mask_new, jnp.exp(fresh - peak), 0.0).astype(BF16)
    total = jnp.sum(weights.astype(F32), axis=1, keepdims=True) + jnp.sum(
        weights_new.astype(F32), axis=1, keepdims=True
    )
    mixture = dot(weights, keys[:, :LAT]) + dot(weights_new, nk_scr[:, :LAT])
    some = total > 0.0
    total = jnp.where(some, total, 1.0)
    logsum = jnp.where(some, peak + jnp.log(total), very_low)
    p2_send[:, :, :LAT] = (mixture / total).astype(BF16).reshape(N_CTX, 32, LAT)
    p2_send[:, :, LAT:] = three_parts(logsum, (256, 128)).astype(BF16).reshape(N_CTX, 32, 128)

    pl.semaphore_wait(barrier, N_Z - 1 + N_Y - 1 + N_CTX - 1)

    def ctx_step(k):
        return (c // 2 + k // 2) % 4 * 2 + (c + k) % 2

    def ctx_back(k):
        return (c // 2 + 4 - k // 2) % 4 * 2 + (c + k) % 2

    ctx_order = (4, 5, 2, 3, 6, 7, 1)
    y_order = (2, 1, 3)

    def ctx_scatter(send, recv, ssem, rsem):
        for k in ctx_order:
            to = ctx_step(k)
            remote(send.at[to], recv.at[k - 1], ssem, rsem, to, ep).start()
        pending.append(lambda: landed(recv, ssem))

    ctx_scatter(p2_send, p2_recv, p2_s, p2_r)

    def info_copy(i, place):
        step, position = place(i)
        to = (z + step) % N_Z
        remote(
            info_send.at[to // 4], info_recv.at[position], info_s, info_r, c, y * N_Z + to
        ).start()

    each(8, lambda i: info_copy(i, far))
    each(7, lambda i: info_copy(i, near))
    pending.append(lambda: landed(info_recv.at[1:N_Z], info_s))

    def uv_copy(k):
        return remote(
            w_uv,
            wuv_vm.at[1:2],
            uv_s.at[k - 1],
            uv_r,
            c,
            (y + k) % N_Y * N_Z + z,
        )

    @pl.when(has_head & (y == x))
    def _():
        for k in y_order:
            uv_copy(k).start()

    def uv_sent():
        @pl.when(has_head & (y == x))
        def _():
            for k in y_order:
                uv_copy(k).wait_send()

    pending.append(uv_sent)

    for k in y_order:
        remote(
            w_out, wout_vm.at[y], wo_s.at[k - 1], wo_r.at[k - 1], c, (y + k) % N_Y * N_Z + z
        ).start()
    for k in y_order:
        pending.append(
            remote(
                w_out, wout_vm.at[y], wo_s.at[k - 1], wo_r.at[k - 1], c, (y + k) % N_Y * N_Z + z
            ).wait_send
        )

    def wo_arrival(k):
        frm = (y + N_Y - k) % N_Y
        return remote(w_out, wout_vm.at[frm], wo_s.at[k - 1], wo_r.at[k - 1], c, frm * N_Z + z)

    landed(p2_recv, p2_r)
    parts = [p2_send[c]] + [p2_recv[i] for i in range(N_CTX - 1)]
    logs = [jnp.sum(p[:, LAT:].astype(F32), axis=1, keepdims=True) for p in parts]
    top = logs[0]
    for l in logs[1:]:
        top = jnp.maximum(top, l)
    above = jnp.zeros((32, LAT), F32)
    below = jnp.zeros((32, 1), F32)
    for p, l in zip(parts, logs):
        f = jnp.exp(l - top)
        above = above + f * p[:, :LAT].astype(F32)
        below = below + f
    att_scr[...] = above / below
    for i in range(8):
        for j in range(4):
            tile_scr[16 * i + 4 * j : 16 * i + 4 * j + 4, :] = att_scr[
                4 * i : 4 * i + 4, 128 * j : 128 * j + 128
            ]
    p3_send[...] = tile_scr[0:128, :].astype(BF16).reshape(8, 16, 128)

    def p3_each(step):
        def one(n):
            i = (z + z_step(n)) % 8

            @pl.when(z != 8 * core + i)
            def _():
                step(i)

        each(8, one)

    def p3_copy(i):
        to = 8 * core + i
        remote(
            p3_send.at[i], p3_recv.at[(to + N_Z - z) % N_Z], p3_s, p3_r, c, y * N_Z + to
        ).start()

    p3_each(p3_copy)

    def p3_sent():
        @pl.when(has_head)
        def _():
            landed(p3_send.at[0:7], p3_s)

        @pl.when(jnp.logical_not(has_head))
        def _():
            landed(p3_send, p3_s)

    pending.append(p3_sent)
    loads[4].wait()
    loads[5].wait()
    for j in range(NJ):
        factor = gain_scr[:, j : j + 1]
        for w in (gate_vm, up_vm):
            block = w[128 * j : 128 * j + 128, :].astype(F32)
            w[128 * j : 128 * j + 128, :] = (block * factor).astype(BF16)
    loads[2].wait()

    def p4_copy(k):
        return remote(p4_send, p4_recv.at[x], p4_s.at[k - 1], p4_r, ctx_step(k), ep)

    @pl.when(has_head)
    def _():
        p3_recv[0] = p3_send[z % 8]
        landed(p3_recv.at[1:N_Z], p3_r)

        @pl.when(y != x)
        def _():
            remote(w_uv, wuv_vm.at[1:2], uv_s.at[0], uv_r, c, x * N_Z + z).wait_recv()

        tile_scr[...] = p3_recv[...].astype(F32).reshape(256, 128)
        for i in range(N_Z):
            for j in range(4):
                lhs_scr[4 * i : 4 * i + 4, 128 * j : 128 * j + 128] = tile_scr[
                    16 * i + 4 * j : 16 * i + 4 * j + 4, :
                ]
        which = jnp.where(y == x, 0, 1).astype(jnp.int32)
        values = dot(lhs_scr[...].astype(BF16), wuv_vm[which]).astype(BF16)
        p4_send[...] = values
        p4_recv[x] = values

        for k in ctx_order:
            p4_copy(k).start()

    def p4_sent():
        @pl.when(has_head)
        def _():
            for k in ctx_order:
                p4_copy(k).wait_send()

    pending.append(p4_sent)

    landed(info_recv.at[1:N_Z], info_r)
    for part in range(2):
        for k in range(8):
            row0 = 64 * part + 8 * k
            col_scr[row0 : row0 + 8, :] = info_recv[8 * part : 8 * part + 8, k, :]
    pick_col = col_scr[:, 0:1].astype(jnp.int32)
    weight_col = col_scr[:, 64:65]
    source = iota((128, 1), 0) % 8
    target = source * 32 + pick_col
    lane = iota((64, 256), 1)
    spread = jnp.where(iota((128, 128), 1) == source * 4 + pick_col, weight_col, 0.0)
    for part in range(2):
        for j in range(NJ):
            sel_scr[part, 64 * j : 64 * j + 64, :] = jnp.where(
                lane == target[64 * part : 64 * part + 64] + 4 * j, 1.0, 0.0
            ).astype(BF16)
        block = jnp.concatenate(
            [spread[64 * part : 64 * part + 64], jnp.zeros((64, 128), F32)], axis=0
        )
        comb = jnp.transpose(block)[0:32, :]
        comb_hi = comb.astype(BF16)
        comb_scr[part, 0] = comb_hi
        comb_scr[part, 1] = (comb - comb_hi.astype(F32)).astype(BF16)

    loads[3].wait()
    for k in y_order:
        wo_arrival(k).wait_recv()
    @pl.when(has_head)
    def _():
        landed(p4_recv.at[0:3], p4_r)

    @pl.when(jnp.logical_not(has_head))
    def _():
        landed(p4_recv, p4_r)

    lhs = jnp.concatenate([p4_recv[k] for k in range(N_Y)], axis=1)

    def to_tiles(values32, first, count):
        wide_scr[0 : 4 * count, :] = values32
        for zz in range(count):
            for j in range(NJ):
                row0 = 32 * (first + zz) + 4 * j
                z_scr[row0 : row0 + 4, :] = wide_scr[
                    4 * zz : 4 * zz + 4, 128 * j : 128 * j + 128
                ]
        tiles = z_scr[32 * first : 32 * (first + count), :]
        return tiles.astype(BF16).reshape(count, 32, 128)

    def z_send(values32, part, send, recv, ssem, rsem):
        send[8 * part : 8 * part + 8] = to_tiles(values32, 8 * part, 8)
        count, place = ((7, near), (8, far))[part]

        def copy(i):
            step, position = place(i)
            remote(
                send.at[position],
                recv.at[step - 1],
                ssem,
                rsem,
                c,
                y * N_Z + (z + N_Z - step) % N_Z,
            ).start()

        each(count, copy)

    def z_total(recv, rsem):
        total = z_scr[0:32, :]
        landed(recv, rsem)
        for i in range(N_Z - 1):
            total = total + recv[i].astype(F32)
        return total

    projection = wout_vm[...].reshape(512, COLS)
    z_send(dot(lhs[16:48], projection), 1, p5_send, p5_recv, p5_s, p5_r)
    others = jnp.concatenate([lhs[0:16], lhs[48:64]], axis=0)
    z_send(dot(others, projection), 0, p5_send, p5_recv, p5_s, p5_r)
    pending.append(lambda: landed(p5_recv, p5_s))
    attention = z_total(p5_recv, p5_r)
    residual = hid_scr[...] + attention
    rounded = residual.astype(BF16)
    p6_send[...] = rounded
    p6_recv[0] = rounded

    def p6_copy(i, place, ssem, rsem):
        step, position = place(i)
        remote(
            p6_send, p6_recv.at[position], ssem, rsem, c, y * N_Z + (z + step) % N_Z
        ).start()

    each(8, lambda i: p6_copy(i, far, p6f_s, p6f_r))
    each(7, lambda i: p6_copy(i, near, p6_s, p6_r))
    pending.append(lambda: landed(p6_recv.at[1:8], p6_s))
    pending.append(lambda: landed(p6_recv.at[8:16], p6f_s))
    res_scr[...] = residual
    small_scr[...] = attention
    for j in range(NJ):
        out[0:4, 128 * j : 128 * j + 128] = small_scr[4 * j : 4 * j + 4, :].astype(BF16)

    def y_send(send, recv, ssem, rsem, sign):
        for k in y_order:
            remote(
                send.at[k], recv.at[k], ssem, rsem, c, (y + N_Y + sign * k) % N_Y * N_Z + z
            ).start()
        pending.append(lambda: landed(recv.at[1:N_Y], ssem))
        recv[0] = send[0]

    def pick_rows(part):
        arrived = p6_recv[8 * part : 8 * part + 8].reshape(256, 128)
        picked = dot(sel_scr[part], arrived).astype(BF16)
        for j in range(NJ):
            p6b_send[part, :, :, 128 * j : 128 * j + 128] = picked[
                64 * j : 64 * j + 64, :
            ].reshape(N_Y, 16, 128)
        y_send(p6b_send.at[part], xe.at[part], p6b_s.at[part], p6b_r.at[part], 1)

    def gate_up(part):
        landed(xe.at[part].at[1:N_Y], p6b_r.at[part])
        rows = xe[part].reshape(64, COLS)
        rows32 = rows.astype(F32)
        squares = jnp.sum(rows32 * rows32, axis=1, keepdims=True)
        p7_send[part, :, :, 2 * HALF :] = (
            three_parts(squares, (64, 128)).astype(BF16).reshape(N_Y, 16, 128)
        )
        p7_send[part, :, :, :HALF] = dot(rows, gate_vm[...]).astype(BF16).reshape(N_Y, 16, HALF)
        p7_send[part, :, :, HALF : 2 * HALF] = (
            dot(rows, up_vm[...]).astype(BF16).reshape(N_Y, 16, HALF)
        )
        side = (core + part) % 2
        for dx in (2, 1, 3):
            there = (x + dx) % 4
            remote(
                p7_send.at[part, there],
                p7_recv.at[2 * dx + side - 1],
                p7_s.at[part],
                p7_r,
                there * 2 + part,
                ep,
            ).start()

        @pl.when(core != part)
        def _():
            remote(
                p7_send.at[part, x], p7_recv.at[0], p7_s.at[part], p7_r, x * 2 + part, ep
            ).start()

    def gate_up_sent(part):
        landed(p7_recv.at[0:3], p7_s.at[part])

        @pl.when(core != part)
        def _():
            landed(p7_recv.at[0], p7_s.at[part])

    landed(p6_recv.at[1:8], p6_r)
    pick_rows(0)
    landed(p6_recv.at[8:16], p6f_r)
    pick_rows(1)
    gate_up(0)
    gate_up(1)
    pending.append(lambda: gate_up_sent(0))
    pending.append(lambda: gate_up_sent(1))

    landed(p7_recv, p7_r)
    sums = p7_send[core, x].astype(F32)
    for i in range(N_CTX - 1):
        sums = sums + p7_recv[i].astype(F32)
    mean = jnp.sum(sums[:, 2 * HALF :], axis=1, keepdims=True) / D
    scale = lax.rsqrt(mean + epsilon)
    gate = sums[:, :HALF] * scale
    up = sums[:, HALF : 2 * HALF] * scale
    middle = (gate / (1.0 + jnp.exp(-gate)) * up).astype(BF16)
    p8_send[...] = middle
    mid_all[core, x] = middle
    for k in ctx_order:
        remote(
            p8_send, mid_all.at[core, x], p8_s.at[k - 1], p8_r.at[k - 1], ctx_step(k), ep
        ).start()
    for k in ctx_order:
        pending.append(
            remote(
                p8_send, mid_all.at[core, x], p8_s.at[k - 1], p8_r.at[k - 1], ctx_step(k), ep
            ).wait_send
        )
    loads[6].wait()

    def project(part):
        side = (core + part) % 2
        for dx in (1, 3, 2):
            frm = (x + 4 - dx) % 4
            sem = 2 * dx + side - 1
            remote(
                p8_send, mid_all.at[part, frm], p8_s.at[sem], p8_r.at[sem], frm * 2 + part, ep
            ).wait_recv()

        @pl.when(core != part)
        def _():
            remote(
                p8_send, mid_all.at[part, x], p8_s.at[0], p8_r.at[0], x * 2 + part, ep
            ).wait_recv()

        produced = dot(mid_all[part].reshape(64, HALF), down_vm[...])
        p9_send[part] = produced.astype(BF16).reshape(N_Y, 16, COLS)
        y_send(p9_send.at[part], p9_recv.at[part], p9_s.at[part], p9_r.at[part], -1)

    project(1)
    project(0)

    def combine(part):
        landed(p9_recv.at[part].at[1:N_Y], p9_r.at[part])
        back = p9_recv[part].reshape(64, COLS)
        mixed = dot(comb_scr[part, 0][:, :64], back) + dot(comb_scr[part, 1][:, :64], back)
        z_send(mixed, part, p10_send, p10_recv, p10_s, p10_r)

    combine(1)
    combine(0)
    finish()
    routed = z_total(p10_recv, p10_r)
    landed(p10_recv, p10_s)
    small_scr[...] = res_scr[...] + routed
    for j in range(NJ):
        out[4:8, 128 * j : 128 * j + 128] = small_scr[4 * j : 4 * j + 4, :].astype(BF16)


def per_device(
    queries,
    new_key,
    latent_cache,
    page_table,
    lengths,
    hidden_in,
    w_uv,
    w_out,
    norm_gain,
    routes,
    route_weight,
    w_gate,
    w_up,
    w_down,
):
    vmem = pl.BlockSpec(memory_space=pltpu.VMEM)
    in_hbm = pl.BlockSpec(memory_space=pltpu.HBM)
    dma = pltpu.SemaphoreType.DMA
    scratch = [
        pltpu.SMEM((4, 1, 4), jnp.int32),
        pltpu.SMEM((4,), jnp.int32),
        pltpu.SMEM((4, TOP), jnp.int32),
        pltpu.SMEM((4, TOP), F32),
        pltpu.VMEM((4, KDIM), BF16),
        pltpu.VMEM((4, COLS), BF16),
        pltpu.VMEM((COLS,), F32),
        pltpu.VMEM((4, 64, KDIM), BF16),
        pltpu.VMEM((1, 16, 64, KDIM), BF16),
        pltpu.VMEM((2, LAT, 128), BF16),
        pltpu.VMEM((N_Y, 128, COLS), BF16),
        pltpu.VMEM((COLS, HALF), BF16),
        pltpu.VMEM((COLS, HALF), BF16),
        pltpu.VMEM((HALF, COLS), BF16),
        pltpu.VMEM((128, KDIM), BF16),
        pltpu.VMEM((32, LAT), F32),
        pltpu.VMEM((256, 128), F32),
        pltpu.VMEM((64, LAT), F32),
        pltpu.VMEM((64, COLS), F32),
        pltpu.VMEM((512, 128), F32),
        pltpu.VMEM((32, 128), F32),
        pltpu.VMEM((32, 128), F32),
        pltpu.VMEM((128, 128), F32),
        pltpu.VMEM((32, 128), F32),
        pltpu.VMEM((128, 128), F32),
        pltpu.VMEM((2, 64 * NJ, 256), BF16),
        pltpu.VMEM((2, 2, 32, 128), BF16),
        pltpu.VMEM((4, 8, 128), F32),
        pltpu.VMEM((N_Z, 8, 128), F32),
        pltpu.VMEM((N_CTX, 32, 640), BF16),
        pltpu.VMEM((N_CTX - 1, 32, 640), BF16),
        pltpu.VMEM((8, 16, 128), BF16),
        pltpu.VMEM((N_Z, 16, 128), BF16),
        pltpu.VMEM((64, 128), BF16),
        pltpu.VMEM((N_Y, 64, 128), BF16),
        pltpu.VMEM((N_Z, 32, 128), BF16),
        pltpu.VMEM((N_Z - 1, 32, 128), BF16),
        pltpu.VMEM((32, 128), BF16),
        pltpu.VMEM((N_Z, 32, 128), BF16),
        pltpu.VMEM((2, N_Y, 16, COLS), BF16),
        pltpu.VMEM((2, N_Y, 16, COLS), BF16),
        pltpu.VMEM((2, 4, 16, 1152), BF16),
        pltpu.VMEM((N_CTX - 1, 16, 1152), BF16),
        pltpu.VMEM((16, HALF), BF16),
        pltpu.VMEM((2, 4, 16, HALF), BF16),
        pltpu.VMEM((2, N_Y, 16, COLS), BF16),
        pltpu.VMEM((2, N_Y, 16, COLS), BF16),
        pltpu.VMEM((N_Z, 32, 128), BF16),
        pltpu.VMEM((N_Z - 1, 32, 128), BF16),
        dma((14,)),
    ]
    scratch += [dma((3,)), dma]
    scratch += [dma((3,)), dma((3,))] + [dma] * 6 + [dma((7,)), dma] + [dma] * 6
    scratch += [dma((2,)), dma((2,))]
    scratch += [dma((2,)), dma]
    for count in (7, 2, 0):
        scratch += [dma((count,)), dma((count,))] if count else [dma, dma]
    both = pl.pallas_call(
        kernel,
        out_shape=jax.ShapeDtypeStruct((8, COLS), BF16),
        in_specs=[in_hbm] * 14,
        out_specs=vmem,
        scratch_shapes=scratch,
        compiler_params=pltpu.CompilerParams(
            collective_id=0, has_side_effects=True, vmem_limit_bytes=60 * 1024 * 1024
        ),
    )(
        page_table,
        lengths,
        routes,
        route_weight,
        new_key,
        hidden_in,
        norm_gain,
        queries,
        latent_cache,
        w_uv,
        w_out,
        w_gate,
        w_up,
        w_down,
    )
    return both[:4], both[4:]


def solution(mesh):
    placed = (
        P("ep", None, None),
        P("ep", None),
        P("ctx", "ep", None, None),
        P("ep", "ctx", None),
        P("ep"),
        P("ep", "ctx"),
        P("ep", None, None),
        P("ep", "ctx"),
        P("ctx"),
        P("ep", None),
        P("ep", None),
        P("ctx", "ep"),
        P("ctx", "ep"),
        P("ep", "ctx"),
    )
    return jax.shard_map(
        per_device,
        mesh=mesh,
        in_specs=placed,
        out_specs=(P("ep", "ctx"), P("ep", "ctx")),
        check_vma=False,
    )
```

```python
import jax
import jax.numpy as jnp
from jax import lax
from jax.experimental import pallas as pl
from jax.experimental.pallas import tpu as pltpu
from jax.sharding import PartitionSpec as P

D = 7168
LAT = 512
KDIM = 576
TOP = 8
N_CTX = 8
N_Y = 4
N_Z = 16
COLS = 896
NJ = 7
HALF = 512

score_scale = 192.0 ** (-0.5)
epsilon = 1e-06
very_low = -1e30

MESH = pl.DeviceIdType.MESH
F32 = jnp.float32
BF16 = jnp.bfloat16


def dot(a, b):
    return jnp.dot(a, b, preferred_element_type=F32)


def dot_nt(a, b):
    return lax.dot_general(a, b, (((1,), (1,)), ((), ())), preferred_element_type=F32)


def iota(shape, dim):
    return lax.broadcasted_iota(jnp.int32, shape, dim)


def three_parts(x, shape):
    hi = x.astype(BF16).astype(F32)
    mid = (x - hi).astype(BF16).astype(F32)
    low = x - hi - mid
    lane = iota(shape, 1)
    zero = jnp.zeros(shape, F32)
    return jnp.where(lane == 0, hi, jnp.where(lane == 1, mid, jnp.where(lane == 2, low, zero)))


def kernel(
    page_table_in,
    lengths_in,
    routes_in,
    route_weight_in,
    new_key_in,
    hidden_in,
    gain_in,
    queries,
    cache,
    w_uv,
    w_out,
    w_gate,
    w_up,
    w_down,
    out,
    page_table,
    lengths,
    routes,
    route_weight,
    new_key,
    hidden,
    gain,
    q_vm,
    cache_vm,
    wuv_vm,
    wout_vm,
    gate_vm,
    up_vm,
    down_vm,
    nk_scr,
    att_scr,
    tile_scr,
    lhs_scr,
    wide_scr,
    z_scr,
    small_scr,
    hid_scr,
    gain_scr,
    res_scr,
    col_scr,
    sel_scr,
    comb_scr,
    info_send,
    info_recv,
    p2_send,
    p2_recv,
    p3_send,
    p3_recv,
    p4_send,
    p4_recv,
    p5_send,
    p5_recv,
    p6_send,
    p6_recv,
    p6b_send,
    xe,
    p7_send,
    p7_recv,
    p7u_send,
    p7u_recv,
    p8_send,
    mid_all,
    p9_send,
    p9_recv,
    p10_send,
    p10_recv,
    lsem,
    uv_s,
    uv_r,
    wo_s,
    wo_r,
    info_s,
    info_r,
    p2_s,
    p2_r,
    p3_s,
    p3_r,
    p4_s,
    p4_r,
    p5_s,
    p5_r,
    p6_s,
    p6_r,
    p6f_s,
    p6f_r,
    p6b_s,
    p6b_r,
    p7_s,
    p7_r,
    p7u_s,
    p7u_r,
    p8_s,
    p8_r,
    p9_s,
    p9_r,
    p10_s,
    p10_r,
):
    c = lax.axis_index("ctx")
    ep = lax.axis_index("ep")
    y = ep // N_Z
    z = ep % N_Z
    x = c // 2
    core = c % 2
    has_head = z // 8 == core

    def remote(src, dst, ssem, rsem, to_ctx, to_ep):
        return pltpu.make_async_remote_copy(
            src_ref=src,
            dst_ref=dst,
            send_sem=ssem,
            recv_sem=rsem,
            device_id={"ctx": to_ctx, "ep": to_ep},
            device_id_type=MESH,
        )

    def each(count, step):
        def body(i, carry):
            step(i)
            return carry

        lax.fori_loop(0, count, body, 0)

    loads = [
        pltpu.make_async_copy(src, dst, lsem.at[i])
        for i, (src, dst) in enumerate(
            [
                (queries, q_vm),
                (cache, cache_vm),
                (w_uv, wuv_vm.at[0:1]),
                (w_out, wout_vm.at[y]),
                (w_gate, gate_vm),
                (w_up, up_vm),
                (w_down, down_vm),
                (page_table_in, page_table),
                (lengths_in, lengths),
                (routes_in, routes),
                (route_weight_in, route_weight),
                (new_key_in, new_key),
                (hidden_in, hidden),
                (gain_in, gain),
            ]
        )
    ]
    for load in loads[:2] + loads[7:] + loads[2:7]:
        load.start()
    pending = []

    def finish():
        for wait in pending:
            wait()

    def landed(buffer, sem):
        pltpu.make_async_copy(buffer, buffer, sem).wait()

    def z_step(i):
        return 8 + (i + 1) // 2 * (1 - 2 * (i % 2))

    def near(i):
        step = z_step(8 + i)
        return step, step % 8

    def far(i):
        step = z_step(i)
        return step, step + 4

    barrier = pltpu.get_barrier_semaphore()

    def greet(to_ctx, to_ep):
        pl.semaphore_signal(
            barrier, inc=1, device_id={"ctx": to_ctx, "ep": to_ep}, device_id_type=MESH
        )

    each(N_Z - 1, lambda i: greet(c, y * N_Z + (z + z_step(i)) % N_Z))
    each(N_Y - 1, lambda i: greet(c, (y + i + 1) % N_Y * N_Z + z))
    each(N_CTX - 1, lambda i: greet((c + i + 1) % N_CTX, ep))

    for load in loads[7:]:
        load.wait()

    row = iota((32, 128), 0)
    expert = ((row // 2) % 4 + y) % 4 * 4 + row // 8
    place = row % 2
    before = jnp.zeros((32, 128), jnp.int32)
    pick = jnp.zeros((32, 128), F32)
    weight = jnp.zeros((32, 128), F32)
    for r in range(4):
        named = jnp.zeros((32, 128), jnp.int32)
        w_r = jnp.zeros((32, 128), F32)
        for k in range(TOP):
            hit = expert == routes[r, k]
            named = jnp.where(hit, 1, named)
            w_r = jnp.where(hit, route_weight[r, k], w_r)
        taken = (named == 1) & (before == place)
        pick = jnp.where(taken, float(r), pick)
        weight = jnp.where(taken, w_r, weight)
        before = before + named
    info = jnp.where(iota((32, 128), 1) < 64, pick, weight)
    info_send[...] = info.reshape(4, 8, 128)
    info_recv[0] = info_send[z // 4]

    hid_scr[28:32, :] = jnp.zeros((4, 128), F32)
    gain_scr[...] = jnp.zeros((128, 128), F32)
    hid32 = hidden[...].astype(F32)
    for j in range(NJ):
        hid_scr[4 * j : 4 * j + 4, :] = hid32[:, 128 * j : 128 * j + 128]
        gain_scr[j : j + 1, :] = gain[128 * j : 128 * j + 128].reshape(1, 128)
    gain_scr[...] = jnp.transpose(gain_scr[...])
    nk_scr[...] = jnp.zeros((128, KDIM), BF16)
    nk_scr[0:4, :] = new_key[...]
    for zz in range(N_Z):
        z_scr[32 * zz + 28 : 32 * zz + 32, :] = jnp.zeros((4, 128), F32)

    col = iota((1, 1024), 1)
    slot = col // 64
    owner = jnp.full((1, 1024), -1, jnp.int32)
    for r in range(4):
        for p in range(4):
            position = (p * N_CTX + c) * 64 + col % 64
            good = (slot == page_table[r, 0, p]) & (position < lengths[r])
            owner = jnp.where(good, r, owner)
    i0 = iota((256, 256), 0)
    shuffle = jnp.where((i0 % 4) * 64 + i0 // 4 == iota((256, 256), 1), 1.0, 0.0).astype(BF16)
    loads[0].wait()
    q = dot(shuffle, q_vm[...].reshape(256, KDIM)).astype(BF16)
    loads[1].wait()
    keys = cache_vm[...].reshape(1024, KDIM)
    scores = dot_nt(q, keys) * score_scale
    fresh = dot_nt(q, nk_scr[...]) * score_scale
    mask = owner == iota((256, 1024), 0) % 4
    mask_new = iota((256, 128), 1) + 1024 * c == iota((256, 128), 0) % 4
    peak = jnp.maximum(
        jnp.max(jnp.where(mask, scores, very_low), axis=1, keepdims=True),
        jnp.max(jnp.where(mask_new, fresh, very_low), axis=1, keepdims=True),
    )
    weights = jnp.where(mask, jnp.exp(scores - peak), 0.0).astype(BF16)
    weights_new = jnp.where(mask_new, jnp.exp(fresh - peak), 0.0).astype(BF16)
    total = jnp.sum(weights.astype(F32), axis=1, keepdims=True) + jnp.sum(
        weights_new.astype(F32), axis=1, keepdims=True
    )
    mixture = dot(weights, keys[:, :LAT]) + dot(weights_new, nk_scr[:, :LAT])
    some = total > 0.0
    total = jnp.where(some, total, 1.0)
    logsum = jnp.where(some, peak + jnp.log(total), very_low)
    mixture = (mixture / total).astype(BF16)
    for j in range(4):
        p2_send[:, 32 * j : 32 * j + 32, :] = mixture[:, 128 * j : 128 * j + 128].reshape(
            N_CTX, 32, 128
        )
    logsum = three_parts(logsum, (256, 128)).reshape(N_CTX, 32, 128)
    p2_send[:, 128:144, :] = jnp.where(
        iota((N_CTX, 16, 128), 2) < 64, logsum[:, :16], jnp.roll(logsum[:, 16:], 64, axis=2)
    ).astype(BF16)

    pl.semaphore_wait(barrier, N_Z - 1 + N_Y - 1 + N_CTX - 1)

    def ctx_step(k):
        return (c // 2 + k // 2) % 4 * 2 + (c + k) % 2

    def ctx_back(k):
        return (c // 2 + 4 - k // 2) % 4 * 2 + (c + k) % 2

    ctx_order = (4, 5, 2, 3, 6, 7, 1)
    y_order = (2, 1, 3)

    def ctx_scatter(send, recv, ssem, rsem):
        for k in ctx_order:
            to = ctx_step(k)
            remote(send.at[to], recv.at[k - 1], ssem, rsem, to, ep).start()
        pending.append(lambda: landed(recv, ssem))

    ctx_scatter(p2_send, p2_recv, p2_s, p2_r)

    def info_copy(i, place):
        step, position = place(i)
        to = (z + step) % N_Z
        remote(
            info_send.at[to // 4], info_recv.at[position], info_s, info_r, c, y * N_Z + to
        ).start()

    each(8, lambda i: info_copy(i, far))
    each(7, lambda i: info_copy(i, near))
    pending.append(lambda: landed(info_recv.at[1:N_Z], info_s))

    def uv_copy(k):
        return remote(
            w_uv,
            wuv_vm.at[1:2],
            uv_s.at[k - 1],
            uv_r,
            c,
            (y + k) % N_Y * N_Z + z,
        )

    @pl.when(has_head & (y == x))
    def _():
        for k in y_order:
            uv_copy(k).start()

    def uv_sent():
        @pl.when(has_head & (y == x))
        def _():
            for k in y_order:
                uv_copy(k).wait_send()

    pending.append(uv_sent)

    for k in y_order:
        remote(
            w_out, wout_vm.at[y], wo_s.at[k - 1], wo_r.at[k - 1], c, (y + k) % N_Y * N_Z + z
        ).start()
    for k in y_order:
        pending.append(
            remote(
                w_out, wout_vm.at[y], wo_s.at[k - 1], wo_r.at[k - 1], c, (y + k) % N_Y * N_Z + z
            ).wait_send
        )

    def wo_arrival(k):
        frm = (y + N_Y - k) % N_Y
        return remote(w_out, wout_vm.at[frm], wo_s.at[k - 1], wo_r.at[k - 1], c, frm * N_Z + z)

    landed(p2_recv, p2_r)
    parts = [p2_send[c]] + [p2_recv[i] for i in range(N_CTX - 1)]
    def row_logs(p):
        both = p[128:144].astype(F32)
        first = iota((16, 128), 1) < 64
        return jnp.concatenate(
            [
                jnp.sum(jnp.where(first, both, 0.0), axis=1, keepdims=True),
                jnp.sum(jnp.where(first, 0.0, both), axis=1, keepdims=True),
            ],
            axis=0,
        )

    logs = [row_logs(p) for p in parts]
    top = logs[0]
    for l in logs[1:]:
        top = jnp.maximum(top, l)
    factors = [jnp.exp(l - top) for l in logs]
    below = factors[0]
    for f in factors[1:]:
        below = below + f
    for j in range(4):
        above = jnp.zeros((32, 128), F32)
        for p, f in zip(parts, factors):
            above = above + f * p[32 * j : 32 * j + 32].astype(F32)
        att_scr[:, 128 * j : 128 * j + 128] = above / below
    for i in range(8):
        for j in range(4):
            tile_scr[16 * i + 4 * j : 16 * i + 4 * j + 4, :] = att_scr[
                4 * i : 4 * i + 4, 128 * j : 128 * j + 128
            ]
    p3_send[...] = tile_scr[0:128, :].astype(BF16).reshape(8, 16, 128)

    def p3_each(step):
        def one(n):
            i = (z + z_step(n)) % 8

            @pl.when(z != 8 * core + i)
            def _():
                step(i)

        each(8, one)

    def p3_copy(i):
        to = 8 * core + i
        remote(
            p3_send.at[i], p3_recv.at[(to + N_Z - z) % N_Z], p3_s, p3_r, c, y * N_Z + to
        ).start()

    p3_each(p3_copy)

    def p3_sent():
        @pl.when(has_head)
        def _():
            landed(p3_send.at[0:7], p3_s)

        @pl.when(jnp.logical_not(has_head))
        def _():
            landed(p3_send, p3_s)

    pending.append(p3_sent)
    loads[4].wait()
    loads[5].wait()
    for j in range(NJ):
        factor = gain_scr[:, j : j + 1]
        for w in (gate_vm, up_vm):
            block = w[128 * j : 128 * j + 128, :].astype(F32)
            w[128 * j : 128 * j + 128, :] = (block * factor).astype(BF16)
    loads[2].wait()

    def p4_copy(k):
        return remote(p4_send, p4_recv.at[x], p4_s.at[k - 1], p4_r, ctx_step(k), ep)

    @pl.when(has_head)
    def _():
        p3_recv[0] = p3_send[z % 8]
        landed(p3_recv.at[1:N_Z], p3_r)

        @pl.when(y != x)
        def _():
            remote(w_uv, wuv_vm.at[1:2], uv_s.at[0], uv_r, c, x * N_Z + z).wait_recv()

        tile_scr[...] = p3_recv[...].astype(F32).reshape(256, 128)
        for i in range(N_Z):
            for j in range(4):
                lhs_scr[4 * i : 4 * i + 4, 128 * j : 128 * j + 128] = tile_scr[
                    16 * i + 4 * j : 16 * i + 4 * j + 4, :
                ]
        which = jnp.where(y == x, 0, 1).astype(jnp.int32)
        values = dot(lhs_scr[...].astype(BF16), wuv_vm[which]).astype(BF16)
        p4_send[...] = values
        p4_recv[x] = values

        for k in ctx_order:
            p4_copy(k).start()

    def p4_sent():
        @pl.when(has_head)
        def _():
            for k in ctx_order:
                p4_copy(k).wait_send()

    pending.append(p4_sent)

    landed(info_recv.at[1:N_Z], info_r)
    for part in range(2):
        for k in range(8):
            row0 = 64 * part + 8 * k
            col_scr[row0 : row0 + 8, :] = info_recv[8 * part : 8 * part + 8, k, :]
    pick_col = col_scr[:, 0:1].astype(jnp.int32)
    weight_col = col_scr[:, 64:65]
    source = iota((128, 1), 0) % 8
    target = source * 32 + pick_col
    lane = iota((64, 256), 1)
    spread = jnp.where(iota((128, 128), 1) == source * 4 + pick_col, weight_col, 0.0)
    for part in range(2):
        for j in range(NJ):
            sel_scr[part, 64 * j : 64 * j + 64, :] = jnp.where(
                lane == target[64 * part : 64 * part + 64] + 4 * j, 1.0, 0.0
            ).astype(BF16)
        block = jnp.concatenate(
            [spread[64 * part : 64 * part + 64], jnp.zeros((64, 128), F32)], axis=0
        )
        comb = jnp.transpose(block)[0:32, :]
        comb_hi = comb.astype(BF16)
        comb_scr[part, 0] = comb_hi
        comb_scr[part, 1] = (comb - comb_hi.astype(F32)).astype(BF16)

    loads[3].wait()
    for k in y_order:
        wo_arrival(k).wait_recv()
    @pl.when(has_head)
    def _():
        landed(p4_recv.at[0:3], p4_r)

    @pl.when(jnp.logical_not(has_head))
    def _():
        landed(p4_recv, p4_r)

    lhs = jnp.concatenate([p4_recv[k] for k in range(N_Y)], axis=1)

    def to_tiles(values32, first, count):
        wide_scr[0 : 4 * count, :] = values32
        for zz in range(count):
            for j in range(NJ):
                row0 = 32 * (first + zz) + 4 * j
                z_scr[row0 : row0 + 4, :] = wide_scr[
                    4 * zz : 4 * zz + 4, 128 * j : 128 * j + 128
                ]
        tiles = z_scr[32 * first : 32 * (first + count), :]
        return tiles.astype(BF16).reshape(count, 32, 128)

    def z_send(values32, part, send, recv, ssem, rsem):
        send[8 * part : 8 * part + 8] = to_tiles(values32, 8 * part, 8)
        count, place = ((7, near), (8, far))[part]

        def copy(i):
            step, position = place(i)
            remote(
                send.at[position],
                recv.at[step - 1],
                ssem,
                rsem,
                c,
                y * N_Z + (z + N_Z - step) % N_Z,
            ).start()

        each(count, copy)

    def z_total(recv, rsem):
        total = z_scr[0:32, :]
        landed(recv, rsem)
        for i in range(N_Z - 1):
            total = total + recv[i].astype(F32)
        return total

    projection = wout_vm[...].reshape(512, COLS)
    z_send(dot(lhs[16:48], projection), 1, p5_send, p5_recv, p5_s, p5_r)
    others = jnp.concatenate([lhs[0:16], lhs[48:64]], axis=0)
    z_send(dot(others, projection), 0, p5_send, p5_recv, p5_s, p5_r)
    pending.append(lambda: landed(p5_recv, p5_s))
    attention = z_total(p5_recv, p5_r)
    residual = hid_scr[...] + attention
    rounded = residual.astype(BF16)
    p6_send[...] = rounded
    p6_recv[0] = rounded

    def p6_copy(i, place, ssem, rsem):
        step, position = place(i)
        remote(
            p6_send, p6_recv.at[position], ssem, rsem, c, y * N_Z + (z + step) % N_Z
        ).start()

    each(8, lambda i: p6_copy(i, far, p6f_s, p6f_r))
    each(7, lambda i: p6_copy(i, near, p6_s, p6_r))
    pending.append(lambda: landed(p6_recv.at[1:8], p6_s))
    pending.append(lambda: landed(p6_recv.at[8:16], p6f_s))
    res_scr[...] = residual
    small_scr[...] = attention
    for j in range(NJ):
        out[0:4, 128 * j : 128 * j + 128] = small_scr[4 * j : 4 * j + 4, :].astype(BF16)

    def y_send(send, recv, ssem, rsem, sign):
        for k in y_order:
            remote(
                send.at[k], recv.at[k], ssem, rsem, c, (y + N_Y + sign * k) % N_Y * N_Z + z
            ).start()
        pending.append(lambda: landed(recv.at[1:N_Y], ssem))
        recv[0] = send[0]

    def pick_rows(part):
        arrived = p6_recv[8 * part : 8 * part + 8].reshape(256, 128)
        picked = dot(sel_scr[part], arrived).astype(BF16)
        for j in range(NJ):
            p6b_send[part, :, :, 128 * j : 128 * j + 128] = picked[
                64 * j : 64 * j + 64, :
            ].reshape(N_Y, 16, 128)
        y_send(p6b_send.at[part], xe.at[part], p6b_s.at[part], p6b_r.at[part], 1)

    def gate_up(part):
        landed(xe.at[part].at[1:N_Y], p6b_r.at[part])
        rows = xe[part].reshape(64, COLS)
        side = (core + part) % 2

        def scatter(send, recv, ssem, rsem):
            for dx in (2, 1, 3):
                there = (x + dx) % 4
                remote(
                    send.at[part, there],
                    recv.at[2 * dx + side - 1],
                    ssem.at[part],
                    rsem,
                    there * 2 + part,
                    ep,
                ).start()

            @pl.when(core != part)
            def _():
                remote(
                    send.at[part, x], recv.at[0], ssem.at[part], rsem, x * 2 + part, ep
                ).start()

        p7_send[part] = dot(rows, gate_vm[...]).astype(BF16).reshape(N_Y, 16, HALF)
        scatter(p7_send, p7_recv, p7_s, p7_r)
        rows32 = rows.astype(F32)
        squares = jnp.sum(rows32 * rows32, axis=1, keepdims=True)
        p7u_send[part, :, :, HALF:] = (
            three_parts(squares, (64, 128)).astype(BF16).reshape(N_Y, 16, 128)
        )
        p7u_send[part, :, :, :HALF] = (
            dot(rows, up_vm[...]).astype(BF16).reshape(N_Y, 16, HALF)
        )
        scatter(p7u_send, p7u_recv, p7u_s, p7u_r)

    def gate_up_sent(part):
        for recv, sem in ((p7_recv, p7_s), (p7u_recv, p7u_s)):
            landed(recv.at[0:3], sem.at[part])

        @pl.when(core != part)
        def _():
            for recv, sem in ((p7_recv, p7_s), (p7u_recv, p7u_s)):
                landed(recv.at[0], sem.at[part])

    landed(p6_recv.at[1:8], p6_r)
    pick_rows(0)
    landed(p6_recv.at[8:16], p6f_r)
    pick_rows(1)
    gate_up(0)
    gate_up(1)
    pending.append(lambda: gate_up_sent(0))
    pending.append(lambda: gate_up_sent(1))

    landed(p7_recv, p7_r)
    gate = p7_send[core, x].astype(F32)
    for i in range(N_CTX - 1):
        gate = gate + p7_recv[i].astype(F32)
    landed(p7u_recv, p7u_r)
    sums = p7u_send[core, x].astype(F32)
    for i in range(N_CTX - 1):
        sums = sums + p7u_recv[i].astype(F32)
    mean = jnp.sum(sums[:, HALF:], axis=1, keepdims=True) / D
    scale = lax.rsqrt(mean + epsilon)
    gate = gate * scale
    up = sums[:, :HALF] * scale
    middle = (gate / (1.0 + jnp.exp(-gate)) * up).astype(BF16)
    p8_send[...] = middle
    mid_all[core, x] = middle
    for k in ctx_order:
        remote(
            p8_send, mid_all.at[core, x], p8_s.at[k - 1], p8_r.at[k - 1], ctx_step(k), ep
        ).start()
    for k in ctx_order:
        pending.append(
            remote(
                p8_send, mid_all.at[core, x], p8_s.at[k - 1], p8_r.at[k - 1], ctx_step(k), ep
            ).wait_send
        )
    loads[6].wait()

    def project(part):
        side = (core + part) % 2
        for dx in (1, 3, 2):
            frm = (x + 4 - dx) % 4
            sem = 2 * dx + side - 1
            remote(
                p8_send, mid_all.at[part, frm], p8_s.at[sem], p8_r.at[sem], frm * 2 + part, ep
            ).wait_recv()

        @pl.when(core != part)
        def _():
            remote(
                p8_send, mid_all.at[part, x], p8_s.at[0], p8_r.at[0], x * 2 + part, ep
            ).wait_recv()

        produced = dot(mid_all[part].reshape(64, HALF), down_vm[...])
        p9_send[part] = produced.astype(BF16).reshape(N_Y, 16, COLS)
        y_send(p9_send.at[part], p9_recv.at[part], p9_s.at[part], p9_r.at[part], -1)

    project(1)
    project(0)

    def combine(part):
        landed(p9_recv.at[part].at[1:N_Y], p9_r.at[part])
        back = p9_recv[part].reshape(64, COLS)
        mixed = dot(comb_scr[part, 0][:, :64], back) + dot(comb_scr[part, 1][:, :64], back)
        z_send(mixed, part, p10_send, p10_recv, p10_s, p10_r)

    combine(1)
    combine(0)
    finish()
    routed = z_total(p10_recv, p10_r)
    landed(p10_recv, p10_s)
    small_scr[...] = res_scr[...] + routed
    for j in range(NJ):
        out[4:8, 128 * j : 128 * j + 128] = small_scr[4 * j : 4 * j + 4, :].astype(BF16)


def per_device(
    queries,
    new_key,
    latent_cache,
    page_table,
    lengths,
    hidden_in,
    w_uv,
    w_out,
    norm_gain,
    routes,
    route_weight,
    w_gate,
    w_up,
    w_down,
):
    vmem = pl.BlockSpec(memory_space=pltpu.VMEM)
    in_hbm = pl.BlockSpec(memory_space=pltpu.HBM)
    dma = pltpu.SemaphoreType.DMA
    scratch = [
        pltpu.SMEM((4, 1, 4), jnp.int32),
        pltpu.SMEM((4,), jnp.int32),
        pltpu.SMEM((4, TOP), jnp.int32),
        pltpu.SMEM((4, TOP), F32),
        pltpu.VMEM((4, KDIM), BF16),
        pltpu.VMEM((4, COLS), BF16),
        pltpu.VMEM((COLS,), F32),
        pltpu.VMEM((4, 64, KDIM), BF16),
        pltpu.VMEM((1, 16, 64, KDIM), BF16),
        pltpu.VMEM((2, LAT, 128), BF16),
        pltpu.VMEM((N_Y, 128, COLS), BF16),
        pltpu.VMEM((COLS, HALF), BF16),
        pltpu.VMEM((COLS, HALF), BF16),
        pltpu.VMEM((HALF, COLS), BF16),
        pltpu.VMEM((128, KDIM), BF16),
        pltpu.VMEM((32, LAT), F32),
        pltpu.VMEM((256, 128), F32),
        pltpu.VMEM((64, LAT), F32),
        pltpu.VMEM((64, COLS), F32),
        pltpu.VMEM((512, 128), F32),
        pltpu.VMEM((32, 128), F32),
        pltpu.VMEM((32, 128), F32),
        pltpu.VMEM((128, 128), F32),
        pltpu.VMEM((32, 128), F32),
        pltpu.VMEM((128, 128), F32),
        pltpu.VMEM((2, 64 * NJ, 256), BF16),
        pltpu.VMEM((2, 2, 32, 128), BF16),
        pltpu.VMEM((4, 8, 128), F32),
        pltpu.VMEM((N_Z, 8, 128), F32),
        pltpu.VMEM((N_CTX, 144, 128), BF16),
        pltpu.VMEM((N_CTX - 1, 144, 128), BF16),
        pltpu.VMEM((8, 16, 128), BF16),
        pltpu.VMEM((N_Z, 16, 128), BF16),
        pltpu.VMEM((64, 128), BF16),
        pltpu.VMEM((N_Y, 64, 128), BF16),
        pltpu.VMEM((N_Z, 32, 128), BF16),
        pltpu.VMEM((N_Z - 1, 32, 128), BF16),
        pltpu.VMEM((32, 128), BF16),
        pltpu.VMEM((N_Z, 32, 128), BF16),
        pltpu.VMEM((2, N_Y, 16, COLS), BF16),
        pltpu.VMEM((2, N_Y, 16, COLS), BF16),
        pltpu.VMEM((2, 4, 16, HALF), BF16),
        pltpu.VMEM((N_CTX - 1, 16, HALF), BF16),
        pltpu.VMEM((2, 4, 16, HALF + 128), BF16),
        pltpu.VMEM((N_CTX - 1, 16, HALF + 128), BF16),
        pltpu.VMEM((16, HALF), BF16),
        pltpu.VMEM((2, 4, 16, HALF), BF16),
        pltpu.VMEM((2, N_Y, 16, COLS), BF16),
        pltpu.VMEM((2, N_Y, 16, COLS), BF16),
        pltpu.VMEM((N_Z, 32, 128), BF16),
        pltpu.VMEM((N_Z - 1, 32, 128), BF16),
        dma((14,)),
    ]
    scratch += [dma((3,)), dma]
    scratch += [dma((3,)), dma((3,))] + [dma] * 6 + [dma((7,)), dma] + [dma] * 6
    scratch += [dma((2,)), dma((2,))]
    scratch += [dma((2,)), dma] * 2
    for count in (7, 2, 0):
        scratch += [dma((count,)), dma((count,))] if count else [dma, dma]
    both = pl.pallas_call(
        kernel,
        out_shape=jax.ShapeDtypeStruct((8, COLS), BF16),
        in_specs=[in_hbm] * 14,
        out_specs=vmem,
        scratch_shapes=scratch,
        compiler_params=pltpu.CompilerParams(
            collective_id=0, has_side_effects=True, vmem_limit_bytes=60 * 1024 * 1024
        ),
    )(
        page_table,
        lengths,
        routes,
        route_weight,
        new_key,
        hidden_in,
        norm_gain,
        queries,
        latent_cache,
        w_uv,
        w_out,
        w_gate,
        w_up,
        w_down,
    )
    return both[:4], both[4:]


def solution(mesh):
    placed = (
        P("ep", None, None),
        P("ep", None),
        P("ctx", "ep", None, None),
        P("ep", "ctx", None),
        P("ep"),
        P("ep", "ctx"),
        P("ep", None, None),
        P("ep", "ctx"),
        P("ctx"),
        P("ep", None),
        P("ep", None),
        P("ctx", "ep"),
        P("ctx", "ep"),
        P("ep", "ctx"),
    )
    return jax.shard_map(
        per_device,
        mesh=mesh,
        in_specs=placed,
        out_specs=(P("ep", "ctx"), P("ep", "ctx")),
        check_vma=False,
    )
```

```python
import jax
import jax.numpy as jnp
from jax import lax
from jax.experimental import pallas as pl
from jax.experimental.pallas import tpu as pltpu
from jax.sharding import PartitionSpec as P

D = 7168
LAT = 512
KDIM = 576
TOP = 8
N_CTX = 8
N_Y = 4
N_Z = 16
COLS = 896
NJ = 7
HALF = 512

score_scale = 192.0 ** (-0.5)
epsilon = 1e-06
very_low = -1e30

MESH = pl.DeviceIdType.MESH
F32 = jnp.float32
BF16 = jnp.bfloat16


def dot(a, b):
    return jnp.dot(a, b, preferred_element_type=F32)


def dot_nt(a, b):
    return lax.dot_general(a, b, (((1,), (1,)), ((), ())), preferred_element_type=F32)


def iota(shape, dim):
    return lax.broadcasted_iota(jnp.int32, shape, dim)


def three_parts(x, shape):
    hi = x.astype(BF16).astype(F32)
    mid = (x - hi).astype(BF16).astype(F32)
    low = x - hi - mid
    lane = iota(shape, 1)
    zero = jnp.zeros(shape, F32)
    return jnp.where(lane == 0, hi, jnp.where(lane == 1, mid, jnp.where(lane == 2, low, zero)))


def kernel(
    page_table_in,
    lengths_in,
    routes_in,
    route_weight_in,
    new_key_in,
    hidden_in,
    gain_in,
    queries,
    cache,
    w_uv,
    w_out,
    w_gate,
    w_up,
    w_down,
    out,
    page_table,
    lengths,
    routes,
    route_weight,
    new_key,
    hidden,
    gain,
    q_vm,
    cache_vm,
    wuv_vm,
    wout_vm,
    gate_vm,
    up_vm,
    down_vm,
    nk_scr,
    att_scr,
    tile_scr,
    lhs_scr,
    wide_scr,
    z_scr,
    small_scr,
    out_scr,
    hid_scr,
    gain_scr,
    res_scr,
    col_scr,
    sel_scr,
    comb_scr,
    info_send,
    info_recv,
    p2_send,
    p2_recv,
    p3_send,
    p3_recv,
    p4_send,
    p4_recv,
    p5_send,
    p5_recv,
    p6_send,
    p6_recv,
    p6b_send,
    xe,
    p7_send,
    p7_recv,
    p7u_send,
    p7u_recv,
    p8_send,
    mid_all,
    p9_send,
    p9_recv,
    p10_send,
    p10_recv,
    lsem,
    uv_s,
    uv_r,
    wo_s,
    wo_r,
    info_s,
    info_r,
    p2_s,
    p2_r,
    p3_s,
    p3_r,
    p4_s,
    p4_r,
    p5_s,
    p5_r,
    p6_s,
    p6_r,
    p6f_s,
    p6f_r,
    p6b_s,
    p6b_r,
    p7_s,
    p7_r,
    p7u_s,
    p7u_r,
    p8_s,
    p8_r,
    p9_s,
    p9_r,
    p10_s,
    p10_r,
):
    c = lax.axis_index("ctx")
    ep = lax.axis_index("ep")
    y = ep // N_Z
    z = ep % N_Z
    x = c // 2
    core = c % 2
    has_head = z // 8 == core

    def remote(src, dst, ssem, rsem, to_ctx, to_ep):
        return pltpu.make_async_remote_copy(
            src_ref=src,
            dst_ref=dst,
            send_sem=ssem,
            recv_sem=rsem,
            device_id={"ctx": to_ctx, "ep": to_ep},
            device_id_type=MESH,
        )

    def each(count, step):
        def body(i, carry):
            step(i)
            return carry

        lax.fori_loop(0, count, body, 0)

    loads = [
        pltpu.make_async_copy(src, dst, lsem.at[i])
        for i, (src, dst) in enumerate(
            [
                (queries, q_vm),
                (cache, cache_vm),
                (w_uv, wuv_vm.at[0:1]),
                (w_out, wout_vm.at[y]),
                (w_gate, gate_vm),
                (w_up, up_vm),
                (w_down, down_vm),
                (page_table_in, page_table),
                (lengths_in, lengths),
                (routes_in, routes),
                (route_weight_in, route_weight),
                (new_key_in, new_key),
                (hidden_in, hidden),
                (gain_in, gain),
            ]
        )
    ]
    for load in loads[:2] + loads[7:] + loads[2:7]:
        load.start()
    pending = []

    def finish():
        for wait in pending:
            wait()

    def landed(buffer, sem):
        pltpu.make_async_copy(buffer, buffer, sem).wait()

    def z_step(i):
        return 8 + (i + 1) // 2 * (1 - 2 * (i % 2))

    def near(i):
        step = z_step(8 + i)
        return step, step % 8

    def far(i):
        step = z_step(i)
        return step, step + 4

    barrier = pltpu.get_barrier_semaphore()

    def greet(to_ctx, to_ep):
        pl.semaphore_signal(
            barrier, inc=1, device_id={"ctx": to_ctx, "ep": to_ep}, device_id_type=MESH
        )

    each(N_Z - 1, lambda i: greet(c, y * N_Z + (z + z_step(i)) % N_Z))
    each(N_Y - 1, lambda i: greet(c, (y + i + 1) % N_Y * N_Z + z))
    each(N_CTX - 1, lambda i: greet((c + i + 1) % N_CTX, ep))

    for load in loads[7:]:
        load.wait()

    row = iota((32, 128), 0)
    expert = ((row // 2) % 4 + y) % 4 * 4 + row // 8
    place = row % 2
    before = jnp.zeros((32, 128), jnp.int32)
    pick = jnp.zeros((32, 128), F32)
    weight = jnp.zeros((32, 128), F32)
    for r in range(4):
        named = jnp.zeros((32, 128), jnp.int32)
        w_r = jnp.zeros((32, 128), F32)
        for k in range(TOP):
            hit = expert == routes[r, k]
            named = jnp.where(hit, 1, named)
            w_r = jnp.where(hit, route_weight[r, k], w_r)
        taken = (named == 1) & (before == place)
        pick = jnp.where(taken, float(r), pick)
        weight = jnp.where(taken, w_r, weight)
        before = before + named
    info = jnp.where(iota((32, 128), 1) < 64, pick, weight)
    info_send[...] = info.reshape(4, 8, 128)
    info_recv[0] = info_send[z // 4]

    hid_scr[28:32, :] = jnp.zeros((4, 128), F32)
    gain_scr[...] = jnp.zeros((128, 128), F32)
    hid32 = hidden[...].astype(F32)
    for j in range(NJ):
        hid_scr[4 * j : 4 * j + 4, :] = hid32[:, 128 * j : 128 * j + 128]
        gain_scr[j : j + 1, :] = gain[128 * j : 128 * j + 128].reshape(1, 128)
    gain_scr[...] = jnp.transpose(gain_scr[...])
    nk_scr[...] = jnp.zeros((128, KDIM), BF16)
    nk_scr[0:4, :] = new_key[...]
    for zz in range(N_Z):
        z_scr[32 * zz + 28 : 32 * zz + 32, :] = jnp.zeros((4, 128), F32)

    col = iota((1, 1024), 1)
    slot = col // 64
    owner = jnp.full((1, 1024), -1, jnp.int32)
    for r in range(4):
        for p in range(4):
            position = (p * N_CTX + c) * 64 + col % 64
            good = (slot == page_table[r, 0, p]) & (position < lengths[r])
            owner = jnp.where(good, r, owner)
    i0 = iota((256, 256), 0)
    shuffle = jnp.where((i0 % 4) * 64 + i0 // 4 == iota((256, 256), 1), 1.0, 0.0).astype(BF16)
    loads[0].wait()
    q = dot(shuffle, q_vm[...].reshape(256, KDIM)).astype(BF16)
    loads[1].wait()
    keys = cache_vm[...].reshape(1024, KDIM)
    scores = dot_nt(q, keys) * score_scale
    fresh = dot_nt(q, nk_scr[...]) * score_scale
    mask = owner == iota((256, 1024), 0) % 4
    mask_new = iota((256, 128), 1) + 1024 * c == iota((256, 128), 0) % 4
    peak = jnp.maximum(
        jnp.max(jnp.where(mask, scores, very_low), axis=1, keepdims=True),
        jnp.max(jnp.where(mask_new, fresh, very_low), axis=1, keepdims=True),
    )
    weights = jnp.where(mask, jnp.exp(scores - peak), 0.0).astype(BF16)
    weights_new = jnp.where(mask_new, jnp.exp(fresh - peak), 0.0).astype(BF16)
    total = jnp.sum(weights.astype(F32), axis=1, keepdims=True) + jnp.sum(
        weights_new.astype(F32), axis=1, keepdims=True
    )
    mixture = dot(weights, keys[:, :LAT]) + dot(weights_new, nk_scr[:, :LAT])
    some = total > 0.0
    total = jnp.where(some, total, 1.0)
    logsum = jnp.where(some, peak + jnp.log(total), very_low)
    mixture = (mixture / total).astype(BF16)
    for j in range(4):
        p2_send[:, 32 * j : 32 * j + 32, :] = mixture[:, 128 * j : 128 * j + 128].reshape(
            N_CTX, 32, 128
        )
    logsum = three_parts(logsum, (256, 128)).reshape(N_CTX, 32, 128)
    p2_send[:, 128:144, :] = jnp.where(
        iota((N_CTX, 16, 128), 2) < 64, logsum[:, :16], jnp.roll(logsum[:, 16:], 64, axis=2)
    ).astype(BF16)

    pl.semaphore_wait(barrier, N_Z - 1 + N_Y - 1 + N_CTX - 1)

    def ctx_step(k):
        return (c // 2 + k // 2) % 4 * 2 + (c + k) % 2

    def ctx_back(k):
        return (c // 2 + 4 - k // 2) % 4 * 2 + (c + k) % 2

    ctx_order = (4, 5, 2, 3, 6, 7, 1)
    y_order = (2, 1, 3)

    def ctx_scatter(send, recv, ssem, rsem):
        for k in ctx_order:
            to = ctx_step(k)
            remote(send.at[to], recv.at[k - 1], ssem, rsem, to, ep).start()
        pending.append(lambda: landed(recv, ssem))

    ctx_scatter(p2_send, p2_recv, p2_s, p2_r)

    def info_copy(i, place):
        step, position = place(i)
        to = (z + step) % N_Z
        remote(
            info_send.at[to // 4], info_recv.at[position], info_s, info_r, c, y * N_Z + to
        ).start()

    each(8, lambda i: info_copy(i, far))
    each(7, lambda i: info_copy(i, near))
    pending.append(lambda: landed(info_recv.at[1:N_Z], info_s))

    def uv_copy(k):
        return remote(
            w_uv,
            wuv_vm.at[1:2],
            uv_s.at[k - 1],
            uv_r,
            c,
            (y + k) % N_Y * N_Z + z,
        )

    @pl.when(has_head & (y == x))
    def _():
        for k in y_order:
            uv_copy(k).start()

    def uv_sent():
        @pl.when(has_head & (y == x))
        def _():
            for k in y_order:
                uv_copy(k).wait_send()

    pending.append(uv_sent)

    for k in y_order:
        remote(
            w_out, wout_vm.at[y], wo_s.at[k - 1], wo_r.at[k - 1], c, (y + k) % N_Y * N_Z + z
        ).start()
    for k in y_order:
        pending.append(
            remote(
                w_out, wout_vm.at[y], wo_s.at[k - 1], wo_r.at[k - 1], c, (y + k) % N_Y * N_Z + z
            ).wait_send
        )

    def wo_arrival(k):
        frm = (y + N_Y - k) % N_Y
        return remote(w_out, wout_vm.at[frm], wo_s.at[k - 1], wo_r.at[k - 1], c, frm * N_Z + z)

    landed(p2_recv, p2_r)
    parts = [p2_send[c]] + [p2_recv[i] for i in range(N_CTX - 1)]
    def row_logs(p):
        both = p[128:144].astype(F32)
        first = iota((16, 128), 1) < 64
        return jnp.concatenate(
            [
                jnp.sum(jnp.where(first, both, 0.0), axis=1, keepdims=True),
                jnp.sum(jnp.where(first, 0.0, both), axis=1, keepdims=True),
            ],
            axis=0,
        )

    logs = [row_logs(p) for p in parts]
    top = logs[0]
    for l in logs[1:]:
        top = jnp.maximum(top, l)
    factors = [jnp.exp(l - top) for l in logs]
    below = factors[0]
    for f in factors[1:]:
        below = below + f
    for j in range(4):
        above = jnp.zeros((32, 128), F32)
        for p, f in zip(parts, factors):
            above = above + f * p[32 * j : 32 * j + 32].astype(F32)
        att_scr[:, 128 * j : 128 * j + 128] = above / below
    for i in range(8):
        for j in range(4):
            tile_scr[16 * i + 4 * j : 16 * i + 4 * j + 4, :] = att_scr[
                4 * i : 4 * i + 4, 128 * j : 128 * j + 128
            ]
    p3_send[...] = tile_scr[0:128, :].astype(BF16).reshape(8, 16, 128)

    def p3_each(step):
        def one(n):
            i = (z + z_step(n)) % 8

            @pl.when(z != 8 * core + i)
            def _():
                step(i)

        each(8, one)

    def p3_copy(i):
        to = 8 * core + i
        remote(
            p3_send.at[i], p3_recv.at[(to + N_Z - z) % N_Z], p3_s, p3_r, c, y * N_Z + to
        ).start()

    p3_each(p3_copy)

    def p3_sent():
        @pl.when(has_head)
        def _():
            landed(p3_send.at[0:7], p3_s)

        @pl.when(jnp.logical_not(has_head))
        def _():
            landed(p3_send, p3_s)

    pending.append(p3_sent)
    loads[4].wait()
    loads[5].wait()
    for j in range(NJ):
        factor = gain_scr[:, j : j + 1]
        for w in (gate_vm, up_vm):
            block = w[128 * j : 128 * j + 128, :].astype(F32)
            w[128 * j : 128 * j + 128, :] = (block * factor).astype(BF16)
    loads[2].wait()

    def p4_copy(k):
        return remote(p4_send, p4_recv.at[x], p4_s.at[k - 1], p4_r, ctx_step(k), ep)

    @pl.when(has_head)
    def _():
        p3_recv[0] = p3_send[z % 8]
        landed(p3_recv.at[1:N_Z], p3_r)

        @pl.when(y != x)
        def _():
            remote(w_uv, wuv_vm.at[1:2], uv_s.at[0], uv_r, c, x * N_Z + z).wait_recv()

        tile_scr[...] = p3_recv[...].astype(F32).reshape(256, 128)
        for i in range(N_Z):
            for j in range(4):
                lhs_scr[4 * i : 4 * i + 4, 128 * j : 128 * j + 128] = tile_scr[
                    16 * i + 4 * j : 16 * i + 4 * j + 4, :
                ]
        which = jnp.where(y == x, 0, 1).astype(jnp.int32)
        values = dot(lhs_scr[...].astype(BF16), wuv_vm[which]).astype(BF16)
        p4_send[...] = values
        p4_recv[x] = values

        for k in ctx_order:
            p4_copy(k).start()

    def p4_sent():
        @pl.when(has_head)
        def _():
            for k in ctx_order:
                p4_copy(k).wait_send()

    pending.append(p4_sent)

    landed(info_recv.at[1:N_Z], info_r)
    for part in range(2):
        for k in range(8):
            row0 = 64 * part + 8 * k
            col_scr[row0 : row0 + 8, :] = info_recv[8 * part : 8 * part + 8, k, :]
    pick_col = col_scr[:, 0:1].astype(jnp.int32)
    weight_col = col_scr[:, 64:65]
    source = iota((128, 1), 0) % 8
    target = source * 32 + pick_col
    lane = iota((64, 256), 1)
    spread = jnp.where(iota((128, 128), 1) == source * 4 + pick_col, weight_col, 0.0)
    for part in range(2):
        for j in range(NJ):
            sel_scr[part, 64 * j : 64 * j + 64, :] = jnp.where(
                lane == target[64 * part : 64 * part + 64] + 4 * j, 1.0, 0.0
            ).astype(BF16)
        block = jnp.concatenate(
            [spread[64 * part : 64 * part + 64], jnp.zeros((64, 128), F32)], axis=0
        )
        comb = jnp.transpose(block)[0:32, :]
        comb_hi = comb.astype(BF16)
        comb_scr[part, 0] = comb_hi
        comb_scr[part, 1] = (comb - comb_hi.astype(F32)).astype(BF16)

    loads[3].wait()
    for k in y_order:
        wo_arrival(k).wait_recv()
    @pl.when(has_head)
    def _():
        landed(p4_recv.at[0:3], p4_r)

    @pl.when(jnp.logical_not(has_head))
    def _():
        landed(p4_recv, p4_r)

    lhs = jnp.concatenate([p4_recv[k] for k in range(N_Y)], axis=1)

    def to_tiles(values32, first, count):
        wide_scr[0 : 4 * count, :] = values32
        for zz in range(count):
            for j in range(NJ):
                row0 = 32 * (first + zz) + 4 * j
                z_scr[row0 : row0 + 4, :] = wide_scr[
                    4 * zz : 4 * zz + 4, 128 * j : 128 * j + 128
                ]
        tiles = z_scr[32 * first : 32 * (first + count), :]
        return tiles.astype(BF16).reshape(count, 32, 128)

    def z_send(values32, part, send, recv, ssem, rsem):
        send[8 * part : 8 * part + 8] = to_tiles(values32, 8 * part, 8)
        count, place = ((7, near), (8, far))[part]

        def copy(i):
            step, position = place(i)
            remote(
                send.at[position],
                recv.at[step - 1],
                ssem,
                rsem,
                c,
                y * N_Z + (z + N_Z - step) % N_Z,
            ).start()

        each(count, copy)

    def z_total(recv, rsem):
        total = z_scr[0:32, :]
        landed(recv, rsem)
        for i in range(N_Z - 1):
            total = total + recv[i].astype(F32)
        return total

    projection = wout_vm[...].reshape(512, COLS)
    z_send(dot(lhs[16:48], projection), 1, p5_send, p5_recv, p5_s, p5_r)
    others = jnp.concatenate([lhs[0:16], lhs[48:64]], axis=0)
    z_send(dot(others, projection), 0, p5_send, p5_recv, p5_s, p5_r)
    pending.append(lambda: landed(p5_recv, p5_s))
    attention = z_total(p5_recv, p5_r)
    residual = hid_scr[...] + attention
    rounded = residual.astype(BF16)
    p6_send[...] = rounded
    p6_recv[0] = rounded

    def p6_copy(i, place, ssem, rsem):
        step, position = place(i)
        remote(
            p6_send, p6_recv.at[position], ssem, rsem, c, y * N_Z + (z + step) % N_Z
        ).start()

    each(8, lambda i: p6_copy(i, far, p6f_s, p6f_r))
    each(7, lambda i: p6_copy(i, near, p6_s, p6_r))
    pending.append(lambda: landed(p6_recv.at[1:8], p6_s))
    pending.append(lambda: landed(p6_recv.at[8:16], p6f_s))
    res_scr[...] = residual
    small_scr[...] = attention
    for j in range(NJ):
        out_scr[0:4, 128 * j : 128 * j + 128] = small_scr[4 * j : 4 * j + 4, :]

    def y_send(send, recv, ssem, rsem, sign):
        for k in y_order:
            remote(
                send.at[k], recv.at[k], ssem, rsem, c, (y + N_Y + sign * k) % N_Y * N_Z + z
            ).start()
        pending.append(lambda: landed(recv.at[1:N_Y], ssem))
        recv[0] = send[0]

    def pick_rows(part):
        arrived = p6_recv[8 * part : 8 * part + 8].reshape(256, 128)
        picked = dot(sel_scr[part], arrived).astype(BF16)
        for j in range(NJ):
            p6b_send[part, :, :, 128 * j : 128 * j + 128] = picked[
                64 * j : 64 * j + 64, :
            ].reshape(N_Y, 16, 128)
        y_send(p6b_send.at[part], xe.at[part], p6b_s.at[part], p6b_r.at[part], 1)

    def gate_up(part):
        landed(xe.at[part].at[1:N_Y], p6b_r.at[part])
        rows = xe[part].reshape(64, COLS)
        side = (core + part) % 2

        def scatter(send, recv, ssem, rsem):
            for dx in (2, 1, 3):
                there = (x + dx) % 4
                remote(
                    send.at[part, there],
                    recv.at[2 * dx + side - 1],
                    ssem.at[part],
                    rsem,
                    there * 2 + part,
                    ep,
                ).start()

            @pl.when(core != part)
            def _():
                remote(
                    send.at[part, x], recv.at[0], ssem.at[part], rsem, x * 2 + part, ep
                ).start()

        p7_send[part] = dot(rows, gate_vm[...]).astype(BF16).reshape(N_Y, 16, HALF)
        scatter(p7_send, p7_recv, p7_s, p7_r)
        rows32 = rows.astype(F32)
        squares = jnp.sum(rows32 * rows32, axis=1, keepdims=True)
        p7u_send[part, :, :, HALF:] = (
            three_parts(squares, (64, 128)).astype(BF16).reshape(N_Y, 16, 128)
        )
        p7u_send[part, :, :, :HALF] = (
            dot(rows, up_vm[...]).astype(BF16).reshape(N_Y, 16, HALF)
        )
        scatter(p7u_send, p7u_recv, p7u_s, p7u_r)

    def gate_up_sent(part):
        for recv, sem in ((p7_recv, p7_s), (p7u_recv, p7u_s)):
            landed(recv.at[0:3], sem.at[part])

        @pl.when(core != part)
        def _():
            for recv, sem in ((p7_recv, p7_s), (p7u_recv, p7u_s)):
                landed(recv.at[0], sem.at[part])

    landed(p6_recv.at[1:8], p6_r)
    pick_rows(0)
    landed(p6_recv.at[8:16], p6f_r)
    pick_rows(1)
    gate_up(0)
    gate_up(1)
    pending.append(lambda: gate_up_sent(0))
    pending.append(lambda: gate_up_sent(1))

    landed(p7_recv, p7_r)
    gate = p7_send[core, x].astype(F32)
    for i in range(N_CTX - 1):
        gate = gate + p7_recv[i].astype(F32)
    landed(p7u_recv, p7u_r)
    sums = p7u_send[core, x].astype(F32)
    for i in range(N_CTX - 1):
        sums = sums + p7u_recv[i].astype(F32)
    mean = jnp.sum(sums[:, HALF:], axis=1, keepdims=True) / D
    scale = lax.rsqrt(mean + epsilon)
    gate = gate * scale
    up = sums[:, :HALF] * scale
    middle = (gate / (1.0 + jnp.exp(-gate)) * up).astype(BF16)
    p8_send[...] = middle
    mid_all[core, x] = middle
    for k in ctx_order:
        remote(
            p8_send, mid_all.at[core, x], p8_s.at[k - 1], p8_r.at[k - 1], ctx_step(k), ep
        ).start()
    for k in ctx_order:
        pending.append(
            remote(
                p8_send, mid_all.at[core, x], p8_s.at[k - 1], p8_r.at[k - 1], ctx_step(k), ep
            ).wait_send
        )
    loads[6].wait()

    def project(part):
        side = (core + part) % 2
        for dx in (1, 3, 2):
            frm = (x + 4 - dx) % 4
            sem = 2 * dx + side - 1
            remote(
                p8_send, mid_all.at[part, frm], p8_s.at[sem], p8_r.at[sem], frm * 2 + part, ep
            ).wait_recv()

        @pl.when(core != part)
        def _():
            remote(
                p8_send, mid_all.at[part, x], p8_s.at[0], p8_r.at[0], x * 2 + part, ep
            ).wait_recv()

        produced = dot(mid_all[part].reshape(64, HALF), down_vm[...])
        p9_send[part] = produced.astype(BF16).reshape(N_Y, 16, COLS)
        y_send(p9_send.at[part], p9_recv.at[part], p9_s.at[part], p9_r.at[part], -1)

    project(1)
    project(0)

    def combine(part):
        landed(p9_recv.at[part].at[1:N_Y], p9_r.at[part])
        back = p9_recv[part].reshape(64, COLS)
        mixed = dot(comb_scr[part, 0][:, :64], back) + dot(comb_scr[part, 1][:, :64], back)
        z_send(mixed, part, p10_send, p10_recv, p10_s, p10_r)

    combine(1)
    combine(0)
    finish()
    routed = z_total(p10_recv, p10_r)
    landed(p10_recv, p10_s)
    small_scr[...] = res_scr[...] + routed
    for j in range(NJ):
        out_scr[4:8, 128 * j : 128 * j + 128] = small_scr[4 * j : 4 * j + 4, :]
    out[...] = out_scr[...].astype(BF16)


def per_device(
    queries,
    new_key,
    latent_cache,
    page_table,
    lengths,
    hidden_in,
    w_uv,
    w_out,
    norm_gain,
    routes,
    route_weight,
    w_gate,
    w_up,
    w_down,
):
    vmem = pl.BlockSpec(memory_space=pltpu.VMEM)
    in_hbm = pl.BlockSpec(memory_space=pltpu.HBM)
    dma = pltpu.SemaphoreType.DMA
    scratch = [
        pltpu.SMEM((4, 1, 4), jnp.int32),
        pltpu.SMEM((4,), jnp.int32),
        pltpu.SMEM((4, TOP), jnp.int32),
        pltpu.SMEM((4, TOP), F32),
        pltpu.VMEM((4, KDIM), BF16),
        pltpu.VMEM((4, COLS), BF16),
        pltpu.VMEM((COLS,), F32),
        pltpu.VMEM((4, 64, KDIM), BF16),
        pltpu.VMEM((1, 16, 64, KDIM), BF16),
        pltpu.VMEM((2, LAT, 128), BF16),
        pltpu.VMEM((N_Y, 128, COLS), BF16),
        pltpu.VMEM((COLS, HALF), BF16),
        pltpu.VMEM((COLS, HALF), BF16),
        pltpu.VMEM((HALF, COLS), BF16),
        pltpu.VMEM((128, KDIM), BF16),
        pltpu.VMEM((32, LAT), F32),
        pltpu.VMEM((256, 128), F32),
        pltpu.VMEM((64, LAT), F32),
        pltpu.VMEM((64, COLS), F32),
        pltpu.VMEM((512, 128), F32),
        pltpu.VMEM((32, 128), F32),
        pltpu.VMEM((8, COLS), F32),
        pltpu.VMEM((32, 128), F32),
        pltpu.VMEM((128, 128), F32),
        pltpu.VMEM((32, 128), F32),
        pltpu.VMEM((128, 128), F32),
        pltpu.VMEM((2, 64 * NJ, 256), BF16),
        pltpu.VMEM((2, 2, 32, 128), BF16),
        pltpu.VMEM((4, 8, 128), F32),
        pltpu.VMEM((N_Z, 8, 128), F32),
        pltpu.VMEM((N_CTX, 144, 128), BF16),
        pltpu.VMEM((N_CTX - 1, 144, 128), BF16),
        pltpu.VMEM((8, 16, 128), BF16),
        pltpu.VMEM((N_Z, 16, 128), BF16),
        pltpu.VMEM((64, 128), BF16),
        pltpu.VMEM((N_Y, 64, 128), BF16),
        pltpu.VMEM((N_Z, 32, 128), BF16),
        pltpu.VMEM((N_Z - 1, 32, 128), BF16),
        pltpu.VMEM((32, 128), BF16),
        pltpu.VMEM((N_Z, 32, 128), BF16),
        pltpu.VMEM((2, N_Y, 16, COLS), BF16),
        pltpu.VMEM((2, N_Y, 16, COLS), BF16),
        pltpu.VMEM((2, 4, 16, HALF), BF16),
        pltpu.VMEM((N_CTX - 1, 16, HALF), BF16),
        pltpu.VMEM((2, 4, 16, HALF + 128), BF16),
        pltpu.VMEM((N_CTX - 1, 16, HALF + 128), BF16),
        pltpu.VMEM((16, HALF), BF16),
        pltpu.VMEM((2, 4, 16, HALF), BF16),
        pltpu.VMEM((2, N_Y, 16, COLS), BF16),
        pltpu.VMEM((2, N_Y, 16, COLS), BF16),
        pltpu.VMEM((N_Z, 32, 128), BF16),
        pltpu.VMEM((N_Z - 1, 32, 128), BF16),
        dma((14,)),
    ]
    scratch += [dma((3,)), dma]
    scratch += [dma((3,)), dma((3,))] + [dma] * 6 + [dma((7,)), dma] + [dma] * 6
    scratch += [dma((2,)), dma((2,))]
    scratch += [dma((2,)), dma] * 2
    for count in (7, 2, 0):
        scratch += [dma((count,)), dma((count,))] if count else [dma, dma]
    both = pl.pallas_call(
        kernel,
        out_shape=jax.ShapeDtypeStruct((8, COLS), BF16),
        in_specs=[in_hbm] * 14,
        out_specs=vmem,
        scratch_shapes=scratch,
        compiler_params=pltpu.CompilerParams(
            collective_id=0, has_side_effects=True, vmem_limit_bytes=60 * 1024 * 1024
        ),
    )(
        page_table,
        lengths,
        routes,
        route_weight,
        new_key,
        hidden_in,
        norm_gain,
        queries,
        latent_cache,
        w_uv,
        w_out,
        w_gate,
        w_up,
        w_down,
    )
    return both[:4], both[4:]


def solution(mesh):
    placed = (
        P("ep", None, None),
        P("ep", None),
        P("ctx", "ep", None, None),
        P("ep", "ctx", None),
        P("ep"),
        P("ep", "ctx"),
        P("ep", None, None),
        P("ep", "ctx"),
        P("ctx"),
        P("ep", None),
        P("ep", None),
        P("ctx", "ep"),
        P("ctx", "ep"),
        P("ep", "ctx"),
    )
    return jax.shard_map(
        per_device,
        mesh=mesh,
        in_specs=placed,
        out_specs=(P("ep", "ctx"), P("ep", "ctx")),
        check_vma=False,
    )
```
